128 devices in a mesh: dp: 16 (over y_hi, z, core), tensor: 8 (over y_lo, x).
Axes of the slice: x: 4, y: 4 (y_hi: 2, y_lo: 2; y = y_hi * 2 + y_lo), z: 4, core: 2. Of those that a mesh axis runs over, the one named last changes fastest.
Arguments:
- layer_input: bfloat16 [4096, 2048], P('dp'), may hold values from -6 to 6
- seq_lengths: int32 [16, 4], P('dp'), may hold values from 0 to 256, as said below
- norm_gains: float32 [2, 2, 2048], replicated, may hold values from 0.5 to 1.5
- conv_kernel: float32 [2, 3584, 4], replicated, may hold values from -3 to 3
- step_bias: float32 [2, 48], replicated, may hold values from -6 to -2
- log_rate: float32 [2, 48], replicated, may hold values from 0 to 2.77
- skip_gain: float32 [2, 48], replicated, may hold values from 0.5 to 1.5
- zx_weight: bfloat16 [2, 2048, 2, 3072], P(None, 'dp', None, 'tensor'), may hold values from -0.125 to 0.125
- bc_weight: bfloat16 [2, 2048, 512], P(None, 'dp'), may hold values from -0.125 to 0.125
- step_weight: bfloat16 [2, 2048, 48], P(None, 'dp'), may hold values from -0.125 to 0.125
- query_weight: bfloat16 [2, 2048, 1024], P(None, 'dp', 'tensor'), may hold values from -0.125 to 0.125
- keyval_weight: bfloat16 [2, 2048, 2, 256], P(None, 'dp'), may hold values from -0.125 to 0.125
- mamba_out_weight: bfloat16 [2, 2048, 3072], P(None, 'dp', 'tensor'), may hold values from -0.109375 to 0.109375
- attn_out_weight: bfloat16 [2, 2048, 1024], P(None, 'dp', 'tensor'), may hold values from -1.5 to 1.5
- gate_up_weight: bfloat16 [2, 2048, 2, 4096], P(None, 'dp', None, 'tensor'), may hold values from -0.125 to 0.125
- down_weight: bfloat16 [2, 2048, 4096], P(None, 'dp', 'tensor'), may hold values from -0.09375 to 0.09375
- cotangent: bfloat16 [4096, 2048], P('dp'), may hold values from -6 to 6
Outputs:
- block_output: float32 [4096, 2048], P('dp')
- input_grad: float32 [4096, 2048], P('dp')
- norm_gains_grad: float32 [2, 2, 2048], replicated
- conv_kernel_grad: float32 [2, 3584, 4], replicated
- step_bias_grad: float32 [2, 48], replicated
- log_rate_grad: float32 [2, 48], replicated
- skip_gain_grad: float32 [2, 48], replicated
- zx_weight_grad: float32 [2, 2048, 2, 3072], P(None, 'dp', None, 'tensor')
- bc_weight_grad: float32 [2, 2048, 512], P(None, ('dp', 'tensor'))
- step_weight_grad: float32 [2, 2048, 48], P(None, ('dp', 'tensor'))
- query_weight_grad: float32 [2, 2048, 1024], P(None, 'dp', 'tensor')
- keyval_weight_grad: float32 [2, 2048, 2, 256], P(None, ('dp', 'tensor'))
- mamba_out_weight_grad: float32 [2, 2048, 3072], P(None, 'dp', 'tensor')
- attn_out_weight_grad: float32 [2, 2048, 1024], P(None, 'dp', 'tensor')
- gate_up_weight_grad: float32 [2, 2048, 2, 4096], P(None, 'dp', None, 'tensor')
- down_weight_grad: float32 [2, 2048, 4096], P(None, 'dp', 'tensor')
The draws below stay inside these ranges and needn't reach their ends.
Inputs may be any that keep to these rules, and one draw needn't show every extreme that they name: `seq_lengths`: each row lists up to 4 sequence lengths of one token group, zero where a slot holds no sequence; a row sums to at most 256, and some row holds a single sequence of 256.
All inputs are finite; a program needn't handle non-finite values.
Results may differ from the reference program's by a relative error of at most 0.034.
Values may be sent and summed in bfloat16 or wider, within the bound.
No kernel may reach another device: no remote copies, remote signals or barrier semaphores. Data moves between devices by JAX's collectives and lax.ppermute only.
A program may use at most 320 MiB of HBM per device.

```python
import math
from functools import partial
import jax
import jax.numpy as jnp
from jax import lax

D = 2048
NH = 48
P_SIZE = 64
N = 256
CONV = 4
HQ = 8
KV = 2
HD = 128
FF = 4096
LAYERS = 2
SLOTS = 4
TOK_DEV = 256
DI = 3072
GROUPS = 16
TOKENS = 4096


def draw_seq_lengths(key, part):
    key = jax.random.fold_in(key, 11)
    key_used, key_cuts, key_full = jax.random.split(key, 3)
    used_slots = jax.random.randint(key_used, (GROUPS, 1), TOK_DEV // 2, TOK_DEV + 1)
    cut_points = jax.random.randint(key_cuts, (GROUPS, SLOTS - 1), 0, TOK_DEV + 1)
    cut_points = jnp.sort(cut_points, axis=1) * used_slots // TOK_DEV
    bounds = jnp.concatenate([jnp.zeros((GROUPS, 1), jnp.int32), cut_points, used_slots], axis=1)
    lengths = bounds[:, 1:] - bounds[:, :-1]
    full_group = jax.random.randint(key_full, (), 0, GROUPS)
    single = jnp.concatenate([jnp.full((1, 1), TOK_DEV, jnp.int32), jnp.zeros((1, SLOTS - 1), jnp.int32)], axis=1)
    chosen = jnp.arange(GROUPS)[:, None] == full_group
    return jnp.where(chosen, single, lengths).astype(jnp.int32)


def shard_levels(stream_key, dims, pieces, low, high):
    factor_of, own = 1.0, jax.random.fold_in(stream_key, 6)
    for dim, parts in pieces:
        steps = jnp.exp(jax.random.uniform(jax.random.fold_in(own, dim), (parts,), jnp.float32, low / len(pieces), high / len(pieces)))
        factor_of = factor_of * jnp.repeat(steps, dims[dim] // parts).reshape([-1 if axis == dim else 1 for axis in range(len(dims))])
    return factor_of


def normal_values(rng, dims, scale, reach, cuts=(), held_as=jnp.bfloat16):
    array = jax.random.normal(rng, dims, jnp.float32) * scale
    if len(cuts) > 0:
        array = shard_levels(rng, dims, cuts, -0.22, 0.18) * array
    return jnp.clip(array, min=-reach, max=reach).astype(held_as)


def setup_inputs(seed: int = 0) -> dict:
    seeds = jax.random.split(jax.random.key(seed), 18)
    return {
        "layer_input": normal_values(seeds[0], (TOKENS, D), 1.0, 6.0, ((0, 16),)),
        "seq_lengths": draw_seq_lengths(jax.random.fold_in(seeds[17], 71), 0),
        "norm_gains": jnp.clip(1.0 + 0.1 * jax.random.normal(seeds[2], (LAYERS, 2, D), jnp.float32), 0.5, 1.5),
        "conv_kernel": normal_values(seeds[3], (LAYERS, DI + 2 * N, CONV), CONV ** -0.5, 3.0, (), jnp.float32),
        "step_bias": jnp.clip(jax.random.uniform(seeds[4], (LAYERS, NH), jnp.float32, -6.0, -2.0), -6.0, -2.0),
        "log_rate": jnp.clip(jax.random.uniform(seeds[5], (LAYERS, NH), jnp.float32, 0.0, 2.77), 0.0, 2.77),
        "skip_gain": jnp.clip(jax.random.uniform(seeds[6], (LAYERS, NH), jnp.float32, 0.5, 1.5), 0.5, 1.5),
        "zx_weight": normal_values(seeds[7], (LAYERS, D, 2, DI), D ** -0.5, 0.125, ((1, 16), (3, 8))),
        "bc_weight": normal_values(seeds[8], (LAYERS, D, 2 * N), D ** -0.5, 0.125, ((1, 16),)),
        "step_weight": normal_values(seeds[9], (LAYERS, D, NH), D ** -0.5, 0.125, ((1, 16),)),
        "query_weight": normal_values(seeds[10], (LAYERS, D, HQ * HD), D ** -0.5, 0.125, ((1, 16), (2, 8))),
        "keyval_weight": normal_values(seeds[11], (LAYERS, D, 2, KV * HD), D ** -0.5, 0.125, ((1, 16),)),
        "mamba_out_weight": normal_values(seeds[12], (LAYERS, D, DI), DI ** -0.5, 0.109375, ((1, 16), (2, 8))),
        "attn_out_weight": normal_values(seeds[13], (LAYERS, D, HQ * HD), (HQ * HD // 64) ** -0.5, 1.5, ((1, 16), (2, 8))),
        "gate_up_weight": normal_values(seeds[14], (LAYERS, D, 2, FF), D ** -0.5, 0.125, ((1, 16), (3, 8))),
        "down_weight": normal_values(seeds[15], (LAYERS, D, FF), FF ** -0.5, 0.09375, ((1, 16), (2, 8))),
        "cotangent": normal_values(seeds[16], (TOKENS, D), 1.0, 6.0, ((0, 16),)),
    }


EPSILON = 1e-05
ROPE_BASE = 10000.0
PRECISE = lax.Precision.HIGHEST

@jax.custom_vjp
def low(v):
    return lax.optimization_barrier(v.astype(jnp.bfloat16)).astype(jnp.float32)

@jax.custom_vjp
def low_back(v):
    return v

def low_keep(v):
    return (low(v), None)

def low_pass(kept, grad):
    return (grad,)

def back_keep(v):
    return (v, None)

def back_low(kept, grad):
    return (low(grad),)
low.defvjp(low_keep, low_pass)
low_back.defvjp(back_keep, back_low)

def layout_of(lengths, row_count):
    seq_ends = jnp.cumsum(lengths).astype(jnp.int32)
    seq_starts = (seq_ends - lengths).astype(jnp.int32)
    position = jnp.arange(row_count, dtype=jnp.int32)
    segment = lax.optimization_barrier(jnp.sum((position[:, None] >= seq_ends[None, :]).astype(jnp.int32), axis=1)).astype(jnp.int32)
    first_of = jnp.concatenate([seq_starts, seq_ends[-1:]])[segment]
    offset = (position - first_of).astype(jnp.int32)
    in_use = (position < seq_ends[-1]).astype(jnp.float32)
    allowed = (segment[:, None] == segment[None, :]) & (position[None, :] <= position[:, None])
    return (offset, allowed, in_use)

def rope_tables(offset, full_width):
    half_width = full_width // 2
    frequency = jnp.exp(jnp.arange(half_width, dtype=jnp.float32) * (-2.0 * math.log(ROPE_BASE) / full_width))
    angles = offset.astype(jnp.float32)[:, None] * frequency[None, :]
    return (jnp.cos(angles)[:, None, :], jnp.sin(angles)[:, None, :])

def rotate(vectors, cosine, sine_table, direction):
    half_width = vectors.shape[-1] // 2
    former = vectors[..., :half_width]
    latter = vectors[..., half_width:]
    return jnp.concatenate([former * cosine - direction * latter * sine_table, latter * cosine + direction * former * sine_table], axis=-1)

def causal_conv(signal, kernel, offset):
    length = signal.shape[0]
    result = jnp.zeros_like(signal)
    for lag_steps in range(CONV):
        shifted = jnp.pad(signal, ((lag_steps, 0), (0, 0)))[:length]
        keeper = (offset >= lag_steps).astype(signal.dtype)[:, None]
        result = result + shifted * keeper * kernel[:, CONV - 1 - lag_steps][None, :]
    return result

def rms_unit(residual):
    factor = lax.rsqrt(lax.optimization_barrier(jnp.mean(residual * residual, axis=1, keepdims=True)) + EPSILON)
    return residual * factor

def layer_forward(residual, offset, allowed, params):
    gain_pair, kernel, step_bias, log_rate, skip_gain, zx_weight, bc_weight, step_weight, query_weight, keyval_weight, mamba_out_weight, attn_out_weight, gate_up_weight, down_weight = params
    length = residual.shape[0]
    allowed_f = allowed.astype(residual.dtype)
    normed = low(rms_unit(residual) * gain_pair[0])
    zx_proj = low_back(jnp.einsum('td,dkc->tkc', normed, zx_weight, precision=PRECISE))
    bc_proj = jnp.dot(normed, bc_weight, precision=PRECISE)
    step_raw = low_back(jnp.dot(normed, step_weight, precision=PRECISE))
    query_proj = low_back(jnp.dot(normed, query_weight, precision=PRECISE))
    keyval = jnp.einsum('td,dkc->tkc', normed, keyval_weight, precision=PRECISE)
    conv_in = jnp.concatenate([zx_proj[:, 1], bc_proj], axis=1)
    conv_act = jax.nn.silu(causal_conv(conv_in, kernel, offset))
    inputs = conv_act[:, :NH * P_SIZE].reshape(length, NH, P_SIZE)
    b_state = conv_act[:, NH * P_SIZE:NH * P_SIZE + N]
    c_state = conv_act[:, NH * P_SIZE + N:]
    step_size = jax.nn.softplus(step_raw + step_bias[None, :])
    log_decay = jnp.cumsum(-step_size * jnp.exp(log_rate)[None, :], axis=0)
    cb_product = jnp.dot(c_state, b_state.T, precision=PRECISE)
    spread_gap = log_decay.T[:, :, None] - log_decay.T[:, None, :]
    decay_factor = jnp.exp(jnp.where(allowed[None], spread_gap, 0.0)) * allowed_f[None]
    scaled = inputs * step_size[:, :, None]
    ssm_out = jnp.einsum('hts,shp->thp', cb_product[None] * decay_factor, scaled, precision=PRECISE)
    ssm_out = ssm_out + skip_gain[None, :, None] * inputs
    gate_z = zx_proj[:, 0].reshape(length, NH, P_SIZE)
    gated_out = low((ssm_out * jax.nn.silu(gate_z)).reshape(length, NH * P_SIZE))
    cosine, sine_table = rope_tables(offset, HD)
    query_rot = rotate(query_proj.reshape(length, HQ, HD), cosine, sine_table, 1.0)
    key_rot = rotate(keyval[:, 0].reshape(length, KV, HD), cosine, sine_table, 1.0)
    values = keyval[:, 1].reshape(length, KV, HD)
    key_rep = jnp.repeat(key_rot, HQ // KV, axis=1)
    value_rep = jnp.repeat(values, HQ // KV, axis=1)
    scores = jnp.einsum('thd,shd->hts', query_rot, key_rep, precision=PRECISE) / math.sqrt(HD)
    scores = jnp.where(allowed[None], scores, -1e+30)
    attn_prob = jax.nn.softmax(scores, axis=-1)
    attended = low(jnp.einsum('hts,shd->thd', attn_prob, value_rep, precision=PRECISE).reshape(length, HQ * HD))
    mixer_out = jnp.dot(gated_out, mamba_out_weight.T, precision=PRECISE)
    mixer_out = mixer_out + jnp.dot(attended, attn_out_weight.T, precision=PRECISE)
    middle = residual + low_back(mixer_out)
    normed_two = low(rms_unit(middle) * gain_pair[1])
    gate_up = low_back(jnp.einsum('td,dkf->tkf', normed_two, gate_up_weight, precision=PRECISE))
    hidden = low(jax.nn.silu(gate_up[:, 0]) * gate_up[:, 1])
    return middle + low_back(jnp.dot(hidden, down_weight.T, precision=PRECISE))

def reference(layer_input, seq_lengths, norm_gains, conv_kernel, step_bias, log_rate, skip_gain, zx_weight, bc_weight, step_weight, query_weight, keyval_weight, mamba_out_weight, attn_out_weight, gate_up_weight, down_weight, cotangent):
    offsets, allowed_all, in_use = jax.vmap(partial(layout_of, row_count=TOK_DEV))(seq_lengths)
    params = tuple((argument.astype(jnp.float32) for argument in (norm_gains, conv_kernel, step_bias, log_rate, skip_gain, zx_weight, bc_weight, step_weight, query_weight, keyval_weight, mamba_out_weight, attn_out_weight, gate_up_weight, down_weight)))

    def run_layers(residual, params_all):
        blocks = residual.reshape(GROUPS, TOK_DEV, D)

        def block_pass(block_item):
            block_in, block_offset, block_allowed = block_item
            for layer_index in range(LAYERS):
                block_in = layer_forward(block_in, block_offset, block_allowed, tuple((member[layer_index] for member in params_all)))
            return block_in
        return lax.map(jax.checkpoint(block_pass), (blocks, offsets, allowed_all)).reshape(TOKENS, D)
    block_output, pull_back = jax.vjp(run_layers, layer_input.astype(jnp.float32), params)
    input_grad, param_grads = pull_back(cotangent.astype(jnp.float32) * in_use.reshape(TOKENS)[:, None])
    return (block_output, input_grad, param_grads[0], param_grads[1], param_grads[2], param_grads[3], param_grads[4], param_grads[5], param_grads[6], param_grads[7], param_grads[8], param_grads[9], param_grads[10], param_grads[11], param_grads[12], param_grads[13])
```

```python
import functools
import math

import jax
import jax.numpy as jnp
from jax import lax
from jax.experimental import pallas as pl
from jax.experimental.pallas import tpu as pltpu
from jax.sharding import PartitionSpec as P

D = 2048
NH = 48
P_SIZE = 64
N = 256
CONV = 4
HQ = 8
KV = 2
HD = 128
LAYERS = 2

EPSILON = 1e-05
ROPE_BASE = 10000.0
PRECISE = lax.Precision.HIGHEST
NO_BATCH = ((), ())
F32 = jnp.float32
BF16 = jnp.bfloat16


def silu_slope(pre_act):
    logistic = jax.nn.sigmoid(pre_act)
    return logistic * (1.0 + pre_act * (1.0 - logistic))


def contract_rows(left_side, right_side, precision=None):
    return lax.dot_general(
        left_side,
        right_side,
        (((0,), (0,)), NO_BATCH),
        precision=precision,
        preferred_element_type=jnp.float32,
    )


def times(left_side, right_side):
    return jnp.dot(left_side, right_side, preferred_element_type=F32)


def times_transposed(left_side, right_side):
    return lax.dot_general(
        left_side, right_side, (((1,), (1,)), NO_BATCH), preferred_element_type=F32
    )


def norm_back(grad_unit, unit_vec, factor):
    return factor * (grad_unit - unit_vec * jnp.mean(grad_unit * unit_vec, axis=1, keepdims=True))


def unit_of(residual):
    factor = lax.rsqrt(jnp.mean(residual * residual, axis=1, keepdims=True) + EPSILON)
    return residual * factor, factor


class Sizes:
    def __init__(self):
        self.n_tensor = lax.axis_size("tensor")
        self.tensor = lax.axis_index("tensor")
        self.heads = NH // self.n_tensor
        self.inner = self.heads * P_SIZE
        self.query_heads = HQ // self.n_tensor
        self.query_width = self.query_heads * HD
        self.head_start = self.tensor * self.heads
        self.keyval = self.tensor * self.query_heads // (HQ // KV)
        self.ff = 4096 // self.n_tensor
        widths = (2 * self.inner, self.query_width, 2 * HD, 2 * N, self.heads)
        ends = [0]
        for w in widths:
            ends.append(ends[-1] + w)
        self.cuts = list(zip(ends[:-1], ends[1:]))
        self.proj = -(-ends[-1] // 128) * 128
        self.mixed = self.inner + self.query_width


def scatter_tokens(partial, sizes):
    n = sizes.n_tensor
    rows = partial.shape[0] // n
    pieces = partial.astype(BF16).reshape(n, rows, D)
    got = lax.all_to_all(pieces, "tensor", 0, 0)
    return jnp.sum(got.astype(F32), axis=0)


def gather_tokens(own, sizes):
    n = sizes.n_tensor
    copies = jnp.broadcast_to(own.astype(BF16)[None], (n, *own.shape))
    return lax.all_to_all(copies, "tensor", 0, 0).reshape(n * own.shape[0], D)


class Ring:
    def __init__(self):
        place = lax.axis_index("dp")
        self.core, self.z, self.y = place % 2, (place // 2) % 4, place // 8
        self.near = ((0, 0), (0, 3), (0, 1), (0, 2), (1, 0), (1, 1), (1, 3), (1, 2))
        own = [self.block(dy, dz, self.core) for dy, dz in self.near]
        other = [self.block(dy, dz, 1 - self.core) for dy, dz in self.near]
        self.own_first = jnp.stack(own + other).astype(jnp.int32)
        self.other_first = jnp.stack(other + own).astype(jnp.int32)

    def block(self, dy, dz, core):
        return ((self.y ^ dy) * 4 + (self.z ^ dz)) * 2 + core

    def swap(self, value, mask):
        n = lax.axis_size("dp")
        return lax.ppermute(value, "dp", [(i, i ^ mask) for i in range(n)])


def place_blocks(order, parts, count):
    block = parts[0].shape[1:]

    def kernel(order_ref, *refs):
        ins, (out, held, came, left) = refs[: len(parts)], refs[len(parts) :]
        sources = [part.at[k] for part in ins for k in range(part.shape[0])]
        reads = [pltpu.make_async_copy(v, held.at[i], came.at[i]) for i, v in enumerate(sources)]
        writes = [
            pltpu.make_async_copy(held.at[i], out.at[order_ref[i]], left.at[i])
            for i in range(count)
        ]
        for c in reads:
            c.start()
        for r, w in zip(reads, writes):
            r.wait()
            w.start()
        for c in writes:
            c.wait()

    return pl.pallas_call(
        kernel,
        out_shape=jax.ShapeDtypeStruct((count, *block), parts[0].dtype),
        in_specs=[pl.BlockSpec(memory_space=pltpu.SMEM)]
        + [pl.BlockSpec(memory_space=pl.ANY)] * len(parts),
        out_specs=pl.BlockSpec(memory_space=pl.ANY),
        scratch_shapes=[
            pltpu.VMEM((count, *block), parts[0].dtype),
            pltpu.SemaphoreType.DMA((count,)),
            pltpu.SemaphoreType.DMA((count,)),
        ],
        compiler_params=pltpu.CompilerParams(vmem_limit_bytes=48 * 2**20),
        name="place_blocks",
    )(order, *parts)


def gather_rows(own, ring):
    rows, cols = own.shape
    first = own[None]
    second = ring.swap(first, 8)
    first_z = ring.swap(first, 6)
    second_z = ring.swap(second, 2)
    first_two = jnp.concatenate([first, first_z], axis=0)
    first_far = ring.swap(first_two, 2)
    second_two = jnp.concatenate([second, second_z], axis=0)
    second_far = ring.swap(second_two, 6)
    half = [first_two, first_far, second_two, second_far]
    rest = [ring.swap(v, 1) for v in half]
    placed = place_blocks(ring.own_first, half + rest, 16)
    return placed.reshape(16 * rows, cols)


def scatter_rows(own, other, ring):
    add = lambda a, b: (a.astype(F32) + b.astype(F32)).astype(BF16)
    got = ring.swap(other, 1)
    far = add(own[2:4], got[2:4])
    far_two = add(own[6:8], got[6:8])
    far = ring.swap(far, 2)
    far_two = ring.swap(far_two, 6)
    mid = add(add_two(own[1:2], got[1:2]), far[1:2])
    mid_two = add(add_two(own[5:6], got[5:6]), far_two[1:2])
    mid = ring.swap(mid, 6)
    mid_two = ring.swap(mid_two, 2)
    last_two = add(add_two(own[4:5], got[4:5]), add_two(far_two[0:1], mid_two))
    last_two = ring.swap(last_two, 8)
    last = add_two(add_two(own[0:1], got[0:1]), add_two(far[0:1], mid))
    return add_two(last, last_two)[0]


def add_two(a, b):
    return a.astype(F32) + b.astype(F32)


def weight_grads(pairs, order, split):
    count, step_blocks = 16, 4
    steps = count // step_blocks
    tokens = pairs[0][0].shape[0]
    rows = pairs[0][0].shape[1] // count
    widths = [y.shape[1] for _, y in pairs]
    total = sum(widths)
    n_x = len(pairs) * step_blocks

    def fill(out_ref, xs, ys):
        at = 0
        for k, (y, w) in enumerate(zip(ys, widths)):
            x = jnp.concatenate([v[...] for v in xs[k * step_blocks : (k + 1) * step_blocks]], axis=1)
            grad = lax.dot_general(x, y[...], (((0,), (0,)), NO_BATCH), preferred_element_type=F32)
            out_ref[:, :, at : at + w] = grad.astype(BF16).reshape(step_blocks, rows, w)
            at += w

    def kernel(order_ref, *refs):
        xs, ys, outs = refs[:n_x], refs[n_x : n_x + len(pairs)], refs[n_x + len(pairs) :]
        if not split:
            fill(outs[0], xs, ys)
            return
        step = pl.program_id(0)

        @pl.when(step < steps // 2)
        def _():
            fill(outs[0], xs, ys)

        @pl.when(step >= steps // 2)
        def _():
            fill(outs[1], xs, ys)

    half = steps // 2
    block = (step_blocks, rows, total)
    if split:
        out_shape = [jax.ShapeDtypeStruct((count // 2, rows, total), BF16)] * 2
        out_specs = [
            pl.BlockSpec(block, lambda i, o: (jnp.minimum(i, half - 1), 0, 0)),
            pl.BlockSpec(block, lambda i, o: (jnp.maximum(i - half, 0), 0, 0)),
        ]
    else:
        out_shape = [jax.ShapeDtypeStruct((count, rows, total), BF16)]
        out_specs = [pl.BlockSpec(block, lambda i, o: (i, 0, 0))]

    def x_spec(k):
        return pl.BlockSpec((tokens, rows), lambda i, o: (0, o[i * step_blocks + k]))

    return pl.pallas_call(
        kernel,
        grid_spec=pltpu.PrefetchScalarGridSpec(
            num_scalar_prefetch=1,
            grid=(steps,),
            in_specs=[x_spec(k) for _ in pairs for k in range(step_blocks)]
            + [pl.BlockSpec((tokens, w), lambda i, o: (0, 0)) for w in widths],
            out_specs=out_specs,
        ),
        out_shape=out_shape,
        compiler_params=pltpu.CompilerParams(vmem_limit_bytes=48 * 2**20),
        cost_estimate=pl.CostEstimate(
            flops=2 * tokens * rows * count * total,
            bytes_accessed=2 * rows * count * total,
            transcendentals=0,
        ),
        name="weight_grads",
    )(order, *(x for x, _ in pairs for _ in range(step_blocks)), *(y for _, y in pairs))


def sum_everywhere(own, sizes):
    n_dp, n = lax.axis_size("dp"), sizes.n_tensor
    part = own.shape[0] // n_dp
    got = lax.all_to_all(own.reshape(n_dp, part, 128), "dp", 0, 0)
    mine = jnp.sum(got, axis=0)
    over_tensor = lax.all_to_all(jnp.broadcast_to(mine[None], (n, part, 128)), "tensor", 0, 0)
    over_dp = lax.all_to_all(
        jnp.broadcast_to(over_tensor[None], (n_dp, n, part, 128)), "dp", 0, 0
    )
    return over_dp.transpose(1, 0, 2, 3).reshape(n, n_dp * part, 128)


def dot_nn(a, b):
    return lax.dot_general(
        a.astype(BF16), b.astype(BF16), (((1,), (0,)), NO_BATCH), preferred_element_type=F32
    )


def dot_nt(a, b):
    return lax.dot_general(
        a.astype(BF16), b.astype(BF16), (((1,), (1,)), NO_BATCH), preferred_element_type=F32
    )


def dot_tn(a, b):
    return lax.dot_general(
        a.astype(BF16), b.astype(BF16), (((0,), (0,)), NO_BATCH), preferred_element_type=F32
    )


def logistic(v):
    return 1.0 / (1.0 + jnp.exp(-v))


def softplus(v):
    return jnp.maximum(v, 0.0) + jnp.log1p(jnp.exp(-jnp.abs(v)))


class Mixer:
    def __init__(self, cuts, inner, proj_ref, taps_ref, heads_ref, column_ref, row_ref):
        length = proj_ref.shape[0]
        self.inner, self.pairs, self.length = inner, inner // 128, length
        (self.zx0, self.zx1), (q0, q1), (kv0, _), (bc0, bc1), (st0, _) = cuts
        offset = column_ref[:, 0:1]
        self.keep = [(offset >= float(j)).astype(F32) for j in range(CONV)]
        across = lax.broadcasted_iota(jnp.int32, (length, length), 1)
        down = lax.broadcasted_iota(jnp.int32, (length, length), 0)
        self.allowed = (column_ref[:, 1:2] == row_ref[0:1, :]) & (across <= down)
        self.lower = (across <= down).astype(F32)
        self.upper = (across >= down).astype(F32)
        self.first_half = lax.broadcasted_iota(jnp.int32, (1, 128), 1) < P_SIZE
        self.query, self.key = proj_ref[:, q0:q1], proj_ref[:, kv0 : kv0 + HD]
        self.value = proj_ref[:, kv0 + HD : kv0 + 2 * HD]
        self.signal = jnp.concatenate([proj_ref[:, inner : 2 * inner], proj_ref[:, bc0:bc1]], axis=1)
        pre = self.signal * self.keep[0] * taps_ref[0:1, :]
        for j in range(1, CONV):
            pre = pre + pltpu.roll(self.signal, j, 0) * self.keep[j] * taps_ref[j : j + 1, :]
        self.pre = pre
        self.pre_gate = logistic(pre)
        self.act = pre * self.pre_gate
        self.b_state = self.act[:, inner : inner + N].astype(BF16)
        self.c_state = self.act[:, inner + N :].astype(BF16)
        self.heads = heads_ref
        self.step_pre = proj_ref[:, st0 : st0 + 128] + heads_ref[0:1, :]
        self.step = softplus(self.step_pre)
        self.rate = heads_ref[1:2, :]
        self.total = jnp.dot(self.lower, -self.step * self.rate, precision=PRECISE)
        self.total_t = self.total.T
        self.cb = dot_nt(self.c_state, self.b_state)
        self.proj_ref = proj_ref

    def by_half(self, first, second):
        return jnp.where(self.first_half, first, second)

    def decay(self, head):
        gap = self.total[:, head : head + 1] - self.total_t[head : head + 1, :]
        return jnp.where(self.allowed, jnp.exp(jnp.where(self.allowed, gap, 0.0)), 0.0)

    def pair(self, p):
        lanes = slice(128 * p, 128 * p + 128)
        a, b = 2 * p, 2 * p + 1
        inputs = self.act[:, lanes]
        step = self.by_half(self.step[:, a : a + 1], self.step[:, b : b + 1])
        skip = self.by_half(self.heads[2:3, a : a + 1], self.heads[2:3, b : b + 1])
        gate = self.proj_ref[:, lanes]
        return inputs, step, skip, gate, inputs * step

    def prob(self, query_rot, key_rot):
        scores = dot_nt(query_rot, key_rot) * (1.0 / math.sqrt(HD))
        scores = jnp.where(self.allowed, scores, -1e30)
        weight = jnp.exp(scores - jnp.max(scores, axis=1, keepdims=True))
        return weight / jnp.sum(weight, axis=1, keepdims=True)


def turn(v, cosine, sine, direction):
    return v * cosine + (direction * sine) * pltpu.roll(v, HD // 2, 1)


def mixer_forward_kernel(cuts, inner, proj, taps, heads, column, row, cosine, sine, out):
    m = Mixer(cuts, inner, proj, taps, heads, column, row)
    for p in range(m.pairs):
        inputs, step, skip, gate, scaled = m.pair(p)
        scaled = scaled.astype(BF16)
        mixed = [dot_nn(m.cb * m.decay(2 * p + k), scaled) for k in range(2)]
        ssm = m.by_half(*mixed) + skip * inputs
        out[:, 128 * p : 128 * p + 128] = (ssm * gate * logistic(gate)).astype(BF16)
    query_rot = turn(m.query, cosine[...], sine[...], 1.0)
    key_rot = turn(m.key, cosine[...], sine[...], 1.0)
    out[:, inner:] = dot_nn(m.prob(query_rot, key_rot), m.value).astype(BF16)


def mixer_backward_kernel(
    cuts, inner, proj, taps, heads, column, row, cosine, sine, grad, out, taps_grad, heads_grad
):
    m = Mixer(cuts, inner, proj, taps, heads, column, row)
    lane = lax.broadcasted_iota(jnp.int32, (1, 128), 1)
    cos, sin = cosine[...], sine[...]
    (q0, q1), (kv0, _), (bc0, bc1), (st0, _) = cuts[1:]

    query_rot, key_rot = turn(m.query, cos, sin, 1.0), turn(m.key, cos, sin, 1.0)
    prob = m.prob(query_rot, key_rot)
    attended_grad = grad[:, inner:]
    out[:, kv0 + HD : kv0 + 2 * HD] = dot_tn(prob, attended_grad).astype(BF16)
    prob_grad = dot_nt(attended_grad, m.value)
    inner_sum = jnp.sum(prob * prob_grad, axis=1, keepdims=True)
    score_grad = prob * (prob_grad - inner_sum) * (1.0 / math.sqrt(HD))
    out[:, q0:q1] = turn(dot_nn(score_grad, key_rot), cos, sin, -1.0).astype(BF16)
    out[:, kv0 : kv0 + HD] = turn(dot_tn(score_grad, query_rot), cos, sin, -1.0).astype(BF16)

    cb_grad = jnp.zeros((m.length, m.length), F32)
    down_sums = jnp.zeros((m.length, 128), F32)
    across_sums = []
    step_grad = jnp.zeros((m.length, 128), F32)
    skip_grad = jnp.zeros((1, 128), F32)
    inputs_grads = []
    for p in range(m.pairs):
        inputs, step, skip, gate, scaled = m.pair(p)
        gated_grad = grad[:, 128 * p : 128 * p + 128]
        sig = logistic(gate)
        ssm_grad = gated_grad * gate * sig
        scaled_b, ssm_grad_b = scaled.astype(BF16), ssm_grad.astype(BF16)
        ssm, scaled_grad = [], []
        for k in range(2):
            h = 2 * p + k
            decay = m.decay(h)
            mixing = m.cb * decay
            mixing_b = mixing.astype(BF16)
            ssm.append(dot_nn(mixing_b, scaled_b))
            scaled_grad.append(dot_tn(mixing_b, ssm_grad_b))
            mine = m.first_half if k == 0 else jnp.logical_not(m.first_half)
            mixing_grad = dot_nt(jnp.where(mine, ssm_grad, 0.0), scaled_b)
            cb_grad = cb_grad + mixing_grad * decay
            gap_grad = mixing_grad * mixing
            down_sums = jnp.where(lane == h, jnp.sum(gap_grad, axis=1, keepdims=True), down_sums)
            across_sums.append(jnp.sum(gap_grad, axis=0, keepdims=True))
        ssm = m.by_half(*ssm) + skip * inputs
        scaled_grad = m.by_half(*scaled_grad)
        slope = sig * (1.0 + gate * (1.0 - sig))
        out[:, 128 * p : 128 * p + 128] = (gated_grad * ssm * slope).astype(BF16)
        inputs_grads.append(scaled_grad * step + ssm_grad * skip)
        by_step, by_skip = scaled_grad * inputs, ssm_grad * inputs
        for k in range(2):
            mine = m.first_half if k == 0 else jnp.logical_not(m.first_half)
            here = lane == 2 * p + k
            step_grad = jnp.where(
                here, jnp.sum(jnp.where(mine, by_step, 0.0), axis=1, keepdims=True), step_grad
            )
            own_skip = jnp.sum(jnp.where(mine, by_skip, 0.0), axis=0, keepdims=True)
            skip_grad = jnp.where(here, jnp.sum(own_skip, axis=1, keepdims=True), skip_grad)

    across = jnp.concatenate(
        across_sums + [jnp.zeros((128 - len(across_sums), m.length), F32)], axis=0
    )
    term_grad = jnp.dot(m.upper, down_sums - across.T, precision=PRECISE)
    step_grad = step_grad - term_grad * m.rate
    step_pre_grad = step_grad * logistic(m.step_pre)
    out[:, st0 : st0 + 128] = step_pre_grad.astype(BF16)
    heads_grad[0:1, :] = jnp.sum(step_pre_grad, axis=0, keepdims=True)
    heads_grad[1:2, :] = -jnp.sum(term_grad * m.step, axis=0, keepdims=True) * m.rate
    heads_grad[2:3, :] = skip_grad
    heads_grad[3:8, :] = jnp.zeros((5, 128), F32)

    c_grad = dot_nn(cb_grad, m.b_state)
    b_grad = dot_tn(cb_grad, m.c_state)
    act_grad = jnp.concatenate(inputs_grads + [b_grad, c_grad], axis=1)
    pre_grad = act_grad * (m.pre_gate * (1.0 + m.pre * (1.0 - m.pre_gate)))
    signal_grad = jnp.zeros_like(pre_grad)
    for j in range(CONV):
        masked = pre_grad * m.keep[j]
        back = masked if j == 0 else pltpu.roll(masked, m.length - j, 0)
        shifted = m.signal if j == 0 else pltpu.roll(m.signal, j, 0)
        signal_grad = signal_grad + back * taps[j : j + 1, :]
        taps_grad[j : j + 1, :] = jnp.sum(masked * shifted, axis=0, keepdims=True)
    taps_grad[CONV:8, :] = jnp.zeros((8 - CONV, pre_grad.shape[1]), F32)
    out[:, inner : 2 * inner] = signal_grad[:, :inner].astype(BF16)
    out[:, bc0:bc1] = signal_grad[:, inner:].astype(BF16)


def whole(shapes):
    return [pl.BlockSpec(s, lambda: (0,) * len(s)) for s in shapes]


def mixer_forward(proj, smalls, geometry, sizes):
    taps, heads = smalls
    length = proj.shape[0]
    ins = (proj, taps, heads, *geometry)
    return pl.pallas_call(
        functools.partial(mixer_forward_kernel, sizes.cuts, sizes.inner),
        in_specs=whole([v.shape for v in ins]),
        out_specs=whole([(length, sizes.mixed)])[0],
        out_shape=jax.ShapeDtypeStruct((length, sizes.mixed), BF16),
        compiler_params=pltpu.CompilerParams(vmem_limit_bytes=48 * 2**20),
        name="mixer_forward",
    )(*ins)


def mixer_backward(mixed_grad, proj, smalls, geometry, sizes):
    taps, heads = smalls
    length = proj.shape[0]
    ins = (proj, taps, heads, *geometry, mixed_grad)
    outs = [
        jax.ShapeDtypeStruct((length, sizes.proj), BF16),
        jax.ShapeDtypeStruct(taps.shape, F32),
        jax.ShapeDtypeStruct(heads.shape, F32),
    ]
    return pl.pallas_call(
        functools.partial(mixer_backward_kernel, sizes.cuts, sizes.inner),
        in_specs=whole([v.shape for v in ins]),
        out_specs=whole([v.shape for v in outs]),
        out_shape=outs,
        compiler_params=pltpu.CompilerParams(vmem_limit_bytes=48 * 2**20),
        name="mixer_backward",
    )(*ins)


def own_smalls(smalls, sizes):
    kernel, step_bias, log_rate, skip_gain = smalls
    own = jnp.concatenate(
        [
            lax.dynamic_slice_in_dim(kernel, sizes.head_start * P_SIZE, sizes.inner, 0),
            kernel[NH * P_SIZE :],
        ],
        axis=0,
    )
    taps = jnp.pad(own[:, ::-1].T, ((0, 8 - CONV), (0, 0)))
    heads = jnp.stack([step_bias, jnp.exp(log_rate), skip_gain])
    heads = lax.dynamic_slice_in_dim(heads, sizes.head_start, sizes.heads, 1)
    return taps, jnp.pad(heads, ((0, 5), (0, 128 - sizes.heads)))


def layout_of(lengths, row_count):
    seq_ends = jnp.cumsum(lengths)
    seq_starts = seq_ends - lengths
    position = jnp.arange(row_count, dtype=jnp.int32)
    past = position[:, None] >= seq_ends[None, :]
    segment = jnp.sum(past.astype(jnp.int32), axis=1)
    first_of = jnp.max(jnp.where(past, seq_ends[None, :], 0), axis=1)
    offset = position - first_of
    in_use = (position < seq_ends[-1]).astype(F32)
    offset, segment = offset.astype(F32), segment.astype(F32)
    column = jnp.pad(jnp.stack([offset, segment], axis=1), ((0, 0), (0, 126)))
    row = jnp.broadcast_to(segment[None], (8, row_count))
    half_width = HD // 2
    frequency = jnp.exp(
        jnp.arange(half_width, dtype=F32) * (-2.0 * math.log(ROPE_BASE) / HD)
    )
    angles = offset[:, None] * frequency[None, :]
    cosine, sine = jnp.cos(angles), jnp.sin(angles)
    tables = jnp.concatenate([cosine, cosine], axis=1), jnp.concatenate([-sine, sine], axis=1)
    return (column, row, *tables), in_use


def body(
    layer_input,
    seq_lengths,
    norm_gains,
    conv_kernel,
    step_bias,
    log_rate,
    skip_gain,
    zx_weight,
    bc_weight,
    step_weight,
    query_weight,
    keyval_weight,
    mamba_out_weight,
    attn_out_weight,
    gate_up_weight,
    down_weight,
    cotangent,
):
    sizes = Sizes()
    ring = Ring()
    length = layer_input.shape[0]
    chunk = length // sizes.n_tensor
    first = sizes.tensor * chunk
    rows_own = zx_weight.shape[1]
    gate_up_width = 2 * sizes.ff
    geometry, in_use = layout_of(seq_lengths[0], length)

    def proj_part(layer):
        step_own = lax.dynamic_slice_in_dim(step_weight[layer], sizes.head_start, sizes.heads, 1)
        pair = lax.dynamic_slice_in_dim(keyval_weight[layer], sizes.keyval * HD, HD, 2)
        parts = [
            zx_weight[layer].reshape(rows_own, -1),
            query_weight[layer],
            pair.reshape(rows_own, -1),
            bc_weight[layer],
            step_own,
        ]
        used = sum(p.shape[1] for p in parts)
        return parts + [jnp.zeros((rows_own, sizes.proj - used), BF16)]

    def out_part(layer):
        return [mamba_out_weight[layer], attn_out_weight[layer]]

    def ffn_part(layer):
        return [gate_up_weight[layer].reshape(rows_own, -1), down_weight[layer]]

    def gathered(parts):
        return lax.all_gather(jnp.concatenate(parts, axis=1), "dp", axis=0, tiled=True)

    mixed_width = sizes.mixed
    w_proj, w_out, w_ffn = {}, {}, {}
    w_proj[0] = gather_rows(jnp.concatenate(proj_part(0), axis=1), ring)
    rest = gathered(out_part(0) + ffn_part(0))
    w_out[0], w_ffn[0] = rest[:, :mixed_width], rest[:, mixed_width:]
    joint = gathered(proj_part(1) + out_part(1))
    w_proj[1], w_out[1] = joint[:, : sizes.proj], joint[:, sizes.proj :]
    w_ffn[1] = gathered(ffn_part(1))
    smalls = [
        own_smalls((conv_kernel[l], step_bias[l], log_rate[l], skip_gain[l]), sizes)
        for l in range(LAYERS)
    ]

    def own_rows(v):
        return lax.dynamic_slice_in_dim(v, first, chunk, 0)

    residual = own_rows(layer_input).astype(F32)
    kept = []
    for layer in range(LAYERS):
        unit_one, factor_one = unit_of(residual)
        if layer == 0:
            full_unit = unit_of(layer_input.astype(F32))[0]
            normed = (full_unit * norm_gains[layer, 0][None, :]).astype(BF16)
        else:
            normed = gather_tokens(unit_one * norm_gains[layer, 0][None, :], sizes)
        proj = times(normed, w_proj[layer])
        mixed = mixer_forward(proj, smalls[layer], geometry, sizes)
        middle = residual + scatter_tokens(times_transposed(mixed, w_out[layer]), sizes)
        unit_two, factor_two = unit_of(middle)
        normed_two = gather_tokens(unit_two * norm_gains[layer, 1][None, :], sizes)
        gate_up = times(normed_two, w_ffn[layer][:, :gate_up_width])
        hidden = (jax.nn.silu(gate_up[:, : sizes.ff]) * gate_up[:, sizes.ff :]).astype(BF16)
        ffn = times_transposed(hidden, w_ffn[layer][:, gate_up_width:])
        residual = middle + scatter_tokens(ffn, sizes)
        kept.append(
            (unit_one, factor_one, normed, proj, mixed, unit_two, factor_two, normed_two, gate_up, hidden)
        )
    block_output = gather_tokens(residual, sizes).astype(F32)

    out_grad = cotangent * in_use.astype(BF16)[:, None]
    gradient = own_rows(out_grad).astype(F32)
    scattered = [None] * LAYERS
    small_list = [None] * LAYERS
    for layer in reversed(range(LAYERS)):
        unit_one, factor_one, normed, proj, mixed, unit_two, factor_two, normed_two, gate_up, hidden = kept[layer]
        if layer < LAYERS - 1:
            out_grad = gather_tokens(gradient, sizes)
        hidden_grad = times(out_grad, w_ffn[layer][:, gate_up_width:])
        gate_pre, up_value = gate_up[:, : sizes.ff], gate_up[:, sizes.ff :]
        gate_up_grad = jnp.concatenate(
            [hidden_grad * up_value * silu_slope(gate_pre), hidden_grad * jax.nn.silu(gate_pre)],
            axis=1,
        ).astype(BF16)
        partial = times_transposed(gate_up_grad, w_ffn[layer][:, :gate_up_width])
        normed_two_grad = scatter_tokens(partial, sizes)
        ffn_pairs = ((normed_two, gate_up_grad), (out_grad, hidden))
        if layer == 0:
            other, own = weight_grads(ffn_pairs, ring.other_first, True)
            ffn_sum = scatter_rows(own, other, ring)
        gain_two_grad = jnp.sum(normed_two_grad * unit_two, axis=0)
        middle_grad = gradient + norm_back(
            normed_two_grad * norm_gains[layer, 1][None, :], unit_two, factor_two
        )
        mix_grad = gather_tokens(middle_grad, sizes)
        mixed_grad = times(mix_grad, w_out[layer])
        proj_grad, *mixer_smalls = mixer_backward(
            mixed_grad, proj, smalls[layer], geometry, sizes
        )
        normed_grad = scatter_tokens(times_transposed(proj_grad, w_proj[layer]), sizes)
        mixer_pairs = ((normed, proj_grad), (mix_grad, mixed))
        if layer == 0:
            other, own = weight_grads(mixer_pairs, ring.other_first, True)
            mixer_sum = scatter_rows(own, other, ring)
        else:
            in_order = jnp.arange(16, dtype=jnp.int32)
            (joint,) = weight_grads(mixer_pairs + ffn_pairs, in_order, False)
            joint = joint.reshape(D, joint.shape[2])
            joint = lax.psum_scatter(joint, "dp", tiled=True)
            cut = sizes.proj + mixed_width
            mixer_sum, ffn_sum = joint[:, :cut], joint[:, cut:]
        gain_one_grad = jnp.sum(normed_grad * unit_one, axis=0)
        gradient = middle_grad + norm_back(
            normed_grad * norm_gains[layer, 0][None, :], unit_one, factor_one
        )
        scattered[layer] = (ffn_sum, mixer_sum)
        small_list[layer] = (jnp.stack([gain_one_grad, gain_two_grad], axis=0), *mixer_smalls)
    input_grad = gather_tokens(gradient, sizes).astype(F32)

    n = sizes.n_tensor
    flat = jnp.concatenate(
        [jnp.stack([m[k] for m in small_list], axis=0).reshape(-1) for k in range(3)]
    )
    packed = -(-flat.size // 16384) * 16384
    flat = jnp.pad(flat, (0, packed - flat.size)).reshape(-1, 128)
    every = sum_everywhere(flat, sizes).reshape(n, packed)
    at, found = 0, []
    channels = sizes.inner + 2 * N
    for shape in ((LAYERS, 2, D), (LAYERS, 8, channels), (LAYERS, 8, 128)):
        size = math.prod(shape)
        found.append(every[:, at : at + size].reshape(n, *shape))
        at += size
    taps = found[1][:, :, :CONV]
    own_taps = taps[..., : sizes.inner].transpose(1, 2, 0, 3).reshape(LAYERS, CONV, NH * P_SIZE)
    taps = jnp.concatenate([own_taps, jnp.sum(taps[..., sizes.inner :], axis=0)], axis=2)
    taps = taps[:, ::-1].transpose(0, 2, 1)
    heads = found[2][:, :, :3, : sizes.heads].transpose(2, 1, 0, 3).reshape(3, LAYERS, NH)
    small_out = (jnp.sum(found[0], axis=0), taps, heads[0], heads[1], heads[2])

    (q0, q1), (kv0, kv1), (bc0, bc1), (st0, st1) = sizes.cuts[1:]
    shared = jnp.stack([m[:, kv0:st1] for _, m in scattered], axis=0)
    width = shared.shape[2]
    rows = rows_own // n
    pieces = shared.reshape(LAYERS, n, rows, width).transpose(1, 0, 2, 3)
    got = lax.all_to_all(pieces, "tensor", 0, 0)
    keyval_got = got[..., : 2 * HD].astype(F32)
    per_pair = n // KV
    keyval_grad = jnp.stack(
        [jnp.sum(keyval_got[k * per_pair : (k + 1) * per_pair], axis=0) for k in range(KV)], axis=0
    )
    keyval_grad = keyval_grad.reshape(KV, LAYERS, rows, 2, HD).transpose(1, 2, 3, 0, 4)
    keyval_grad = keyval_grad.reshape(LAYERS, rows, 2, KV * HD)
    bc_grad = jnp.sum(got[..., bc0 - kv0 : bc1 - kv0].astype(F32), axis=0)
    step_grad = got[..., st0 - kv0 :].astype(F32).transpose(1, 2, 0, 3).reshape(LAYERS, rows, NH)

    def stacked(pick, dims):
        return jnp.stack([pick(*s).astype(F32).reshape(rows_own, *dims) for s in scattered], axis=0)

    zx_grad = stacked(lambda f, m: m[:, : 2 * sizes.inner], (2, sizes.inner))
    query_grad = stacked(lambda f, m: m[:, q0:q1], (sizes.query_width,))
    mamba_out_grad = stacked(
        lambda f, m: m[:, sizes.proj : sizes.proj + sizes.inner], (sizes.inner,)
    )
    attn_out_grad = stacked(lambda f, m: m[:, sizes.proj + sizes.inner :], (sizes.query_width,))
    gate_up_grad = stacked(lambda f, m: f[:, :gate_up_width], (2, sizes.ff))
    down_grad = stacked(lambda f, m: f[:, gate_up_width:], (sizes.ff,))
    return (
        block_output,
        input_grad,
        *small_out,
        zx_grad,
        bc_grad,
        step_grad,
        query_grad,
        keyval_grad,
        mamba_out_grad,
        attn_out_grad,
        gate_up_grad,
        down_grad,
    )


def solution(mesh):
    placed = (
        P("dp", None),
        P("dp", None),
        P(),
        P(),
        P(),
        P(),
        P(),
        P(None, "dp", None, "tensor"),
        P(None, "dp", None),
        P(None, "dp", None),
        P(None, "dp", "tensor"),
        P(None, "dp", None, None),
        P(None, "dp", "tensor"),
        P(None, "dp", "tensor"),
        P(None, "dp", None, "tensor"),
        P(None, "dp", "tensor"),
        P("dp", None),
    )
    return jax.shard_map(
        body,
        mesh=mesh,
        in_specs=placed,
        out_specs=(
            P("dp", None),
            P("dp", None),
            P(),
            P(),
            P(),
            P(),
            P(),
            P(None, "dp", None, "tensor"),
            P(None, ("dp", "tensor"), None),
            P(None, ("dp", "tensor"), None),
            P(None, "dp", "tensor"),
            P(None, ("dp", "tensor"), None, None),
            P(None, "dp", "tensor"),
            P(None, "dp", "tensor"),
            P(None, "dp", None, "tensor"),
            P(None, "dp", "tensor"),
        ),
        check_vma=False,
    )
```

```python
import functools
import math

import jax
import jax.numpy as jnp
from jax import lax
from jax.experimental import pallas as pl
from jax.experimental.pallas import tpu as pltpu
from jax.sharding import PartitionSpec as P

D = 2048
NH = 48
P_SIZE = 64
N = 256
CONV = 4
HQ = 8
KV = 2
HD = 128
LAYERS = 2

EPSILON = 1e-05
ROPE_BASE = 10000.0
PRECISE = lax.Precision.HIGHEST
NO_BATCH = ((), ())
F32 = jnp.float32
BF16 = jnp.bfloat16


def times(left_side, right_side):
    return jnp.dot(left_side, right_side, preferred_element_type=F32)


def times_transposed(left_side, right_side):
    return lax.dot_general(
        left_side, right_side, (((1,), (1,)), NO_BATCH), preferred_element_type=F32
    )


def norm_back(grad_unit, unit_vec, factor):
    return factor * (grad_unit - unit_vec * jnp.mean(grad_unit * unit_vec, axis=1, keepdims=True))


def unit_of(residual):
    factor = lax.rsqrt(jnp.mean(residual * residual, axis=1, keepdims=True) + EPSILON)
    return residual * factor, factor


class Sizes:
    def __init__(self):
        self.n_tensor = lax.axis_size("tensor")
        self.tensor = lax.axis_index("tensor")
        self.heads = NH // self.n_tensor
        self.inner = self.heads * P_SIZE
        self.query_heads = HQ // self.n_tensor
        self.query_width = self.query_heads * HD
        self.head_start = self.tensor * self.heads
        self.keyval = self.tensor * self.query_heads // (HQ // KV)
        self.ff = 4096 // self.n_tensor
        widths = (2 * self.inner, self.query_width, 2 * HD, 2 * N, self.heads)
        ends = [0]
        for w in widths:
            ends.append(ends[-1] + w)
        self.cuts = list(zip(ends[:-1], ends[1:]))
        self.proj = -(-ends[-1] // 128) * 128
        self.mixed = self.inner + self.query_width
        self.left = ends[1]
        self.rest = self.proj - self.left


class Ring:
    def __init__(self):
        place = lax.axis_index("dp")
        self.core, self.z, self.y = place % 2, (place // 2) % 4, place // 8
        near = ((0, 0), (0, 3), (0, 1), (0, 2), (1, 0), (1, 1), (1, 3), (1, 2))
        own = [self.block(dy, dz, self.core) for dy, dz in near]
        other = [self.block(dy, dz, 1 - self.core) for dy, dz in near]
        self.own_first = jnp.stack(own + other).astype(jnp.int32)
        self.other_first = jnp.stack(other + own).astype(jnp.int32)

    def block(self, dy, dz, core):
        return ((self.y ^ dy) * 4 + (self.z ^ dz)) * 2 + core

    def swap(self, value, mask):
        n = lax.axis_size("dp")
        return lax.ppermute(value, "dp", [(i, i ^ mask) for i in range(n)])


def place_blocks(order, parts, count):
    block = parts[0].shape[1:]

    def kernel(order_ref, *refs):
        ins, (out, held, came, left) = refs[: len(parts)], refs[len(parts) :]
        sources = [part.at[k] for part in ins for k in range(part.shape[0])]
        reads = [pltpu.make_async_copy(v, held.at[i], came.at[i]) for i, v in enumerate(sources)]
        writes = [
            pltpu.make_async_copy(held.at[i], out.at[order_ref[i]], left.at[i])
            for i in range(count)
        ]
        for c in reads:
            c.start()
        for r, w in zip(reads, writes):
            r.wait()
            w.start()
        for c in writes:
            c.wait()

    return pl.pallas_call(
        kernel,
        out_shape=jax.ShapeDtypeStruct((count, *block), parts[0].dtype),
        in_specs=[pl.BlockSpec(memory_space=pltpu.SMEM)]
        + [pl.BlockSpec(memory_space=pl.ANY)] * len(parts),
        out_specs=pl.BlockSpec(memory_space=pl.ANY),
        scratch_shapes=[
            pltpu.VMEM((count, *block), parts[0].dtype),
            pltpu.SemaphoreType.DMA((count,)),
            pltpu.SemaphoreType.DMA((count,)),
        ],
        compiler_params=pltpu.CompilerParams(vmem_limit_bytes=48 * 2**20),
        cost_estimate=TINY,
        name="place_blocks",
    )(order, *parts)


def together(*values):
    return lax.optimization_barrier(values)


def after(value, pairs):
    flat = [v for pair in pairs for v in pair]
    value, *flat = together(value, *flat)
    return value, tuple(zip(flat[::2], flat[1::2]))


def paired_sum(a, b, c, d):
    return (a + b) + (c + d)


class RowGather:
    def __init__(self, own, ring):
        self.ring, self.first = ring, own[None]

    def step_y(self):
        return self.ring.swap(self.first, 8), self.ring.swap(self.first, 6)

    def step_z(self, arrived):
        self.second, near = arrived
        self.first = jnp.concatenate([self.first, near], axis=0)
        return (self.ring.swap(self.second, 2),)

    def step_far(self, arrived):
        self.second = jnp.concatenate([self.second, arrived[0]], axis=0)
        return (
            self.ring.swap(self.first, 2),
            self.ring.swap(self.second, 6),
            self.ring.swap(self.first, 1),
            self.ring.swap(self.second, 1),
        )

    def step_core(self, arrived):
        self.first_far, self.second_far, self.first_other, self.second_other = arrived
        return self.ring.swap(self.first_far, 1), self.ring.swap(self.second_far, 1)

    def blocks(self, arrived):
        return [
            self.first,
            self.first_far,
            self.second,
            self.second_far,
            self.first_other,
            arrived[0],
            self.second_other,
            arrived[1],
        ]

    def rows(self, blocks):
        placed = place_blocks(self.ring.own_first, blocks, 16)
        return placed.reshape(-1, placed.shape[2])


def add_blocks(outs, dtype):
    terms = [t for out in outs for block in out for t in block]
    rows, cols = terms[0][0].shape[1:]

    def kernel(*refs):
        at = 0
        for ref, out in zip(refs[len(terms) :], outs):
            for k, block in enumerate(out):
                total = refs[at][0].astype(F32)
                for term in refs[at + 1 : at + len(block)]:
                    total = total + term[0].astype(F32)
                ref[k] = total.astype(dtype)
                at += len(block)

    def spec(index):
        return pl.BlockSpec((1, rows, cols), lambda i: (index, 0, 0))

    return pl.pallas_call(
        kernel,
        grid=(1,),
        in_specs=[spec(index) for _, index in terms],
        out_specs=[pl.BlockSpec((len(out), rows, cols), lambda i: (0, 0, 0)) for out in outs],
        out_shape=[jax.ShapeDtypeStruct((len(out), rows, cols), dtype) for out in outs],
        compiler_params=pltpu.CompilerParams(vmem_limit_bytes=48 * 2**20),
        cost_estimate=TINY,
        name="add_blocks",
    )(*(array for array, _ in terms))


class RowScatter:
    def __init__(self, halves, ring):
        self.ring, (self.other, self.own) = ring, halves

    def both(self, index):
        return [(self.own, index), (self.got, index)]

    def step_core(self):
        return (self.ring.swap(self.other, 1),)

    def add_far(self, arrived):
        (self.got,) = arrived
        return add_blocks([[self.both(2), self.both(3)], [self.both(6), self.both(7)]], BF16)

    def step_z(self, far):
        return self.ring.swap(far[0], 2), self.ring.swap(far[1], 6)

    def add_mid(self, arrived):
        self.far, self.far_two = arrived
        return add_blocks(
            [[self.both(1) + [(self.far, 1)]], [self.both(5) + [(self.far_two, 1)]]], BF16
        )

    def step_z_again(self, mid):
        return self.ring.swap(mid[0], 6), self.ring.swap(mid[1], 2)

    def add_last(self, arrived):
        self.mid, mid_two = arrived
        return add_blocks([[self.both(4) + [(self.far_two, 0), (mid_two, 0)]]], BF16)

    def step_y(self, last):
        return (self.ring.swap(last[0], 8),)

    def total(self, arrived):
        (last,) = arrived
        terms = self.both(0) + [(self.far, 0), (self.mid, 0), (last, 0)]
        return add_blocks([[terms]], F32)[0][0]


TINY = pl.CostEstimate(flops=1, bytes_accessed=1, transcendentals=0)


def rows_matmul(x, order, parts, width, weight):
    tokens, block, n = x.shape[0], parts[0].shape[1], len(parts)

    def kernel(order_ref, x_ref, w_ref, *refs):
        refs[n][...] = mm(x_ref[...], w_ref[...], NN)
        total = None
        for k, part in enumerate(refs[:n]):
            lanes = [
                pl.ds(pl.multiple_of(order_ref[2 * k + h] * block, block), block) for h in (0, 1)
            ]
            rows = jnp.concatenate([x_ref[:, v] for v in lanes], axis=1)
            term = mm(rows, part[:, :, :width].reshape(2 * block, width), NN)
            total = term if total is None else total + term
        refs[n + 1][...] = total

    return pl.pallas_call(
        kernel,
        in_specs=[pl.BlockSpec(memory_space=pltpu.SMEM)]
        + [pl.BlockSpec(memory_space=pltpu.VMEM)] * (2 + n),
        out_specs=[pl.BlockSpec(memory_space=pltpu.VMEM)] * 2,
        out_shape=[
            jax.ShapeDtypeStruct((tokens, weight.shape[1]), F32),
            jax.ShapeDtypeStruct((tokens, width), F32),
        ],
        compiler_params=pltpu.CompilerParams(vmem_limit_bytes=56 * 2**20),
        cost_estimate=TINY,
        name="rows_matmul",
    )(order, x, weight, *parts)


def rows_out(mixed, order, parts, start):
    tokens, block, n = mixed.shape[0], parts[0].shape[1], len(parts)

    def kernel(order_ref, x_ref, *refs):
        out = refs[n]
        for k, part in enumerate(refs[:n]):
            rows = part[:, :, start:].reshape(2 * block, x_ref.shape[1])
            term = dot_nt(x_ref[...], rows).astype(BF16)
            for h in (0, 1):
                lanes = pl.ds(pl.multiple_of(order_ref[2 * k + h] * block, block), block)
                out[:, lanes] = term[:, h * block : (h + 1) * block]

    return pl.pallas_call(
        kernel,
        in_specs=[pl.BlockSpec(memory_space=pltpu.SMEM)]
        + [pl.BlockSpec(memory_space=pltpu.VMEM)] * (1 + n),
        out_specs=pl.BlockSpec(memory_space=pltpu.VMEM),
        out_shape=jax.ShapeDtypeStruct((tokens, D), BF16),
        compiler_params=pltpu.CompilerParams(vmem_limit_bytes=56 * 2**20),
        cost_estimate=TINY,
        name="rows_out",
    )(order, mixed, *parts)


def weight_grads(pairs, order, split):
    count, step_blocks = 16, 4
    steps = count // step_blocks
    tokens = pairs[0][0].shape[0]
    rows = pairs[0][0].shape[1] // count
    widths = [y.shape[1] for _, y in pairs]
    total = sum(widths)
    n_x = len(pairs) * step_blocks

    def fill(out_ref, xs, ys):
        at = 0
        for k, (y, w) in enumerate(zip(ys, widths)):
            x = jnp.concatenate([v[...] for v in xs[k * step_blocks : (k + 1) * step_blocks]], axis=1)
            grad = lax.dot_general(x, y[...], (((0,), (0,)), NO_BATCH), preferred_element_type=F32)
            out_ref[:, :, at : at + w] = grad.astype(BF16).reshape(step_blocks, rows, w)
            at += w

    def kernel(order_ref, *refs):
        xs, ys, outs = refs[:n_x], refs[n_x : n_x + len(pairs)], refs[n_x + len(pairs) :]
        if not split:
            fill(outs[0], xs, ys)
            return
        step = pl.program_id(0)

        @pl.when(step < steps // 2)
        def _():
            fill(outs[0], xs, ys)

        @pl.when(step >= steps // 2)
        def _():
            fill(outs[1], xs, ys)

    half = steps // 2
    block = (step_blocks, rows, total)
    if split:
        out_shape = [jax.ShapeDtypeStruct((count // 2, rows, total), BF16)] * 2
        out_specs = [
            pl.BlockSpec(block, lambda i, o: (jnp.minimum(i, half - 1), 0, 0)),
            pl.BlockSpec(block, lambda i, o: (jnp.maximum(i - half, 0), 0, 0)),
        ]
    else:
        out_shape = [jax.ShapeDtypeStruct((count, rows, total), BF16)]
        out_specs = [pl.BlockSpec(block, lambda i, o: (i, 0, 0))]

    def x_spec(k):
        return pl.BlockSpec((tokens, rows), lambda i, o: (0, o[i * step_blocks + k]))

    return pl.pallas_call(
        kernel,
        grid_spec=pltpu.PrefetchScalarGridSpec(
            num_scalar_prefetch=1,
            grid=(steps,),
            in_specs=[x_spec(k) for _ in pairs for k in range(step_blocks)]
            + [pl.BlockSpec((tokens, w), lambda i, o: (0, 0)) for w in widths],
            out_specs=out_specs,
        ),
        out_shape=out_shape,
        compiler_params=pltpu.CompilerParams(vmem_limit_bytes=48 * 2**20),
        cost_estimate=TINY,
        name="weight_grads",
    )(order, *(x for x, _ in pairs for _ in range(step_blocks)), *(y for _, y in pairs))


def dot_nn(a, b):
    return lax.dot_general(
        a.astype(BF16), b.astype(BF16), (((1,), (0,)), NO_BATCH), preferred_element_type=F32
    )


def dot_nt(a, b):
    return lax.dot_general(
        a.astype(BF16), b.astype(BF16), (((1,), (1,)), NO_BATCH), preferred_element_type=F32
    )


def dot_tn(a, b):
    return lax.dot_general(
        a.astype(BF16), b.astype(BF16), (((0,), (0,)), NO_BATCH), preferred_element_type=F32
    )


def logistic(v):
    return 1.0 / (1.0 + jnp.exp(-v))


def softplus(v):
    return jnp.maximum(v, 0.0) + jnp.log1p(jnp.exp(-jnp.abs(v)))


class Mixer:
    def __init__(self, cuts, inner, proj_ref, rest_ref, taps_ref, heads_ref, column_ref, row_ref):
        length, left = proj_ref.shape
        self.inner, self.pairs, self.length = inner, inner // 128, length
        (self.zx0, self.zx1), (q0, q1), (kv0, _), (bc0, bc1), (st0, _) = cuts
        offset = column_ref[:, 0:1]
        self.keep = [(offset >= float(j)).astype(F32) for j in range(CONV)]
        across = lax.broadcasted_iota(jnp.int32, (length, length), 1)
        down = lax.broadcasted_iota(jnp.int32, (length, length), 0)
        self.allowed = (column_ref[:, 1:2] == row_ref[0:1, :]) & (across <= down)
        self.lower = (across <= down).astype(F32)
        self.upper = (across >= down).astype(F32)
        self.first_half = lax.broadcasted_iota(jnp.int32, (1, 128), 1) < P_SIZE
        q0, q1, kv0 = q0 - left, q1 - left, kv0 - left
        self.query, self.key = rest_ref[:, q0:q1], rest_ref[:, kv0 : kv0 + HD]
        self.value = rest_ref[:, kv0 + HD : kv0 + 2 * HD]
        self.signal = jnp.concatenate(
            [proj_ref[:, inner : 2 * inner], rest_ref[:, bc0 - left : bc1 - left]], axis=1
        )
        pre = self.signal * self.keep[0] * taps_ref[CONV - 1 : CONV, :]
        for j in range(1, CONV):
            tap = taps_ref[CONV - 1 - j : CONV - j, :]
            pre = pre + pltpu.roll(self.signal, j, 0) * self.keep[j] * tap
        self.pre = pre
        self.pre_gate = logistic(pre)
        self.act = pre * self.pre_gate
        self.b_state = self.act[:, inner : inner + N].astype(BF16)
        self.c_state = self.act[:, inner + N :].astype(BF16)
        self.heads = heads_ref
        self.step_pre = rest_ref[:, st0 - left : st0 - left + 128] + heads_ref[0:1, :]
        self.step = softplus(self.step_pre)
        self.rate = heads_ref[1:2, :]
        self.total = jnp.dot(self.lower, -self.step * self.rate, precision=PRECISE)
        self.total_t = self.total.T
        self.cb = dot_nt(self.c_state, self.b_state)
        self.proj_ref = proj_ref

    def by_half(self, first, second):
        return jnp.where(self.first_half, first, second)

    def decay(self, head):
        gap = self.total[:, head : head + 1] - self.total_t[head : head + 1, :]
        return jnp.where(self.allowed, jnp.exp(jnp.where(self.allowed, gap, 0.0)), 0.0)

    def pair(self, p):
        lanes = slice(128 * p, 128 * p + 128)
        a, b = 2 * p, 2 * p + 1
        inputs = self.act[:, lanes]
        step = self.by_half(self.step[:, a : a + 1], self.step[:, b : b + 1])
        skip = self.by_half(self.heads[2:3, a : a + 1], self.heads[2:3, b : b + 1])
        gate = self.proj_ref[:, lanes]
        return inputs, step, skip, gate, inputs * step

    def prob(self, query_rot, key_rot):
        scores = dot_nt(query_rot, key_rot) * (1.0 / math.sqrt(HD))
        scores = jnp.where(self.allowed, scores, -1e30)
        weight = jnp.exp(scores - jnp.max(scores, axis=1, keepdims=True))
        return weight / jnp.sum(weight, axis=1, keepdims=True)


def turn(v, cosine, sine, direction):
    return v * cosine + (direction * sine) * pltpu.roll(v, HD // 2, 1)


def mixer_forward_kernel(cuts, inner, proj, rest, taps, heads, column, row, cosine, sine, out):
    m = Mixer(cuts, inner, proj, rest, taps, heads, column, row)
    for p in range(m.pairs):
        inputs, step, skip, gate, scaled = m.pair(p)
        scaled = scaled.astype(BF16)
        mixed = [dot_nn(m.cb * m.decay(2 * p + k), scaled) for k in range(2)]
        ssm = m.by_half(*mixed) + skip * inputs
        out[:, 128 * p : 128 * p + 128] = (ssm * gate * logistic(gate)).astype(BF16)
    query_rot = turn(m.query, cosine[...], sine[...], 1.0)
    key_rot = turn(m.key, cosine[...], sine[...], 1.0)
    out[:, inner:] = dot_nn(m.prob(query_rot, key_rot), m.value).astype(BF16)


def mixer_backward_kernel(
    cuts, inner, proj, rest, taps, heads, column, row, cosine, sine, grad, out, out_rest, taps_grad, heads_grad
):
    m = Mixer(cuts, inner, proj, rest, taps, heads, column, row)
    lane = lax.broadcasted_iota(jnp.int32, (1, 128), 1)
    cos, sin = cosine[...], sine[...]
    (q0, q1), (kv0, _), (bc0, bc1), (st0, _) = cuts[1:]
    left = proj.shape[1]
    q0, q1, kv0 = q0 - left, q1 - left, kv0 - left

    query_rot, key_rot = turn(m.query, cos, sin, 1.0), turn(m.key, cos, sin, 1.0)
    prob = m.prob(query_rot, key_rot)
    attended_grad = grad[:, inner:]
    out_rest[:, kv0 + HD : kv0 + 2 * HD] = dot_tn(prob, attended_grad).astype(BF16)
    prob_grad = dot_nt(attended_grad, m.value)
    inner_sum = jnp.sum(prob * prob_grad, axis=1, keepdims=True)
    score_grad = prob * (prob_grad - inner_sum) * (1.0 / math.sqrt(HD))
    out_rest[:, q0:q1] = turn(dot_nn(score_grad, key_rot), cos, sin, -1.0).astype(BF16)
    out_rest[:, kv0 : kv0 + HD] = turn(dot_tn(score_grad, query_rot), cos, sin, -1.0).astype(BF16)

    cb_grad = jnp.zeros((m.length, m.length), F32)
    down_sums = jnp.zeros((m.length, 128), F32)
    across_sums = []
    step_grad = jnp.zeros((m.length, 128), F32)
    skip_grad = jnp.zeros((1, 128), F32)
    inputs_grads = []
    for p in range(m.pairs):
        inputs, step, skip, gate, scaled = m.pair(p)
        gated_grad = grad[:, 128 * p : 128 * p + 128]
        sig = logistic(gate)
        ssm_grad = gated_grad * gate * sig
        scaled_b, ssm_grad_b = scaled.astype(BF16), ssm_grad.astype(BF16)
        ssm, scaled_grad = [], []
        for k in range(2):
            h = 2 * p + k
            decay = m.decay(h)
            mixing = m.cb * decay
            mixing_b = mixing.astype(BF16)
            ssm.append(dot_nn(mixing_b, scaled_b))
            scaled_grad.append(dot_tn(mixing_b, ssm_grad_b))
            mine = m.first_half if k == 0 else jnp.logical_not(m.first_half)
            mixing_grad = dot_nt(jnp.where(mine, ssm_grad, 0.0), scaled_b)
            cb_grad = cb_grad + mixing_grad * decay
            gap_grad = mixing_grad * mixing
            down_sums = jnp.where(lane == h, jnp.sum(gap_grad, axis=1, keepdims=True), down_sums)
            across_sums.append(jnp.sum(gap_grad, axis=0, keepdims=True))
        ssm = m.by_half(*ssm) + skip * inputs
        scaled_grad = m.by_half(*scaled_grad)
        slope = sig * (1.0 + gate * (1.0 - sig))
        out[:, 128 * p : 128 * p + 128] = (gated_grad * ssm * slope).astype(BF16)
        inputs_grads.append(scaled_grad * step + ssm_grad * skip)
        by_step, by_skip = scaled_grad * inputs, ssm_grad * inputs
        for k in range(2):
            mine = m.first_half if k == 0 else jnp.logical_not(m.first_half)
            here = lane == 2 * p + k
            step_grad = jnp.where(
                here, jnp.sum(jnp.where(mine, by_step, 0.0), axis=1, keepdims=True), step_grad
            )
            own_skip = jnp.sum(jnp.where(mine, by_skip, 0.0), axis=0, keepdims=True)
            skip_grad = jnp.where(here, jnp.sum(own_skip, axis=1, keepdims=True), skip_grad)

    across = jnp.concatenate(
        across_sums + [jnp.zeros((128 - len(across_sums), m.length), F32)], axis=0
    )
    term_grad = jnp.dot(m.upper, down_sums - across.T, precision=PRECISE)
    step_grad = step_grad - term_grad * m.rate
    step_pre_grad = step_grad * logistic(m.step_pre)
    out_rest[:, st0 - left : st0 - left + 128] = step_pre_grad.astype(BF16)
    heads_grad[0:1, :] = jnp.sum(step_pre_grad, axis=0, keepdims=True)
    heads_grad[1:2, :] = -jnp.sum(term_grad * m.step, axis=0, keepdims=True) * m.rate
    heads_grad[2:3, :] = skip_grad
    heads_grad[3:8, :] = jnp.zeros((5, 128), F32)

    c_grad = dot_nn(cb_grad, m.b_state)
    b_grad = dot_tn(cb_grad, m.c_state)
    act_grad = jnp.concatenate(inputs_grads + [b_grad, c_grad], axis=1)
    pre_grad = act_grad * (m.pre_gate * (1.0 + m.pre * (1.0 - m.pre_gate)))
    signal_grad = jnp.zeros_like(pre_grad)
    for j in range(CONV):
        masked = pre_grad * m.keep[j]
        back = masked if j == 0 else pltpu.roll(masked, m.length - j, 0)
        shifted = m.signal if j == 0 else pltpu.roll(m.signal, j, 0)
        k = CONV - 1 - j
        signal_grad = signal_grad + back * taps[k : k + 1, :]
        taps_grad[k : k + 1, :] = jnp.sum(masked * shifted, axis=0, keepdims=True)
    taps_grad[CONV:8, :] = jnp.zeros((8 - CONV, pre_grad.shape[1]), F32)
    out[:, inner : 2 * inner] = signal_grad[:, :inner].astype(BF16)
    out_rest[:, bc0 - left : bc1 - left] = signal_grad[:, inner:].astype(BF16)


def mm(a, b, dims):
    return lax.dot_general(a, b, (dims, NO_BATCH), preferred_element_type=F32)


NN, NT = ((1,), (0,)), ((1,), (1,))


def proj_forward(x, weight, sizes):
    tokens, depth = x.shape
    tile = 256
    first, steps = sizes.left // tile, sizes.proj // tile

    def kernel(x_ref, w_ref, left, rest):
        value = mm(x_ref[...], w_ref[...], NN)
        step = pl.program_id(0)

        @pl.when(step < first)
        def _():
            left[...] = value

        @pl.when(step >= first)
        def _():
            rest[...] = value

    return pl.pallas_call(
        kernel,
        grid=(steps,),
        in_specs=[
            pl.BlockSpec((tokens, depth), lambda i: (0, 0)),
            pl.BlockSpec((depth, tile), lambda i: (0, i)),
        ],
        out_specs=[
            pl.BlockSpec((tokens, tile), lambda i: (0, jnp.minimum(i, first - 1))),
            pl.BlockSpec((tokens, tile), lambda i: (0, jnp.maximum(i - first, 0))),
        ],
        out_shape=[
            jax.ShapeDtypeStruct((tokens, sizes.left), F32),
            jax.ShapeDtypeStruct((tokens, sizes.rest), F32),
        ],
        compiler_params=pltpu.CompilerParams(vmem_limit_bytes=48 * 2**20),
        cost_estimate=TINY,
        name="proj_forward",
    )(x, weight)


def proj_backward(grads, w_zx, w_rest):
    rest = w_rest[:, : grads[1].shape[1]]
    return times_transposed(grads[0], w_zx) + times_transposed(grads[1], rest)


def feed_forward_call(kernel, name, x, tiled, weight, ff, tiled_outs, tile=256):
    tokens, depth = x[0].shape
    steps = ff // tile

    def whole_kernel(*refs):
        *rest, out, total = refs
        step = pl.program_id(0)
        term = kernel(*rest)

        @pl.when(step == 0)
        def _():
            total[...] = term

        @pl.when(step > 0)
        def _():
            total[...] += term

        @pl.when(step == steps - 1)
        def _():
            out[...] = total[...].astype(BF16)

    def column(part):
        return pl.BlockSpec((depth, tile), lambda i: (0, part * steps + i))

    def tile_spec(_):
        return pl.BlockSpec((tokens, tile), lambda i: (0, i))

    return pl.pallas_call(
        whole_kernel,
        grid=(steps,),
        in_specs=[pl.BlockSpec((tokens, depth), lambda i: (0, 0)) for _ in x]
        + [tile_spec(v) for v in tiled]
        + [column(k) for k in range(3)],
        out_specs=[tile_spec(v) for v in tiled_outs]
        + [pl.BlockSpec((tokens, depth), lambda i: (0, 0))],
        out_shape=[jax.ShapeDtypeStruct((tokens, ff), v) for v in tiled_outs]
        + [jax.ShapeDtypeStruct((tokens, depth), BF16)],
        scratch_shapes=[pltpu.VMEM((tokens, depth), F32)],
        compiler_params=pltpu.CompilerParams(vmem_limit_bytes=56 * 2**20),
        cost_estimate=TINY,
        name=name,
    )(*x, *tiled, weight, weight, weight)


def gate_grads(hidden_grad, gate, up):
    sig = logistic(gate)
    gate_grad = hidden_grad * up * (sig * (1.0 + gate * (1.0 - sig)))
    return gate_grad.astype(BF16), (hidden_grad * gate * sig).astype(BF16)


def feed_forward(x, weight, ff):
    def kernel(x_ref, w_gate, w_up, w_down, gate_ref, up_ref, hidden_ref):
        gate, up = mm(x_ref[...], w_gate[...], NN), mm(x_ref[...], w_up[...], NN)
        hidden = (gate * logistic(gate) * up).astype(BF16)
        gate_ref[...], up_ref[...], hidden_ref[...] = gate, up, hidden
        return mm(hidden, w_down[...], NT)

    return feed_forward_call(kernel, "feed_forward", (x,), (), weight, ff, (F32, F32, BF16))


def feed_forward_both(x, grad, weight, ff):
    def kernel(x_ref, grad_ref, w_gate, w_up, w_down, hidden_ref, gate_out, up_out):
        gate, up = mm(x_ref[...], w_gate[...], NN), mm(x_ref[...], w_up[...], NN)
        hidden_ref[...] = (gate * logistic(gate) * up).astype(BF16)
        grads = gate_grads(mm(grad_ref[...], w_down[...], NN), gate, up)
        gate_out[...], up_out[...] = grads
        return mm(grads[0], w_gate[...], NT) + mm(grads[1], w_up[...], NT)

    return feed_forward_call(
        kernel, "feed_forward_both", (x, grad), (), weight, ff, (BF16, BF16, BF16)
    )


def feed_forward_back(grad, gate, up, weight, ff):
    def kernel(grad_ref, gate_ref, up_ref, w_gate, w_up, w_down, gate_out, up_out):
        grads = gate_grads(mm(grad_ref[...], w_down[...], NN), gate_ref[...], up_ref[...])
        gate_out[...], up_out[...] = grads
        return mm(grads[0], w_gate[...], NT) + mm(grads[1], w_up[...], NT)

    return feed_forward_call(
        kernel, "feed_forward_back", (grad,), (gate, up), weight, ff, (BF16, BF16)
    )


def whole(shapes):
    return [pl.BlockSpec(memory_space=pltpu.VMEM) for _ in shapes]


def mixer_forward(proj, smalls, geometry, sizes):
    length = proj[0].shape[0]
    ins = (*proj, *smalls, *geometry)
    return pl.pallas_call(
        functools.partial(mixer_forward_kernel, sizes.cuts, sizes.inner),
        in_specs=whole([v.shape for v in ins]),
        out_specs=whole([(length, sizes.mixed)])[0],
        out_shape=jax.ShapeDtypeStruct((length, sizes.mixed), BF16),
        compiler_params=pltpu.CompilerParams(vmem_limit_bytes=48 * 2**20),
        cost_estimate=TINY,
        name="mixer_forward",
    )(*ins)


def mixer_backward(mixed_grad, proj, smalls, geometry, sizes):
    ins = (*proj, *smalls, *geometry, mixed_grad)
    outs = [jax.ShapeDtypeStruct(v.shape, BF16) for v in proj]
    outs += [jax.ShapeDtypeStruct(v.shape, F32) for v in smalls]
    return pl.pallas_call(
        functools.partial(mixer_backward_kernel, sizes.cuts, sizes.inner),
        in_specs=whole([v.shape for v in ins]),
        out_specs=whole([v.shape for v in outs]),
        out_shape=outs,
        compiler_params=pltpu.CompilerParams(vmem_limit_bytes=48 * 2**20),
        cost_estimate=TINY,
        name="mixer_backward",
    )(*ins)


def chunk_norm(got, residual, gain):
    n, rows, width = got.shape

    def kernel(got_ref, residual_ref, gain_ref, out, copies):
        total = residual_ref[...]
        for k in range(n):
            total = total + got_ref[k].astype(F32)
        out[...] = total
        normed = (unit_of(total)[0] * gain_ref[...]).astype(BF16)
        for k in range(n):
            copies[k] = normed

    ins = (got, residual, gain[None])
    outs = [jax.ShapeDtypeStruct((rows, width), F32), jax.ShapeDtypeStruct(got.shape, BF16)]
    return pl.pallas_call(
        kernel,
        in_specs=whole([v.shape for v in ins]),
        out_specs=whole([v.shape for v in outs]),
        out_shape=outs,
        cost_estimate=TINY,
        name="chunk_norm",
    )(*ins)


def chunk_norm_back(got, residual, gain, gradient):
    n, rows, width = got.shape

    def kernel(got_ref, residual_ref, gain_ref, gradient_ref, out, copies, gain_grad):
        normed_grad = got_ref[0].astype(F32)
        for k in range(1, n):
            normed_grad = normed_grad + got_ref[k].astype(F32)
        unit, factor = unit_of(residual_ref[...])
        gain_grad[...] = jnp.sum(normed_grad * unit, axis=0, keepdims=True)
        total = gradient_ref[...] + norm_back(normed_grad * gain_ref[...], unit, factor)
        out[...] = total
        total = total.astype(BF16)
        for k in range(n):
            copies[k] = total

    ins = (got, residual, gain[None], gradient)
    outs = [
        jax.ShapeDtypeStruct((rows, width), F32),
        jax.ShapeDtypeStruct(got.shape, BF16),
        jax.ShapeDtypeStruct((1, width), F32),
    ]
    return pl.pallas_call(
        kernel,
        in_specs=whole([v.shape for v in ins]),
        out_specs=whole([v.shape for v in outs]),
        out_shape=outs,
        cost_estimate=TINY,
        name="chunk_norm_back",
    )(*ins)


def own_smalls(smalls, sizes):
    kernel, step_bias, log_rate, skip_gain = smalls
    own = jnp.concatenate(
        [
            lax.dynamic_slice_in_dim(kernel, sizes.head_start * P_SIZE, sizes.inner, 0),
            kernel[NH * P_SIZE :],
        ],
        axis=0,
    )
    taps = jnp.pad(own.T, ((0, 8 - CONV), (0, 0)))
    heads = jnp.stack([step_bias, jnp.exp(log_rate), skip_gain])
    heads = lax.dynamic_slice_in_dim(heads, sizes.head_start, sizes.heads, 1)
    return taps, jnp.pad(heads, ((0, 5), (0, 128 - sizes.heads)))


def layout_of(lengths, row_count):
    seq_ends = jnp.cumsum(lengths)
    seq_starts = seq_ends - lengths
    position = jnp.arange(row_count, dtype=jnp.int32)
    past = position[:, None] >= seq_ends[None, :]
    segment = jnp.sum(past.astype(jnp.int32), axis=1)
    first_of = jnp.max(jnp.where(past, seq_ends[None, :], 0), axis=1)
    offset = position - first_of
    in_use = (position < seq_ends[-1]).astype(F32)
    offset, segment = offset.astype(F32), segment.astype(F32)
    column = jnp.pad(jnp.stack([offset, segment], axis=1), ((0, 0), (0, 126)))
    row = jnp.broadcast_to(segment[None], (8, row_count))
    half_width = HD // 2
    frequency = jnp.exp(
        jnp.arange(half_width, dtype=F32) * (-2.0 * math.log(ROPE_BASE) / HD)
    )
    angles = offset[:, None] * frequency[None, :]
    cosine, sine = jnp.cos(angles), jnp.sin(angles)
    tables = jnp.concatenate([cosine, cosine], axis=1), jnp.concatenate([-sine, sine], axis=1)
    return (column, row, *tables), in_use


def body(
    layer_input,
    seq_lengths,
    norm_gains,
    conv_kernel,
    step_bias,
    log_rate,
    skip_gain,
    zx_weight,
    bc_weight,
    step_weight,
    query_weight,
    keyval_weight,
    mamba_out_weight,
    attn_out_weight,
    gate_up_weight,
    down_weight,
    cotangent,
):
    sizes = Sizes()
    ring = Ring()
    length = layer_input.shape[0]
    chunk = length // sizes.n_tensor
    first = sizes.tensor * chunk
    rows_own = zx_weight.shape[1]
    gate_up_width = 2 * sizes.ff
    geometry, in_use = layout_of(seq_lengths[0], length)

    def zx_part(layer):
        return [zx_weight[layer].reshape(rows_own, -1)]

    def rest_part(layer):
        step_own = lax.dynamic_slice_in_dim(step_weight[layer], sizes.head_start, sizes.heads, 1)
        pair = lax.dynamic_slice_in_dim(keyval_weight[layer], sizes.keyval * HD, HD, 2)
        parts = [query_weight[layer], pair.reshape(rows_own, -1), bc_weight[layer], step_own]
        used = sum(p.shape[1] for p in parts)
        return parts + [jnp.zeros((rows_own, sizes.rest - used), BF16)]

    def out_part(layer):
        return [mamba_out_weight[layer], attn_out_weight[layer]]

    def ffn_part(layer):
        return [gate_up_weight[layer].reshape(rows_own, -1), down_weight[layer]]

    def joined(parts):
        return jnp.concatenate(parts, axis=1)

    def gathered(parts):
        return lax.all_gather(joined(parts), "dp", axis=0, tiled=True)

    smalls = [
        own_smalls((conv_kernel[l], step_bias[l], log_rate[l], skip_gain[l]), sizes)
        for l in range(LAYERS)
    ]

    def own_rows(v):
        return lax.dynamic_slice_in_dim(v, first, chunk, 0)

    def gained(unit, layer, which):
        return unit * norm_gains[layer, which][None, :]

    def to_chunks(partial):
        return partial.astype(BF16).reshape(sizes.n_tensor, chunk, D)

    def exchange(pieces):
        return lax.all_to_all(pieces, "tensor", 0, 0)

    def copies(own):
        return jnp.broadcast_to(own.astype(BF16)[None], (sizes.n_tensor, *own.shape))

    def summed(got):
        return jnp.sum(got.astype(F32), axis=0)

    def full(got):
        return got.reshape(length, D)

    w_ffn = {}
    rows = RowGather(joined(rest_part(0) + out_part(0)), ring)
    w_zx_a = gathered(zx_part(0))
    moved = together(*rows.step_y())
    moved = together(*rows.step_z(moved))
    moved = together(*rows.step_far(moved))
    blocks_a = rows.blocks(together(*rows.step_core(moved)))
    w_ffn[0] = gathered(ffn_part(0))
    w_ffn[1] = gathered(ffn_part(1))

    residual_a = own_rows(layer_input).astype(F32)
    full_unit = unit_of(layer_input.astype(F32))[0]
    normed_a = gained(full_unit, 0, 0).astype(BF16)
    proj_a = rows_matmul(normed_a, ring.own_first, blocks_a, sizes.rest, w_zx_a)
    mixed_a = mixer_forward(proj_a, smalls[0], geometry, sizes)
    own_c = joined(zx_part(1) + rest_part(1) + out_part(1))
    rows_c = RowGather(own_c, ring)
    partial = rows_out(mixed_a, ring.own_first, blocks_a, sizes.rest)
    partial, *moved = together(partial, *rows_c.step_y())
    got = exchange(to_chunks(partial))
    got, *moved = together(got, *rows_c.step_z(moved))
    middle_a, own = chunk_norm(got, residual_a, norm_gains[0, 1])
    got = exchange(own)
    moved = rows_c.step_far(moved)
    normed_b = full(got)
    gate_a, up_a, hidden_a, partial = feed_forward(normed_b, w_ffn[0], sizes.ff)
    got = exchange(to_chunks(partial))
    got, *moved = together(got, *moved)
    moved = rows_c.step_core(moved)

    residual_c, own = chunk_norm(got, middle_a, norm_gains[1, 0])
    got = exchange(own)
    w_joint_c = rows_c.rows(rows_c.blocks(moved))
    got, w_joint_c = together(got, w_joint_c)
    w_out_c = w_joint_c[:, sizes.proj :]
    normed_c = full(got)
    proj_c = proj_forward(normed_c, w_joint_c, sizes)
    mixed_c = mixer_forward(proj_c, smalls[1], geometry, sizes)
    got = exchange(to_chunks(times_transposed(mixed_c, w_out_c)))
    middle_c, own = chunk_norm(got, residual_c, norm_gains[1, 1])
    got = exchange(own)
    w_rest_a = rows.rows(blocks_a)
    got, w_rest_a = together(got, w_rest_a)
    normed_d = full(got)

    out_grad_c = cotangent * in_use.astype(BF16)[:, None]
    gradient = own_rows(out_grad_c).astype(F32)
    hidden_c, gate_grad_c, up_grad_c, partial = feed_forward_both(
        normed_d, out_grad_c, w_ffn[1], sizes.ff
    )
    pairs = ((normed_d, gate_grad_c), (normed_d, up_grad_c), (out_grad_c, hidden_c))
    partial, pairs = after(partial, pairs)
    got = exchange(to_chunks(partial))
    in_order = jnp.arange(16, dtype=jnp.int32)
    (ffn_c,) = weight_grads(pairs, in_order, False)
    got, ffn_c = together(got, ffn_c)
    ffn_c = lax.psum_scatter(ffn_c.reshape(D, -1), "dp", tiled=True)
    middle_grad, own, gain_d = chunk_norm_back(got, middle_c, norm_gains[1, 1], gradient)
    got = exchange(own)
    mix_grad_c = full(got)
    ffn_partial = times_transposed(hidden_c, w_ffn[1][:, gate_up_width:])
    mix_grad_c, ffn_partial = together(mix_grad_c, ffn_partial)
    block_got = exchange(to_chunks(ffn_partial))
    mixed_grad = times(mix_grad_c, w_out_c)
    *proj_grad_c, taps_c, heads_c = mixer_backward(mixed_grad, proj_c, smalls[1], geometry, sizes)
    partial = proj_backward(proj_grad_c, w_joint_c[:, : sizes.left], w_joint_c[:, sizes.left :])
    partial, block_got = together(partial, block_got)
    mix_c_pairs = (*((normed_c, v) for v in proj_grad_c), (mix_grad_c, mixed_c))
    got = exchange(to_chunks(partial))
    gradient, own, gain_c = chunk_norm_back(got, residual_c, norm_gains[1, 0], middle_grad)
    got = exchange(own)

    out_grad_a = full(got)
    gate_grad_a, up_grad_a, partial = feed_forward_back(
        out_grad_a, gate_a, up_a, w_ffn[0], sizes.ff
    )
    pairs = ((normed_b, gate_grad_a), (normed_b, up_grad_a), (out_grad_a, hidden_a))
    pairs = (*mix_c_pairs, *pairs)
    partial, pairs = after(partial, pairs)
    got = exchange(to_chunks(partial))
    (joint,) = weight_grads(pairs, in_order, False)
    got, joint = together(got, joint)
    joint = lax.psum_scatter(joint.reshape(D, -1), "dp", tiled=True)
    middle_grad, own, gain_b = chunk_norm_back(got, middle_a, norm_gains[0, 1], gradient)
    got = exchange(own)
    mix_grad_a = full(got)
    block_own = copies(middle_c + summed(block_got))
    mix_grad_a, block_own = together(mix_grad_a, block_own)
    block_got = exchange(block_own)
    mixed_grad = times(mix_grad_a, w_rest_a[:, sizes.rest :])
    *proj_grad_a, taps_a, heads_a = mixer_backward(mixed_grad, proj_a, smalls[0], geometry, sizes)
    (q0, q1), (kv0, kv1), (bc0, bc1), (st0, st1) = sizes.cuts[1:]
    pairs = (*((normed_a, v) for v in proj_grad_a), (mix_grad_a, mixed_a))
    *proj_grad_a, other, own = together(
        *proj_grad_a, *weight_grads(pairs, ring.other_first, True)
    )
    mix_a = RowScatter((other, own), ring)
    partial = proj_backward(proj_grad_a, w_zx_a, w_rest_a)
    pieces = to_chunks(partial)
    pieces, block_got, *moved = together(pieces, block_got, *mix_a.step_core())
    got = exchange(pieces)
    moved = mix_a.step_z(mix_a.add_far(moved))
    block_output = full(block_got).astype(F32)

    n = sizes.n_tensor
    gain_a = jnp.sum(partial * full_unit, axis=0, keepdims=True)
    small = (
        jnp.concatenate([gain_a, gain_b, gain_c, gain_d]),
        jnp.stack([taps_a[:CONV], taps_c[:CONV]]),
        jnp.stack([heads_a[:3], heads_c[:3]]),
    )
    flat = jnp.concatenate([v.reshape(-1, 128) for v in small])
    got, flat = together(got, flat)
    small_got = exchange(jnp.broadcast_to(flat[None], (n, *flat.shape)))
    gradient, own, unused = chunk_norm_back(got, residual_a, norm_gains[0, 0], middle_grad)
    small_got, own = together(small_got, own)
    got = exchange(own)
    at, found = 0, []
    for v in small:
        count = v.size // 128
        found.append(small_got[:, at : at + count].reshape(n, *v.shape))
        at += count
    gains = jnp.sum(found[0], axis=0)
    own_taps = found[1][..., : sizes.inner].transpose(1, 2, 0, 3)
    own_taps = own_taps.reshape(LAYERS, CONV, NH * P_SIZE)
    taps = jnp.concatenate([own_taps, jnp.sum(found[1][..., sizes.inner :], axis=0)], axis=2)
    heads = found[2][..., : sizes.heads].transpose(2, 1, 0, 3).reshape(3 * LAYERS, NH)
    heads = jnp.pad(heads, ((0, 8 - 3 * LAYERS), (0, 128 - NH)))
    flat = jnp.concatenate([v.reshape(-1, 128) for v in (gains, taps, heads)])
    flat, *moved = together(flat, *moved)
    others = [ring.swap(flat, mask) for mask in (2, 4, 6)]
    moved = mix_a.step_z_again(mix_a.add_mid(moved))
    got, *others = together(got, *others)
    input_grad = full(got).astype(F32)
    flat = paired_sum(flat, *others)
    others = [ring.swap(flat, mask) for mask in (1, 8, 9)]
    *moved, o1, o2, o3 = together(*moved, *others)
    moved = mix_a.step_y(mix_a.add_last(moved))
    flat = paired_sum(flat, o1, o2, o3)
    (last,) = moved
    last, flat = together(last, flat)
    mix_sum_a = mix_a.total([last])
    cut = sizes.proj + sizes.mixed
    ffn_sum_c, mix_sum_c, ffn_sum_a = ffn_c, joint[:, :cut], joint[:, cut:]
    shared = [mix_sum_a[:, kv0:st1], mix_sum_c[:, kv0:st1]]
    shared = jnp.stack([v.astype(BF16) for v in shared], axis=0)
    width = shared.shape[2]
    rows = rows_own // n
    pieces = shared.reshape(LAYERS, n, rows, width).transpose(1, 0, 2, 3)
    got = lax.all_to_all(pieces, "tensor", 0, 0)
    gains = flat[: gains.size // 128].reshape(LAYERS, 2, D)
    taps = flat[gains.size // 128 : -8].reshape(LAYERS, CONV, -1).transpose(0, 2, 1)
    heads = flat[-8:, :NH].reshape(8, NH)[: 3 * LAYERS].reshape(3, LAYERS, NH)
    small_out = (gains, taps, heads[0], heads[1], heads[2])

    keyval_got = got[..., : 2 * HD].astype(F32)
    per_pair = n // KV
    keyval_grad = jnp.stack(
        [jnp.sum(keyval_got[k * per_pair : (k + 1) * per_pair], axis=0) for k in range(KV)], axis=0
    )
    keyval_grad = keyval_grad.reshape(KV, LAYERS, rows, 2, HD).transpose(1, 2, 3, 0, 4)
    keyval_grad = keyval_grad.reshape(LAYERS, rows, 2, KV * HD)
    bc_grad = jnp.sum(got[..., bc0 - kv0 : bc1 - kv0].astype(F32), axis=0)
    step_grad = got[..., st0 - kv0 :].astype(F32).transpose(1, 2, 0, 3).reshape(LAYERS, rows, NH)

    def stacked(first_layer, second_layer, at, dims):
        pair = [v[:, at : at + math.prod(dims)] for v in (first_layer, second_layer)]
        return jnp.stack([v.astype(F32).reshape(rows_own, *dims) for v in pair], axis=0)

    zx_grad = stacked(mix_sum_a, mix_sum_c, 0, (2, sizes.inner))
    query_grad = stacked(mix_sum_a, mix_sum_c, q0, (sizes.query_width,))
    mamba_out_grad = stacked(mix_sum_a, mix_sum_c, sizes.proj, (sizes.inner,))
    at = sizes.proj + sizes.inner
    attn_out_grad = stacked(mix_sum_a, mix_sum_c, at, (sizes.query_width,))
    gate_up_grad = stacked(ffn_sum_a, ffn_sum_c, 0, (2, sizes.ff))
    down_grad = stacked(ffn_sum_a, ffn_sum_c, gate_up_width, (sizes.ff,))
    return (
        block_output,
        input_grad,
        *small_out,
        zx_grad,
        bc_grad,
        step_grad,
        query_grad,
        keyval_grad,
        mamba_out_grad,
        attn_out_grad,
        gate_up_grad,
        down_grad,
    )


def solution(mesh):
    placed = (
        P("dp", None),
        P("dp", None),
        P(),
        P(),
        P(),
        P(),
        P(),
        P(None, "dp", None, "tensor"),
        P(None, "dp", None),
        P(None, "dp", None),
        P(None, "dp", "tensor"),
        P(None, "dp", None, None),
        P(None, "dp", "tensor"),
        P(None, "dp", "tensor"),
        P(None, "dp", None, "tensor"),
        P(None, "dp", "tensor"),
        P("dp", None),
    )
    return jax.shard_map(
        body,
        mesh=mesh,
        in_specs=placed,
        out_specs=(
            P("dp", None),
            P("dp", None),
            P(),
            P(),
            P(),
            P(),
            P(),
            P(None, "dp", None, "tensor"),
            P(None, ("dp", "tensor"), None),
            P(None, ("dp", "tensor"), None),
            P(None, "dp", "tensor"),
            P(None, ("dp", "tensor"), None, None),
            P(None, "dp", "tensor"),
            P(None, "dp", "tensor"),
            P(None, "dp", None, "tensor"),
            P(None, "dp", "tensor"),
        ),
        check_vma=False,
    )
```

```python
import functools
import math

import jax
import jax.numpy as jnp
from jax import lax
from jax.experimental import pallas as pl
from jax.experimental.pallas import tpu as pltpu
from jax.sharding import PartitionSpec as P

D = 2048
NH = 48
P_SIZE = 64
N = 256
CONV = 4
HQ = 8
KV = 2
HD = 128
LAYERS = 2

EPSILON = 1e-05
ROPE_BASE = 10000.0
PRECISE = lax.Precision.HIGHEST
NO_BATCH = ((), ())
F32 = jnp.float32
BF16 = jnp.bfloat16


def times(left_side, right_side):
    return jnp.dot(left_side, right_side, preferred_element_type=F32)


def times_transposed(left_side, right_side):
    return lax.dot_general(
        left_side, right_side, (((1,), (1,)), NO_BATCH), preferred_element_type=F32
    )


def norm_back(grad_unit, unit_vec, factor):
    return factor * (grad_unit - unit_vec * jnp.mean(grad_unit * unit_vec, axis=1, keepdims=True))


def unit_of(residual):
    factor = lax.rsqrt(jnp.mean(residual * residual, axis=1, keepdims=True) + EPSILON)
    return residual * factor, factor


class Sizes:
    def __init__(self):
        self.n_tensor = lax.axis_size("tensor")
        self.tensor = lax.axis_index("tensor")
        self.heads = NH // self.n_tensor
        self.inner = self.heads * P_SIZE
        self.query_heads = HQ // self.n_tensor
        self.query_width = self.query_heads * HD
        self.head_start = self.tensor * self.heads
        self.keyval = self.tensor * self.query_heads // (HQ // KV)
        self.ff = 4096 // self.n_tensor
        widths = (2 * self.inner, self.query_width, 2 * HD, 2 * N, self.heads)
        ends = [0]
        for w in widths:
            ends.append(ends[-1] + w)
        self.cuts = list(zip(ends[:-1], ends[1:]))
        self.proj = -(-ends[-1] // 128) * 128
        self.mixed = self.inner + self.query_width
        self.left = ends[1]
        self.rest = self.proj - self.left


class Ring:
    def __init__(self):
        place = lax.axis_index("dp")
        self.core, self.z, self.y = place % 2, (place // 2) % 4, place // 8
        near = ((0, 0), (0, 3), (0, 1), (0, 2), (1, 0), (1, 1), (1, 3), (1, 2))
        own = [self.block(dy, dz, self.core) for dy, dz in near]
        other = [self.block(dy, dz, 1 - self.core) for dy, dz in near]
        self.own_first = jnp.stack(own + other).astype(jnp.int32)
        self.other_first = jnp.stack(other + own).astype(jnp.int32)

    def block(self, dy, dz, core):
        return ((self.y ^ dy) * 4 + (self.z ^ dz)) * 2 + core

    def swap(self, value, mask):
        n = lax.axis_size("dp")
        return lax.ppermute(value, "dp", [(i, i ^ mask) for i in range(n)])


def place_blocks(order, parts, count):
    block = parts[0].shape[1:]

    def kernel(order_ref, *refs):
        ins, (out, held, came, left) = refs[: len(parts)], refs[len(parts) :]
        sources = [part.at[k] for part in ins for k in range(part.shape[0])]
        reads = [pltpu.make_async_copy(v, held.at[i], came.at[i]) for i, v in enumerate(sources)]
        writes = [
            pltpu.make_async_copy(held.at[i], out.at[order_ref[i]], left.at[i])
            for i in range(count)
        ]
        for c in reads:
            c.start()
        for r, w in zip(reads, writes):
            r.wait()
            w.start()
        for c in writes:
            c.wait()

    return pl.pallas_call(
        kernel,
        out_shape=jax.ShapeDtypeStruct((count, *block), parts[0].dtype),
        in_specs=[pl.BlockSpec(memory_space=pltpu.SMEM)]
        + [pl.BlockSpec(memory_space=pl.ANY)] * len(parts),
        out_specs=pl.BlockSpec(memory_space=pl.ANY),
        scratch_shapes=[
            pltpu.VMEM((count, *block), parts[0].dtype),
            pltpu.SemaphoreType.DMA((count,)),
            pltpu.SemaphoreType.DMA((count,)),
        ],
        compiler_params=pltpu.CompilerParams(vmem_limit_bytes=48 * 2**20),
        cost_estimate=TINY,
        name="place_blocks",
    )(order, *parts)


def together(*values):
    return lax.optimization_barrier(values)


def after(value, pairs):
    flat = [v for pair in pairs for v in pair]
    value, *flat = together(value, *flat)
    return value, tuple(zip(flat[::2], flat[1::2]))


def paired_sum(a, b, c, d):
    return (a + b) + (c + d)


class RowGather:
    def __init__(self, own, ring):
        self.ring, self.first = ring, own[None]

    def step_y(self):
        return self.ring.swap(self.first, 8), self.ring.swap(self.first, 6)

    def step_z(self, arrived):
        self.second, near = arrived
        self.first = jnp.concatenate([self.first, near], axis=0)
        return (self.ring.swap(self.second, 2),)

    def step_far(self, arrived):
        self.second = jnp.concatenate([self.second, arrived[0]], axis=0)
        return (
            self.ring.swap(self.first, 2),
            self.ring.swap(self.second, 6),
            self.ring.swap(self.first, 1),
            self.ring.swap(self.second, 1),
        )

    def step_core(self, arrived):
        self.first_far, self.second_far, self.first_other, self.second_other = arrived
        return self.ring.swap(self.first_far, 1), self.ring.swap(self.second_far, 1)

    def blocks(self, arrived):
        return [
            self.first,
            self.first_far,
            self.second,
            self.second_far,
            self.first_other,
            arrived[0],
            self.second_other,
            arrived[1],
        ]

    def rows(self, blocks):
        placed = place_blocks(self.ring.own_first, blocks, 16)
        return placed.reshape(-1, placed.shape[2])


def add_blocks(outs, dtype):
    terms = [t for out in outs for block in out for t in block]
    rows, cols = terms[0][0].shape[1:]

    def kernel(*refs):
        at = 0
        for ref, out in zip(refs[len(terms) :], outs):
            for k, block in enumerate(out):
                total = refs[at][0].astype(F32)
                for term in refs[at + 1 : at + len(block)]:
                    total = total + term[0].astype(F32)
                ref[k] = total.astype(dtype)
                at += len(block)

    def spec(index):
        return pl.BlockSpec((1, rows, cols), lambda i: (index, 0, 0))

    return pl.pallas_call(
        kernel,
        grid=(1,),
        in_specs=[spec(index) for _, index in terms],
        out_specs=[pl.BlockSpec((len(out), rows, cols), lambda i: (0, 0, 0)) for out in outs],
        out_shape=[jax.ShapeDtypeStruct((len(out), rows, cols), dtype) for out in outs],
        compiler_params=pltpu.CompilerParams(vmem_limit_bytes=48 * 2**20),
        cost_estimate=TINY,
        name="add_blocks",
    )(*(array for array, _ in terms))


class RowScatter:
    def __init__(self, halves, ring):
        self.ring, (self.other, self.own) = ring, halves

    def both(self, index):
        return [(self.own, index), (self.got, index)]

    def step_core(self):
        return (self.ring.swap(self.other, 1),)

    def add_far(self, arrived):
        (self.got,) = arrived
        return add_blocks([[self.both(2), self.both(3)], [self.both(6), self.both(7)]], BF16)

    def step_z(self, far):
        return self.ring.swap(far[0], 2), self.ring.swap(far[1], 6)

    def add_mid(self, arrived):
        self.far, self.far_two = arrived
        return add_blocks(
            [[self.both(1) + [(self.far, 1)]], [self.both(5) + [(self.far_two, 1)]]], BF16
        )

    def step_z_again(self, mid):
        return self.ring.swap(mid[0], 6), self.ring.swap(mid[1], 2)

    def add_last(self, arrived):
        self.mid, mid_two = arrived
        return add_blocks([[self.both(4) + [(self.far_two, 0), (mid_two, 0)]]], BF16)

    def step_y(self, last):
        return (self.ring.swap(last[0], 8),)

    def terms(self, last):
        return self.own, self.got, self.far, self.mid, last


TINY = pl.CostEstimate(flops=1, bytes_accessed=1, transcendentals=0)


def rows_matmul(x, order, parts, width, weight):
    tokens, block, n = x.shape[0], parts[0].shape[1], len(parts)

    def kernel(order_ref, x_ref, w_ref, *refs):
        refs[n][...] = mm(x_ref[...], w_ref[...], NN)
        total = None
        for k, part in enumerate(refs[:n]):
            lanes = [
                pl.ds(pl.multiple_of(order_ref[2 * k + h] * block, block), block) for h in (0, 1)
            ]
            rows = jnp.concatenate([x_ref[:, v] for v in lanes], axis=1)
            term = mm(rows, part[:, :, :width].reshape(2 * block, width), NN)
            total = term if total is None else total + term
        refs[n + 1][...] = total

    return pl.pallas_call(
        kernel,
        in_specs=[pl.BlockSpec(memory_space=pltpu.SMEM)]
        + [pl.BlockSpec(memory_space=pltpu.VMEM)] * (2 + n),
        out_specs=[pl.BlockSpec(memory_space=pltpu.VMEM)] * 2,
        out_shape=[
            jax.ShapeDtypeStruct((tokens, weight.shape[1]), F32),
            jax.ShapeDtypeStruct((tokens, width), F32),
        ],
        compiler_params=pltpu.CompilerParams(vmem_limit_bytes=56 * 2**20),
        cost_estimate=TINY,
        name="rows_matmul",
    )(order, x, weight, *parts)


def rows_out(mixed, order, parts, start):
    tokens, block, n = mixed.shape[0], parts[0].shape[1], len(parts)

    def kernel(order_ref, x_ref, *refs):
        out = refs[n]
        for k, part in enumerate(refs[:n]):
            rows = part[:, :, start:].reshape(2 * block, x_ref.shape[1])
            term = dot_nt(x_ref[...], rows).astype(BF16)
            for h in (0, 1):
                lanes = pl.ds(pl.multiple_of(order_ref[2 * k + h] * block, block), block)
                out[:, lanes] = term[:, h * block : (h + 1) * block]

    return pl.pallas_call(
        kernel,
        in_specs=[pl.BlockSpec(memory_space=pltpu.SMEM)]
        + [pl.BlockSpec(memory_space=pltpu.VMEM)] * (1 + n),
        out_specs=pl.BlockSpec(memory_space=pltpu.VMEM),
        out_shape=jax.ShapeDtypeStruct((tokens, D), BF16),
        compiler_params=pltpu.CompilerParams(vmem_limit_bytes=56 * 2**20),
        cost_estimate=TINY,
        name="rows_out",
    )(order, mixed, *parts)


def weight_grads(pairs, order, split):
    count, step_blocks = 16, 4
    steps = count // step_blocks
    tokens = pairs[0][0].shape[0]
    rows = pairs[0][0].shape[1] // count
    widths = [y.shape[1] for _, y in pairs]
    total = sum(widths)
    n_x = len(pairs) * step_blocks

    def fill(out_ref, xs, ys):
        at = 0
        for k, (y, w) in enumerate(zip(ys, widths)):
            x = jnp.concatenate([v[...] for v in xs[k * step_blocks : (k + 1) * step_blocks]], axis=1)
            grad = lax.dot_general(x, y[...], (((0,), (0,)), NO_BATCH), preferred_element_type=F32)
            out_ref[:, :, at : at + w] = grad.astype(BF16).reshape(step_blocks, rows, w)
            at += w

    def kernel(order_ref, *refs):
        xs, ys, outs = refs[:n_x], refs[n_x : n_x + len(pairs)], refs[n_x + len(pairs) :]
        if not split:
            fill(outs[0], xs, ys)
            return
        step = pl.program_id(0)

        @pl.when(step < steps // 2)
        def _():
            fill(outs[0], xs, ys)

        @pl.when(step >= steps // 2)
        def _():
            fill(outs[1], xs, ys)

    half = steps // 2
    block = (step_blocks, rows, total)
    if split:
        out_shape = [jax.ShapeDtypeStruct((count // 2, rows, total), BF16)] * 2
        out_specs = [
            pl.BlockSpec(block, lambda i, o: (jnp.minimum(i, half - 1), 0, 0)),
            pl.BlockSpec(block, lambda i, o: (jnp.maximum(i - half, 0), 0, 0)),
        ]
    else:
        out_shape = [jax.ShapeDtypeStruct((count, rows, total), BF16)]
        out_specs = [pl.BlockSpec(block, lambda i, o: (i, 0, 0))]

    def x_spec(k):
        return pl.BlockSpec((tokens, rows), lambda i, o: (0, o[i * step_blocks + k]))

    return pl.pallas_call(
        kernel,
        grid_spec=pltpu.PrefetchScalarGridSpec(
            num_scalar_prefetch=1,
            grid=(steps,),
            in_specs=[x_spec(k) for _ in pairs for k in range(step_blocks)]
            + [pl.BlockSpec((tokens, w), lambda i, o: (0, 0)) for w in widths],
            out_specs=out_specs,
        ),
        out_shape=out_shape,
        compiler_params=pltpu.CompilerParams(vmem_limit_bytes=48 * 2**20),
        cost_estimate=TINY,
        name="weight_grads",
    )(order, *(x for x, _ in pairs for _ in range(step_blocks)), *(y for _, y in pairs))


def dot_nn(a, b):
    return lax.dot_general(
        a.astype(BF16), b.astype(BF16), (((1,), (0,)), NO_BATCH), preferred_element_type=F32
    )


def dot_nt(a, b):
    return lax.dot_general(
        a.astype(BF16), b.astype(BF16), (((1,), (1,)), NO_BATCH), preferred_element_type=F32
    )


def dot_tn(a, b):
    return lax.dot_general(
        a.astype(BF16), b.astype(BF16), (((0,), (0,)), NO_BATCH), preferred_element_type=F32
    )


def logistic(v):
    return 1.0 / (1.0 + jnp.exp(-v))


def softplus(v):
    return jnp.maximum(v, 0.0) + jnp.log1p(jnp.exp(-jnp.abs(v)))


class Mixer:
    def __init__(self, cuts, inner, proj_ref, rest_ref, taps_ref, heads_ref, column_ref, row_ref):
        length, left = proj_ref.shape
        self.inner, self.pairs, self.length = inner, inner // 128, length
        (self.zx0, self.zx1), (q0, q1), (kv0, _), (bc0, bc1), (st0, _) = cuts
        offset = column_ref[:, 0:1]
        self.keep = [(offset >= float(j)).astype(F32) for j in range(CONV)]
        across = lax.broadcasted_iota(jnp.int32, (length, length), 1)
        down = lax.broadcasted_iota(jnp.int32, (length, length), 0)
        self.allowed = (column_ref[:, 1:2] == row_ref[0:1, :]) & (across <= down)
        self.lower = (across <= down).astype(F32)
        self.upper = (across >= down).astype(F32)
        self.first_half = lax.broadcasted_iota(jnp.int32, (1, 128), 1) < P_SIZE
        q0, q1, kv0 = q0 - left, q1 - left, kv0 - left
        self.query, self.key = rest_ref[:, q0:q1], rest_ref[:, kv0 : kv0 + HD]
        self.value = rest_ref[:, kv0 + HD : kv0 + 2 * HD]
        self.signal = jnp.concatenate(
            [proj_ref[:, inner : 2 * inner], rest_ref[:, bc0 - left : bc1 - left]], axis=1
        )
        pre = self.signal * self.keep[0] * taps_ref[CONV - 1 : CONV, :]
        for j in range(1, CONV):
            tap = taps_ref[CONV - 1 - j : CONV - j, :]
            pre = pre + pltpu.roll(self.signal, j, 0) * self.keep[j] * tap
        self.pre = pre
        self.pre_gate = logistic(pre)
        self.act = pre * self.pre_gate
        self.b_state = self.act[:, inner : inner + N].astype(BF16)
        self.c_state = self.act[:, inner + N :].astype(BF16)
        self.heads = heads_ref
        self.step_pre = rest_ref[:, st0 - left : st0 - left + 128] + heads_ref[0:1, :]
        self.step = softplus(self.step_pre)
        self.rate = heads_ref[1:2, :]
        self.total = jnp.dot(self.lower, -self.step * self.rate, precision=PRECISE)
        self.total_t = self.total.T
        self.cb = dot_nt(self.c_state, self.b_state)
        self.proj_ref = proj_ref

    def by_half(self, first, second):
        return jnp.where(self.first_half, first, second)

    def decay(self, head):
        gap = self.total[:, head : head + 1] - self.total_t[head : head + 1, :]
        return jnp.where(self.allowed, jnp.exp(jnp.where(self.allowed, gap, 0.0)), 0.0)

    def pair(self, p):
        lanes = slice(128 * p, 128 * p + 128)
        a, b = 2 * p, 2 * p + 1
        inputs = self.act[:, lanes]
        step = self.by_half(self.step[:, a : a + 1], self.step[:, b : b + 1])
        skip = self.by_half(self.heads[2:3, a : a + 1], self.heads[2:3, b : b + 1])
        gate = self.proj_ref[:, lanes]
        return inputs, step, skip, gate, inputs * step

    def prob(self, query_rot, key_rot):
        scores = dot_nt(query_rot, key_rot) * (1.0 / math.sqrt(HD))
        scores = jnp.where(self.allowed, scores, -1e30)
        weight = jnp.exp(scores - jnp.max(scores, axis=1, keepdims=True))
        return weight / jnp.sum(weight, axis=1, keepdims=True)


def turn(v, cosine, sine, direction):
    return v * cosine + (direction * sine) * pltpu.roll(v, HD // 2, 1)


def mixer_forward_kernel(cuts, inner, proj, rest, taps, heads, column, row, cosine, sine, out):
    m = Mixer(cuts, inner, proj, rest, taps, heads, column, row)
    for p in range(m.pairs):
        inputs, step, skip, gate, scaled = m.pair(p)
        scaled = scaled.astype(BF16)
        mixed = [dot_nn(m.cb * m.decay(2 * p + k), scaled) for k in range(2)]
        ssm = m.by_half(*mixed) + skip * inputs
        out[:, 128 * p : 128 * p + 128] = (ssm * gate * logistic(gate)).astype(BF16)
    query_rot = turn(m.query, cosine[...], sine[...], 1.0)
    key_rot = turn(m.key, cosine[...], sine[...], 1.0)
    out[:, inner:] = dot_nn(m.prob(query_rot, key_rot), m.value).astype(BF16)


def mixer_backward_kernel(
    cuts, inner, proj, rest, taps, heads, column, row, cosine, sine, grad, out, out_rest, taps_grad, heads_grad
):
    m = Mixer(cuts, inner, proj, rest, taps, heads, column, row)
    lane = lax.broadcasted_iota(jnp.int32, (1, 128), 1)
    cos, sin = cosine[...], sine[...]
    (q0, q1), (kv0, _), (bc0, bc1), (st0, _) = cuts[1:]
    left = proj.shape[1]
    q0, q1, kv0 = q0 - left, q1 - left, kv0 - left

    query_rot, key_rot = turn(m.query, cos, sin, 1.0), turn(m.key, cos, sin, 1.0)
    prob = m.prob(query_rot, key_rot)
    attended_grad = grad[:, inner:]
    out_rest[:, kv0 + HD : kv0 + 2 * HD] = dot_tn(prob, attended_grad).astype(BF16)
    prob_grad = dot_nt(attended_grad, m.value)
    inner_sum = jnp.sum(prob * prob_grad, axis=1, keepdims=True)
    score_grad = prob * (prob_grad - inner_sum) * (1.0 / math.sqrt(HD))
    out_rest[:, q0:q1] = turn(dot_nn(score_grad, key_rot), cos, sin, -1.0).astype(BF16)
    out_rest[:, kv0 : kv0 + HD] = turn(dot_tn(score_grad, query_rot), cos, sin, -1.0).astype(BF16)

    cb_grad = jnp.zeros((m.length, m.length), F32)
    down_sums = jnp.zeros((m.length, 128), F32)
    across_sums = []
    step_grad = jnp.zeros((m.length, 128), F32)
    skip_grad = jnp.zeros((1, 128), F32)
    inputs_grads = []
    for p in range(m.pairs):
        inputs, step, skip, gate, scaled = m.pair(p)
        gated_grad = grad[:, 128 * p : 128 * p + 128]
        sig = logistic(gate)
        ssm_grad = gated_grad * gate * sig
        scaled_b, ssm_grad_b = scaled.astype(BF16), ssm_grad.astype(BF16)
        ssm, scaled_grad = [], []
        for k in range(2):
            h = 2 * p + k
            decay = m.decay(h)
            mixing = m.cb * decay
            mixing_b = mixing.astype(BF16)
            ssm.append(dot_nn(mixing_b, scaled_b))
            scaled_grad.append(dot_tn(mixing_b, ssm_grad_b))
            mine = m.first_half if k == 0 else jnp.logical_not(m.first_half)
            mixing_grad = dot_nt(jnp.where(mine, ssm_grad, 0.0), scaled_b)
            cb_grad = cb_grad + mixing_grad * decay
            gap_grad = mixing_grad * mixing
            down_sums = jnp.where(lane == h, jnp.sum(gap_grad, axis=1, keepdims=True), down_sums)
            across_sums.append(jnp.sum(gap_grad, axis=0, keepdims=True))
        ssm = m.by_half(*ssm) + skip * inputs
        scaled_grad = m.by_half(*scaled_grad)
        slope = sig * (1.0 + gate * (1.0 - sig))
        out[:, 128 * p : 128 * p + 128] = (gated_grad * ssm * slope).astype(BF16)
        inputs_grads.append(scaled_grad * step + ssm_grad * skip)
        by_step, by_skip = scaled_grad * inputs, ssm_grad * inputs
        for k in range(2):
            mine = m.first_half if k == 0 else jnp.logical_not(m.first_half)
            here = lane == 2 * p + k
            step_grad = jnp.where(
                here, jnp.sum(jnp.where(mine, by_step, 0.0), axis=1, keepdims=True), step_grad
            )
            own_skip = jnp.sum(jnp.where(mine, by_skip, 0.0), axis=0, keepdims=True)
            skip_grad = jnp.where(here, jnp.sum(own_skip, axis=1, keepdims=True), skip_grad)

    across = jnp.concatenate(
        across_sums + [jnp.zeros((128 - len(across_sums), m.length), F32)], axis=0
    )
    term_grad = jnp.dot(m.upper, down_sums - across.T, precision=PRECISE)
    step_grad = step_grad - term_grad * m.rate
    step_pre_grad = step_grad * logistic(m.step_pre)
    out_rest[:, st0 - left : st0 - left + 128] = step_pre_grad.astype(BF16)
    heads_grad[0:1, :] = jnp.sum(step_pre_grad, axis=0, keepdims=True)
    heads_grad[1:2, :] = -jnp.sum(term_grad * m.step, axis=0, keepdims=True) * m.rate
    heads_grad[2:3, :] = skip_grad
    heads_grad[3:8, :] = jnp.zeros((5, 128), F32)

    c_grad = dot_nn(cb_grad, m.b_state)
    b_grad = dot_tn(cb_grad, m.c_state)
    act_grad = jnp.concatenate(inputs_grads + [b_grad, c_grad], axis=1)
    pre_grad = act_grad * (m.pre_gate * (1.0 + m.pre * (1.0 - m.pre_gate)))
    signal_grad = jnp.zeros_like(pre_grad)
    for j in range(CONV):
        masked = pre_grad * m.keep[j]
        back = masked if j == 0 else pltpu.roll(masked, m.length - j, 0)
        shifted = m.signal if j == 0 else pltpu.roll(m.signal, j, 0)
        k = CONV - 1 - j
        signal_grad = signal_grad + back * taps[k : k + 1, :]
        taps_grad[k : k + 1, :] = jnp.sum(masked * shifted, axis=0, keepdims=True)
    taps_grad[CONV:8, :] = jnp.zeros((8 - CONV, pre_grad.shape[1]), F32)
    out[:, inner : 2 * inner] = signal_grad[:, :inner].astype(BF16)
    out_rest[:, bc0 - left : bc1 - left] = signal_grad[:, inner:].astype(BF16)


def mm(a, b, dims):
    return lax.dot_general(a, b, (dims, NO_BATCH), preferred_element_type=F32)


NN, NT = ((1,), (0,)), ((1,), (1,))


def proj_forward(x, weight, sizes):
    tokens, depth = x.shape
    tile = 256
    first, steps = sizes.left // tile, sizes.proj // tile

    def kernel(x_ref, w_ref, left, rest):
        value = mm(x_ref[...], w_ref[...], NN)
        step = pl.program_id(0)

        @pl.when(step < first)
        def _():
            left[...] = value

        @pl.when(step >= first)
        def _():
            rest[...] = value

    return pl.pallas_call(
        kernel,
        grid=(steps,),
        in_specs=[
            pl.BlockSpec((tokens, depth), lambda i: (0, 0)),
            pl.BlockSpec((depth, tile), lambda i: (0, i)),
        ],
        out_specs=[
            pl.BlockSpec((tokens, tile), lambda i: (0, jnp.minimum(i, first - 1))),
            pl.BlockSpec((tokens, tile), lambda i: (0, jnp.maximum(i - first, 0))),
        ],
        out_shape=[
            jax.ShapeDtypeStruct((tokens, sizes.left), F32),
            jax.ShapeDtypeStruct((tokens, sizes.rest), F32),
        ],
        compiler_params=pltpu.CompilerParams(vmem_limit_bytes=48 * 2**20),
        cost_estimate=TINY,
        name="proj_forward",
    )(x, weight)


def proj_backward(grads, w_zx, w_rest):
    rest = w_rest[:, : grads[1].shape[1]]
    return times_transposed(grads[0], w_zx) + times_transposed(grads[1], rest)


def feed_forward_call(kernel, name, x, tiled, weight, ff, tiled_outs, tile=256):
    tokens, depth = x[0].shape
    steps = ff // tile

    def whole_kernel(*refs):
        *rest, out, total = refs
        step = pl.program_id(0)
        term = kernel(*rest)

        @pl.when(step == 0)
        def _():
            total[...] = term

        @pl.when(step > 0)
        def _():
            total[...] += term

        @pl.when(step == steps - 1)
        def _():
            out[...] = total[...].astype(BF16)

    def column(part):
        return pl.BlockSpec((depth, tile), lambda i: (0, part * steps + i))

    def tile_spec(_):
        return pl.BlockSpec((tokens, tile), lambda i: (0, i))

    return pl.pallas_call(
        whole_kernel,
        grid=(steps,),
        in_specs=[pl.BlockSpec((tokens, depth), lambda i: (0, 0)) for _ in x]
        + [tile_spec(v) for v in tiled]
        + [column(k) for k in range(3)],
        out_specs=[tile_spec(v) for v in tiled_outs]
        + [pl.BlockSpec((tokens, depth), lambda i: (0, 0))],
        out_shape=[jax.ShapeDtypeStruct((tokens, ff), v) for v in tiled_outs]
        + [jax.ShapeDtypeStruct((tokens, depth), BF16)],
        scratch_shapes=[pltpu.VMEM((tokens, depth), F32)],
        compiler_params=pltpu.CompilerParams(vmem_limit_bytes=56 * 2**20),
        cost_estimate=TINY,
        name=name,
    )(*x, *tiled, weight, weight, weight)


def gate_grads(hidden_grad, gate, up):
    sig = logistic(gate)
    gate_grad = hidden_grad * up * (sig * (1.0 + gate * (1.0 - sig)))
    return gate_grad.astype(BF16), (hidden_grad * gate * sig).astype(BF16)


def feed_forward(x, weight, ff):
    def kernel(x_ref, w_gate, w_up, w_down, gate_ref, up_ref, hidden_ref):
        gate, up = mm(x_ref[...], w_gate[...], NN), mm(x_ref[...], w_up[...], NN)
        hidden = (gate * logistic(gate) * up).astype(BF16)
        gate_ref[...], up_ref[...], hidden_ref[...] = gate, up, hidden
        return mm(hidden, w_down[...], NT)

    return feed_forward_call(kernel, "feed_forward", (x,), (), weight, ff, (F32, F32, BF16))


def feed_forward_both(x, grad, weight, ff):
    def kernel(x_ref, grad_ref, w_gate, w_up, w_down, hidden_ref, gate_out, up_out):
        gate, up = mm(x_ref[...], w_gate[...], NN), mm(x_ref[...], w_up[...], NN)
        hidden_ref[...] = (gate * logistic(gate) * up).astype(BF16)
        grads = gate_grads(mm(grad_ref[...], w_down[...], NN), gate, up)
        gate_out[...], up_out[...] = grads
        return mm(grads[0], w_gate[...], NT) + mm(grads[1], w_up[...], NT)

    return feed_forward_call(
        kernel, "feed_forward_both", (x, grad), (), weight, ff, (BF16, BF16, BF16)
    )


def feed_forward_back(grad, gate, up, weight, ff):
    def kernel(grad_ref, gate_ref, up_ref, w_gate, w_up, w_down, gate_out, up_out):
        grads = gate_grads(mm(grad_ref[...], w_down[...], NN), gate_ref[...], up_ref[...])
        gate_out[...], up_out[...] = grads
        return mm(grads[0], w_gate[...], NT) + mm(grads[1], w_up[...], NT)

    return feed_forward_call(
        kernel, "feed_forward_back", (grad,), (gate, up), weight, ff, (BF16, BF16)
    )


def whole(shapes):
    return [pl.BlockSpec(memory_space=pltpu.VMEM) for _ in shapes]


def mixer_forward(proj, smalls, geometry, sizes):
    length = proj[0].shape[0]
    ins = (*proj, *smalls, *geometry)
    return pl.pallas_call(
        functools.partial(mixer_forward_kernel, sizes.cuts, sizes.inner),
        in_specs=whole([v.shape for v in ins]),
        out_specs=whole([(length, sizes.mixed)])[0],
        out_shape=jax.ShapeDtypeStruct((length, sizes.mixed), BF16),
        compiler_params=pltpu.CompilerParams(vmem_limit_bytes=48 * 2**20),
        cost_estimate=TINY,
        name="mixer_forward",
    )(*ins)


def mixer_backward(mixed_grad, proj, smalls, geometry, sizes):
    ins = (*proj, *smalls, *geometry, mixed_grad)
    outs = [jax.ShapeDtypeStruct(v.shape, BF16) for v in proj]
    outs += [jax.ShapeDtypeStruct(v.shape, F32) for v in smalls]
    return pl.pallas_call(
        functools.partial(mixer_backward_kernel, sizes.cuts, sizes.inner),
        in_specs=whole([v.shape for v in ins]),
        out_specs=whole([v.shape for v in outs]),
        out_shape=outs,
        compiler_params=pltpu.CompilerParams(vmem_limit_bytes=48 * 2**20),
        cost_estimate=TINY,
        name="mixer_backward",
    )(*ins)


def chunk_norm(got, residual, gain):
    n, rows, width = got.shape

    def kernel(got_ref, residual_ref, gain_ref, out, copies):
        total = residual_ref[...]
        for k in range(n):
            total = total + got_ref[k].astype(F32)
        out[...] = total
        normed = (unit_of(total)[0] * gain_ref[...]).astype(BF16)
        for k in range(n):
            copies[k] = normed

    ins = (got, residual, gain[None])
    outs = [jax.ShapeDtypeStruct((rows, width), F32), jax.ShapeDtypeStruct(got.shape, BF16)]
    return pl.pallas_call(
        kernel,
        in_specs=whole([v.shape for v in ins]),
        out_specs=whole([v.shape for v in outs]),
        out_shape=outs,
        cost_estimate=TINY,
        name="chunk_norm",
    )(*ins)


def chunk_norm_back(got, residual, gain, gradient, extra=None):
    n, rows, width = got.shape
    sent = rows if extra is None else rows + extra.shape[0]

    def kernel(got_ref, residual_ref, gain_ref, gradient_ref, *refs):
        out, copies, gain_grad = refs[-3:]
        normed_grad = got_ref[0].astype(F32)
        for k in range(1, n):
            normed_grad = normed_grad + got_ref[k].astype(F32)
        unit, factor = unit_of(residual_ref[...])
        gain_grad[...] = jnp.sum(normed_grad * unit, axis=0, keepdims=True)
        total = gradient_ref[...] + norm_back(normed_grad * gain_ref[...], unit, factor)
        out[...] = total
        total = total.astype(BF16)
        for k in range(n):
            copies[k, :rows] = total
            if extra is not None:
                copies[k, rows:] = refs[0][...]

    ins = (got, residual, gain[None], gradient) + (() if extra is None else (extra,))
    outs = [
        jax.ShapeDtypeStruct((rows, width), F32),
        jax.ShapeDtypeStruct((n, sent, width), BF16),
        jax.ShapeDtypeStruct((1, width), F32),
    ]
    return pl.pallas_call(
        kernel,
        in_specs=whole([v.shape for v in ins]),
        out_specs=whole([v.shape for v in outs]),
        out_shape=outs,
        cost_estimate=TINY,
        name="chunk_norm_back",
    )(*ins)


SMALL_ROWS, SMALL_WIDTH = 32, 1024


def pack_smalls(gains, taps, heads, n):
    gain_rows = len(gains) * D // SMALL_WIDTH
    tap_rows = len(taps) * CONV

    def kernel(*refs):
        *ins, out, held = refs
        held[...] = jnp.zeros(held.shape, F32)
        for g, ref in enumerate(ins[: len(gains)]):
            for h in range(D // SMALL_WIDTH):
                row = g * (D // SMALL_WIDTH) + h
                held[row : row + 1, :] = ref[:, h * SMALL_WIDTH : (h + 1) * SMALL_WIDTH]
        for l, ref in enumerate(ins[len(gains) : len(gains) + len(taps)]):
            row = gain_rows + l * CONV
            held[row : row + CONV, : ref.shape[1]] = ref[:CONV, :]
        for l, ref in enumerate(ins[len(gains) + len(taps) :]):
            row = gain_rows + tap_rows + 3 * l
            held[row : row + 3, :128] = ref[:3, :]
        for k in range(n):
            out[k] = held[...].astype(BF16)

    ins = (*gains, *taps, *heads)
    return pl.pallas_call(
        kernel,
        in_specs=whole([v.shape for v in ins]),
        out_specs=whole([0])[0],
        out_shape=jax.ShapeDtypeStruct((n, SMALL_ROWS, SMALL_WIDTH), BF16),
        scratch_shapes=[pltpu.VMEM((SMALL_ROWS, SMALL_WIDTH), F32)],
        cost_estimate=TINY,
        name="pack_smalls",
    )(*ins)


def join_smalls(got, sizes):
    n = got.shape[0]
    per_gain = D // SMALL_WIDTH
    gain_rows, inner = 4 * per_gain, sizes.inner
    width = NH * P_SIZE + 2 * N

    def kernel(got_ref, out):
        out[...] = jnp.zeros(out.shape, F32)
        taps = slice(gain_rows, gain_rows + 8)
        parts = [got_ref[k].astype(F32) for k in range(n)]
        for k, part in enumerate(parts):
            out[:8, k * inner : (k + 1) * inner] = part[taps, :inner]
        total = sum(parts[1:], parts[0])
        shared, gains = total[taps, inner : inner + 2 * N], total[:gain_rows]
        heads = parts[0][gain_rows + 8 : gain_rows + 16, :128]
        for k in range(1, n):
            part = parts[k][gain_rows + 8 : gain_rows + 16, :128]
            heads = heads + pltpu.roll(part, k * sizes.heads, 1)
        out[:8, n * inner :] = shared
        for g in range(4):
            for h in range(per_gain):
                lanes = slice(h * SMALL_WIDTH, (h + 1) * SMALL_WIDTH)
                row = g * per_gain + h
                out[8 + g : 9 + g, lanes] = gains[row : row + 1, :]
        for m in range(6):
            out[12:13, 128 * m : 128 * m + 128] = heads[m : m + 1, :]

    return pl.pallas_call(
        kernel,
        in_specs=whole([0]),
        out_specs=whole([0])[0],
        out_shape=jax.ShapeDtypeStruct((16, width), F32),
        cost_estimate=TINY,
        name="join_smalls",
    )(got)


def first_blocks(arrays):
    return [
        pl.BlockSpec((1, *v.shape[1:]), lambda i: (0, 0, 0)) if v.ndim == 3 else whole([0])[0]
        for v in arrays
    ]


def added(refs):
    total = refs[0][0].astype(F32)
    for ref in refs[1:]:
        total = total + ref[0].astype(F32)
    return total


def finish_mixers(layers, sizes, cuts):
    count, n = len(layers[0]), sizes.n_tensor
    rows = layers[0][0].shape[1]
    (q0, q1), out0, end = cuts, sizes.proj, sizes.proj + sizes.mixed
    edges = (0, q0, q1, out0, out0 + sizes.inner, end)

    def kernel(*refs):
        zx, query, mamba, attn, pieces = refs[2 * count :]
        for l in range(2):
            total = added(refs[l * count : (l + 1) * count])
            parts = [total[:, a:b] for a, b in zip(edges[:-1], edges[1:])]
            zx[l], query[l], mamba[l], attn[l] = parts[0], parts[1], parts[3], parts[4]
            shared = parts[2].astype(BF16)
            for k in range(n):
                pieces[k, l] = shared[k * (rows // n) : (k + 1) * (rows // n)]

    ins = (*layers[0], *layers[1])
    outs = [jax.ShapeDtypeStruct((2, rows, w), F32) for w in (q0, q1 - q0, sizes.inner, end - edges[4])]
    outs.append(jax.ShapeDtypeStruct((n, 2, rows // n, out0 - q1), BF16))
    return pl.pallas_call(
        kernel,
        grid=(1,),
        in_specs=first_blocks(ins),
        out_specs=whole(outs),
        out_shape=outs,
        compiler_params=pltpu.CompilerParams(vmem_limit_bytes=48 * 2**20),
        cost_estimate=TINY,
        name="finish_mixers",
    )(*ins)


def finish_feed_forward(first, second, cut):
    rows, width = second.shape

    def kernel(first_ref, second_ref, gate_up, down):
        for l, ref in enumerate((first_ref, second_ref)):
            total = ref[...].astype(F32)
            gate_up[l], down[l] = total[:, :cut], total[:, cut:]

    ins = (first, second)
    outs = [jax.ShapeDtypeStruct((2, rows, w), F32) for w in (cut, width - cut)]
    return pl.pallas_call(
        kernel,
        in_specs=whole(ins),
        out_specs=whole(outs),
        out_shape=outs,
        cost_estimate=TINY,
        name="finish_feed_forward",
    )(*ins)


def finish_shared(got, sizes):
    n, layers, rows, _ = got.shape
    pair = n // KV

    def kernel(got_ref, keyval, bc, step):
        for l in range(layers):
            parts = [got_ref[k, l].astype(F32) for k in range(n)]
            for p in range(KV):
                mine = sum(parts[p * pair + 1 : (p + 1) * pair], parts[p * pair])
                for c in range(2):
                    at = (c * KV + p) * HD
                    keyval[l, :, at : at + HD] = mine[:, c * HD : (c + 1) * HD]
            bc[l] = sum([v[:, 2 * HD : 2 * HD + 2 * N] for v in parts[1:]], parts[0][:, 2 * HD : 2 * HD + 2 * N])
            steps = parts[0][:, 2 * HD + 2 * N :]
            for k in range(1, n):
                steps = steps + pltpu.roll(parts[k][:, 2 * HD + 2 * N :], k * sizes.heads, 1)
            step[l] = steps[:, :NH]

    outs = [jax.ShapeDtypeStruct((layers, rows, w), F32) for w in (2 * KV * HD, 2 * N, NH)]
    return pl.pallas_call(
        kernel,
        in_specs=whole([0]),
        out_specs=whole(outs),
        out_shape=outs,
        cost_estimate=TINY,
        name="finish_shared",
    )(got)


def own_smalls(smalls, sizes):
    kernel, step_bias, log_rate, skip_gain = smalls
    own = jnp.concatenate(
        [
            lax.dynamic_slice_in_dim(kernel, sizes.head_start * P_SIZE, sizes.inner, 0),
            kernel[NH * P_SIZE :],
        ],
        axis=0,
    )
    taps = jnp.pad(own.T, ((0, 8 - CONV), (0, 0)))
    heads = jnp.stack([step_bias, jnp.exp(log_rate), skip_gain])
    heads = lax.dynamic_slice_in_dim(heads, sizes.head_start, sizes.heads, 1)
    return taps, jnp.pad(heads, ((0, 5), (0, 128 - sizes.heads)))


def layout_of(lengths, row_count):
    seq_ends = jnp.cumsum(lengths)
    seq_starts = seq_ends - lengths
    position = jnp.arange(row_count, dtype=jnp.int32)
    past = position[:, None] >= seq_ends[None, :]
    segment = jnp.sum(past.astype(jnp.int32), axis=1)
    first_of = jnp.max(jnp.where(past, seq_ends[None, :], 0), axis=1)
    offset = position - first_of
    in_use = (position < seq_ends[-1]).astype(F32)
    offset, segment = offset.astype(F32), segment.astype(F32)
    column = jnp.pad(jnp.stack([offset, segment], axis=1), ((0, 0), (0, 126)))
    row = jnp.broadcast_to(segment[None], (8, row_count))
    half_width = HD // 2
    frequency = jnp.exp(
        jnp.arange(half_width, dtype=F32) * (-2.0 * math.log(ROPE_BASE) / HD)
    )
    angles = offset[:, None] * frequency[None, :]
    cosine, sine = jnp.cos(angles), jnp.sin(angles)
    tables = jnp.concatenate([cosine, cosine], axis=1), jnp.concatenate([-sine, sine], axis=1)
    return (column, row, *tables), in_use


def body(
    layer_input,
    seq_lengths,
    norm_gains,
    conv_kernel,
    step_bias,
    log_rate,
    skip_gain,
    zx_weight,
    bc_weight,
    step_weight,
    query_weight,
    keyval_weight,
    mamba_out_weight,
    attn_out_weight,
    gate_up_weight,
    down_weight,
    cotangent,
):
    sizes = Sizes()
    ring = Ring()
    length = layer_input.shape[0]
    chunk = length // sizes.n_tensor
    first = sizes.tensor * chunk
    rows_own = zx_weight.shape[1]
    gate_up_width = 2 * sizes.ff
    geometry, in_use = layout_of(seq_lengths[0], length)

    def zx_part(layer):
        return [zx_weight[layer].reshape(rows_own, -1)]

    def rest_part(layer):
        step_own = lax.dynamic_slice_in_dim(step_weight[layer], sizes.head_start, sizes.heads, 1)
        pair = lax.dynamic_slice_in_dim(keyval_weight[layer], sizes.keyval * HD, HD, 2)
        parts = [query_weight[layer], pair.reshape(rows_own, -1), bc_weight[layer], step_own]
        used = sum(p.shape[1] for p in parts)
        return parts + [jnp.zeros((rows_own, sizes.rest - used), BF16)]

    def out_part(layer):
        return [mamba_out_weight[layer], attn_out_weight[layer]]

    def ffn_part(layer):
        return [gate_up_weight[layer].reshape(rows_own, -1), down_weight[layer]]

    def joined(parts):
        return jnp.concatenate(parts, axis=1)

    def gathered(parts):
        return lax.all_gather(joined(parts), "dp", axis=0, tiled=True)

    smalls = [
        own_smalls((conv_kernel[l], step_bias[l], log_rate[l], skip_gain[l]), sizes)
        for l in range(LAYERS)
    ]

    def own_rows(v):
        return lax.dynamic_slice_in_dim(v, first, chunk, 0)

    def gained(unit, layer, which):
        return unit * norm_gains[layer, which][None, :]

    def to_chunks(partial):
        return partial.astype(BF16).reshape(sizes.n_tensor, chunk, D)

    def exchange(pieces):
        return lax.all_to_all(pieces, "tensor", 0, 0)

    def copies(own):
        return jnp.broadcast_to(own.astype(BF16)[None], (sizes.n_tensor, *own.shape))

    def summed(got):
        return jnp.sum(got.astype(F32), axis=0)

    def full(got):
        return got.reshape(length, D)

    w_ffn = {}
    rows = RowGather(joined(rest_part(0) + out_part(0)), ring)
    w_zx_a = gathered(zx_part(0))
    moved = together(*rows.step_y())
    moved = together(*rows.step_z(moved))
    moved = together(*rows.step_far(moved))
    blocks_a = rows.blocks(together(*rows.step_core(moved)))
    w_ffn[0] = gathered(ffn_part(0))
    w_ffn[1] = gathered(ffn_part(1))

    residual_a = own_rows(layer_input).astype(F32)
    full_unit = unit_of(layer_input.astype(F32))[0]
    normed_a = gained(full_unit, 0, 0).astype(BF16)
    proj_a = rows_matmul(normed_a, ring.own_first, blocks_a, sizes.rest, w_zx_a)
    mixed_a = mixer_forward(proj_a, smalls[0], geometry, sizes)
    own_c = joined(zx_part(1) + rest_part(1) + out_part(1))
    rows_c = RowGather(own_c, ring)
    partial = rows_out(mixed_a, ring.own_first, blocks_a, sizes.rest)
    partial, *moved = together(partial, *rows_c.step_y())
    got = exchange(to_chunks(partial))
    moved = rows_c.step_z(moved)
    middle_a, own = chunk_norm(got, residual_a, norm_gains[0, 1])
    got = exchange(own)
    got, *moved = together(got, *moved)
    moved = rows_c.step_far(moved)
    normed_b = full(got)
    gate_a, up_a, hidden_a, partial = feed_forward(normed_b, w_ffn[0], sizes.ff)
    got = exchange(to_chunks(partial))
    got, *moved = together(got, *moved)
    moved = rows_c.step_core(moved)

    residual_c, own = chunk_norm(got, middle_a, norm_gains[1, 0])
    got = exchange(own)
    w_joint_c = rows_c.rows(rows_c.blocks(moved))
    got, w_joint_c = together(got, w_joint_c)
    w_out_c = w_joint_c[:, sizes.proj :]
    normed_c = full(got)
    proj_c = proj_forward(normed_c, w_joint_c, sizes)
    mixed_c = mixer_forward(proj_c, smalls[1], geometry, sizes)
    got = exchange(to_chunks(times_transposed(mixed_c, w_out_c)))
    middle_c, own = chunk_norm(got, residual_c, norm_gains[1, 1])
    got = exchange(own)
    w_rest_a = rows.rows(blocks_a)
    got, w_rest_a = together(got, w_rest_a)
    normed_d = full(got)

    out_grad_c = cotangent * in_use.astype(BF16)[:, None]
    gradient = own_rows(out_grad_c).astype(F32)
    hidden_c, gate_grad_c, up_grad_c, partial = feed_forward_both(
        normed_d, out_grad_c, w_ffn[1], sizes.ff
    )
    pairs = ((normed_d, gate_grad_c), (normed_d, up_grad_c), (out_grad_c, hidden_c))
    partial, pairs = after(partial, pairs)
    got = exchange(to_chunks(partial))
    in_order = jnp.arange(16, dtype=jnp.int32)
    (ffn_c,) = weight_grads(pairs, in_order, False)
    got, ffn_c = together(got, ffn_c)
    ffn_c = lax.psum_scatter(ffn_c.reshape(D, -1), "dp", tiled=True)
    middle_grad, own, gain_d = chunk_norm_back(got, middle_c, norm_gains[1, 1], gradient)
    got = exchange(own)
    mix_grad_c = full(got)
    ffn_partial = times_transposed(hidden_c, w_ffn[1][:, gate_up_width:])
    mix_grad_c, ffn_partial = together(mix_grad_c, ffn_partial)
    block_got = exchange(to_chunks(ffn_partial))
    mixed_grad = times(mix_grad_c, w_out_c)
    *proj_grad_c, taps_c, heads_c = mixer_backward(mixed_grad, proj_c, smalls[1], geometry, sizes)
    partial = proj_backward(proj_grad_c, w_joint_c[:, : sizes.left], w_joint_c[:, sizes.left :])
    partial, block_got = together(partial, block_got)
    pairs = (*((normed_c, v) for v in proj_grad_c), (mix_grad_c, mixed_c))
    partial, pairs = after(partial, pairs)
    got = exchange(to_chunks(partial))
    got, *halves = together(got, *weight_grads(pairs, ring.other_first, True))
    mix_c = RowScatter(halves, ring)
    gradient, own, gain_c = chunk_norm_back(got, residual_c, norm_gains[1, 0], middle_grad)
    got = exchange(own)
    got, *far = together(got, *mix_c.add_far(mix_c.step_core()))
    mix_c_moved = mix_c.step_z(far)

    out_grad_a = full(got)
    gate_grad_a, up_grad_a, partial = feed_forward_back(
        out_grad_a, gate_a, up_a, w_ffn[0], sizes.ff
    )
    pairs = ((normed_b, gate_grad_a), (normed_b, up_grad_a), (out_grad_a, hidden_a))
    partial, pairs = after(partial, pairs)
    got = exchange(to_chunks(partial))
    (ffn_a,) = weight_grads(pairs, in_order, False)
    got, ffn_a, ffn_c, *mix_c_moved = together(got, ffn_a, ffn_c, *mix_c_moved)
    ffn_a = lax.psum_scatter(ffn_a.reshape(D, -1), "dp", tiled=True)
    middle_grad, own, gain_b = chunk_norm_back(got, middle_a, norm_gains[0, 1], gradient)
    got = exchange(own)
    mix_c_moved = mix_c.step_z_again(mix_c.add_mid(mix_c_moved))
    got, *mix_c_moved = together(got, *mix_c_moved)
    mix_grad_a = full(got)
    block_own = (middle_c + summed(block_got)).astype(BF16)
    mixed_grad = times(mix_grad_a, w_rest_a[:, sizes.rest :])
    *proj_grad_a, taps_a, heads_a = mixer_backward(mixed_grad, proj_a, smalls[0], geometry, sizes)
    pairs = (*((normed_a, v) for v in proj_grad_a), (mix_grad_a, mixed_a))
    mix_c_moved = mix_c.step_y(mix_c.add_last(mix_c_moved))
    *proj_grad_a, other, own = together(
        *proj_grad_a, *weight_grads(pairs, ring.other_first, True)
    )
    mix_a = RowScatter((other, own), ring)
    pieces = to_chunks(proj_backward(proj_grad_a, w_zx_a, w_rest_a))
    pieces, mix_a_got = together(pieces, *mix_a.step_core())
    pieces, f0, f1 = together(pieces, *mix_a.add_far([mix_a_got]))
    moved = mix_a.step_z((f0, f1))
    got = exchange(pieces)
    got, y_c = together(got, *mix_c_moved)
    got, block_own, m0, m1 = together(got, block_own, *moved)
    unused, own, gain_a = chunk_norm_back(
        got, residual_a, norm_gains[0, 0], middle_grad, block_own
    )
    got = exchange(own)
    moved = mix_a.step_z_again(mix_a.add_mid([m0, m1]))
    small = pack_smalls(
        (gain_a, gain_b, gain_c, gain_d), (taps_a, taps_c), (heads_a, heads_c), sizes.n_tensor
    )
    last = mix_a.add_last(moved)
    got, small, ffn_a, mix_a.mid, *last = together(got, small, ffn_a, mix_a.mid, *last)
    moved = mix_a.step_y(last)
    small_got = exchange(small)
    (last,) = moved
    zx_grad, query_grad, mamba_out_grad, attn_out_grad, pieces = finish_mixers(
        (mix_a.terms(last), mix_c.terms(y_c)), sizes, sizes.cuts[1]
    )
    small_got, pieces = together(small_got, pieces)
    shared_got = exchange(pieces)
    small = join_smalls(small_got, sizes)
    others = [ring.swap(small, mask) for mask in (2, 4, 6)]
    unused, small, ffn_a, ffn_c, got, *others = together(
        pieces, small, ffn_a, ffn_c, got, *others
    )
    gate_up_grad, down_grad = finish_feed_forward(ffn_a, ffn_c, gate_up_width)
    input_grad, block_output = full(got[:, :chunk]).astype(F32), full(got[:, chunk:]).astype(F32)
    small = paired_sum(small, *others)
    others = [ring.swap(small, mask) for mask in (1, 8, 9)]
    shared_got, *others = together(shared_got, *others)
    small = paired_sum(small, *others)
    keyval_grad, bc_grad, step_grad = finish_shared(shared_got, sizes)
    keyval_grad = keyval_grad.reshape(LAYERS, -1, 2, KV * HD)
    zx_grad = zx_grad.reshape(LAYERS, rows_own, 2, sizes.inner)
    gate_up_grad = gate_up_grad.reshape(LAYERS, rows_own, 2, sizes.ff)
    gains = small[8:12, :D].reshape(LAYERS, 2, D)
    taps = small[:8].reshape(LAYERS, CONV, -1).transpose(0, 2, 1)
    heads = small[12, : 6 * 128].reshape(LAYERS, 3, 128)[:, :, :NH]
    small_out = (gains, taps, heads[:, 0], heads[:, 1], heads[:, 2])
    return (
        block_output,
        input_grad,
        *small_out,
        zx_grad,
        bc_grad,
        step_grad,
        query_grad,
        keyval_grad,
        mamba_out_grad,
        attn_out_grad,
        gate_up_grad,
        down_grad,
    )


def solution(mesh):
    placed = (
        P("dp", None),
        P("dp", None),
        P(),
        P(),
        P(),
        P(),
        P(),
        P(None, "dp", None, "tensor"),
        P(None, "dp", None),
        P(None, "dp", None),
        P(None, "dp", "tensor"),
        P(None, "dp", None, None),
        P(None, "dp", "tensor"),
        P(None, "dp", "tensor"),
        P(None, "dp", None, "tensor"),
        P(None, "dp", "tensor"),
        P("dp", None),
    )
    return jax.shard_map(
        body,
        mesh=mesh,
        in_specs=placed,
        out_specs=(
            P("dp", None),
            P("dp", None),
            P(),
            P(),
            P(),
            P(),
            P(),
            P(None, "dp", None, "tensor"),
            P(None, ("dp", "tensor"), None),
            P(None, ("dp", "tensor"), None),
            P(None, "dp", "tensor"),
            P(None, ("dp", "tensor"), None, None),
            P(None, "dp", "tensor"),
            P(None, "dp", "tensor"),
            P(None, "dp", None, "tensor"),
            P(None, "dp", "tensor"),
        ),
        check_vma=False,
    )
```

```python
import functools
import math

import jax
import jax.numpy as jnp
from jax import lax
from jax.experimental import pallas as pl
from jax.experimental.pallas import tpu as pltpu
from jax.sharding import PartitionSpec as P

D = 2048
NH = 48
P_SIZE = 64
N = 256
CONV = 4
HQ = 8
KV = 2
HD = 128
LAYERS = 2

EPSILON = 1e-05
ROPE_BASE = 10000.0
PRECISE = lax.Precision.HIGHEST
NO_BATCH = ((), ())
F32 = jnp.float32
BF16 = jnp.bfloat16


def times(left_side, right_side):
    return jnp.dot(left_side, right_side, preferred_element_type=F32)


def times_transposed(left_side, right_side):
    return lax.dot_general(
        left_side, right_side, (((1,), (1,)), NO_BATCH), preferred_element_type=F32
    )


def norm_back(grad_unit, unit_vec, factor):
    return factor * (grad_unit - unit_vec * jnp.mean(grad_unit * unit_vec, axis=1, keepdims=True))


def unit_of(residual):
    factor = lax.rsqrt(jnp.mean(residual * residual, axis=1, keepdims=True) + EPSILON)
    return residual * factor, factor


class Sizes:
    def __init__(self):
        self.n_tensor = lax.axis_size("tensor")
        self.tensor = lax.axis_index("tensor")
        self.heads = NH // self.n_tensor
        self.inner = self.heads * P_SIZE
        self.query_heads = HQ // self.n_tensor
        self.query_width = self.query_heads * HD
        self.head_start = self.tensor * self.heads
        self.keyval = self.tensor * self.query_heads // (HQ // KV)
        self.ff = 4096 // self.n_tensor
        widths = (2 * self.inner, self.query_width, 2 * HD, 2 * N, self.heads)
        ends = [0]
        for w in widths:
            ends.append(ends[-1] + w)
        self.cuts = list(zip(ends[:-1], ends[1:]))
        self.proj = -(-ends[-1] // 128) * 128
        self.mixed = self.inner + self.query_width
        self.left = ends[1]
        self.rest = self.proj - self.left


class Ring:
    def __init__(self):
        place = lax.axis_index("dp")
        self.core, self.z, self.y = place % 2, (place // 2) % 4, place // 8
        near = ((0, 0), (0, 3), (0, 1), (0, 2), (1, 0), (1, 1), (1, 3), (1, 2))
        own = [self.block(dy, dz, self.core) for dy, dz in near]
        other = [self.block(dy, dz, 1 - self.core) for dy, dz in near]
        self.own_first = jnp.stack(own + other).astype(jnp.int32)
        self.other_first = jnp.stack(other + own).astype(jnp.int32)

    def block(self, dy, dz, core):
        return ((self.y ^ dy) * 4 + (self.z ^ dz)) * 2 + core

    def swap(self, value, mask):
        n = lax.axis_size("dp")
        return lax.ppermute(value, "dp", [(i, i ^ mask) for i in range(n)])


def place_blocks(order, parts, count):
    block = parts[0].shape[1:]

    def kernel(order_ref, *refs):
        ins, (out, held, came, left) = refs[: len(parts)], refs[len(parts) :]
        sources = [part.at[k] for part in ins for k in range(part.shape[0])]
        reads = [pltpu.make_async_copy(v, held.at[i], came.at[i]) for i, v in enumerate(sources)]
        writes = [
            pltpu.make_async_copy(held.at[i], out.at[order_ref[i]], left.at[i])
            for i in range(count)
        ]
        for c in reads:
            c.start()
        for r, w in zip(reads, writes):
            r.wait()
            w.start()
        for c in writes:
            c.wait()

    return pl.pallas_call(
        kernel,
        out_shape=jax.ShapeDtypeStruct((count, *block), parts[0].dtype),
        in_specs=[pl.BlockSpec(memory_space=pltpu.SMEM)]
        + [pl.BlockSpec(memory_space=pl.ANY)] * len(parts),
        out_specs=pl.BlockSpec(memory_space=pl.ANY),
        scratch_shapes=[
            pltpu.VMEM((count, *block), parts[0].dtype),
            pltpu.SemaphoreType.DMA((count,)),
            pltpu.SemaphoreType.DMA((count,)),
        ],
        compiler_params=pltpu.CompilerParams(vmem_limit_bytes=48 * 2**20),
        cost_estimate=TINY,
        name="place_blocks",
    )(order, *parts)


def together(*values):
    return lax.optimization_barrier(values)


def after(value, pairs):
    flat = [v for pair in pairs for v in pair]
    value, *flat = together(value, *flat)
    return value, tuple(zip(flat[::2], flat[1::2]))


def paired_sum(a, b, c, d):
    return (a + b) + (c + d)


class RowGather:
    def __init__(self, own, ring):
        self.ring, self.first = ring, own[None]

    def step_y(self):
        return self.ring.swap(self.first, 8), self.ring.swap(self.first, 6)

    def step_z(self, arrived):
        self.second, near = arrived
        self.first = jnp.concatenate([self.first, near], axis=0)
        return (self.ring.swap(self.second, 2),)

    def step_far(self, arrived):
        self.second = jnp.concatenate([self.second, arrived[0]], axis=0)
        return (
            self.ring.swap(self.first, 2),
            self.ring.swap(self.second, 6),
            self.ring.swap(self.first, 1),
            self.ring.swap(self.second, 1),
        )

    def step_core(self, arrived):
        self.first_far, self.second_far, self.first_other, self.second_other = arrived
        return self.ring.swap(self.first_far, 1), self.ring.swap(self.second_far, 1)

    def blocks(self, arrived):
        return [
            self.first,
            self.first_far,
            self.second,
            self.second_far,
            self.first_other,
            arrived[0],
            self.second_other,
            arrived[1],
        ]

    def rows(self, blocks):
        placed = place_blocks(self.ring.own_first, blocks, 16)
        return placed.reshape(-1, placed.shape[2])


def add_blocks(outs, dtype):
    terms = [t for out in outs for block in out for t in block]
    rows, cols = terms[0][0].shape[1:]

    def kernel(*refs):
        at = 0
        for ref, out in zip(refs[len(terms) :], outs):
            for k, block in enumerate(out):
                total = refs[at][0].astype(F32)
                for term in refs[at + 1 : at + len(block)]:
                    total = total + term[0].astype(F32)
                ref[k] = total.astype(dtype)
                at += len(block)

    def spec(index):
        return pl.BlockSpec((1, rows, cols), lambda i: (index, 0, 0))

    return pl.pallas_call(
        kernel,
        grid=(1,),
        in_specs=[spec(index) for _, index in terms],
        out_specs=[pl.BlockSpec((len(out), rows, cols), lambda i: (0, 0, 0)) for out in outs],
        out_shape=[jax.ShapeDtypeStruct((len(out), rows, cols), dtype) for out in outs],
        compiler_params=pltpu.CompilerParams(vmem_limit_bytes=48 * 2**20),
        cost_estimate=TINY,
        name="add_blocks",
    )(*(array for array, _ in terms))


class RowScatter:
    def __init__(self, halves, ring):
        self.ring, (self.other, self.own) = ring, halves

    def both(self, index):
        return [(self.own, index), (self.got, index)]

    def step_core(self):
        return (self.ring.swap(self.other, 1),)

    def add_far(self, arrived):
        (self.got,) = arrived
        return add_blocks([[self.both(2), self.both(3)], [self.both(6), self.both(7)]], BF16)

    def step_z(self, far):
        return self.ring.swap(far[0], 2), self.ring.swap(far[1], 6)

    def add_mid(self, arrived):
        self.far, self.far_two = arrived
        return add_blocks(
            [[self.both(1) + [(self.far, 1)]], [self.both(5) + [(self.far_two, 1)]]], BF16
        )

    def step_z_again(self, mid):
        return self.ring.swap(mid[0], 6), self.ring.swap(mid[1], 2)

    def add_last(self, arrived):
        self.mid, mid_two = arrived
        return add_blocks([[self.both(4) + [(self.far_two, 0), (mid_two, 0)]]], BF16)

    def step_y(self, last):
        return (self.ring.swap(last[0], 8),)

    def terms(self, last):
        return self.own, self.got, self.far, self.mid, last


TINY = pl.CostEstimate(flops=1, bytes_accessed=1, transcendentals=0)


def rows_matmul(x, order, parts, width, weight):
    tokens, block, n = x.shape[0], parts[0].shape[1], len(parts)

    def kernel(order_ref, x_ref, w_ref, *refs):
        refs[n][...] = mm(x_ref[...], w_ref[...], NN)
        total = None
        for k, part in enumerate(refs[:n]):
            lanes = [
                pl.ds(pl.multiple_of(order_ref[2 * k + h] * block, block), block) for h in (0, 1)
            ]
            rows = jnp.concatenate([x_ref[:, v] for v in lanes], axis=1)
            term = mm(rows, part[:, :, :width].reshape(2 * block, width), NN)
            total = term if total is None else total + term
        refs[n + 1][...] = total

    return pl.pallas_call(
        kernel,
        in_specs=[pl.BlockSpec(memory_space=pltpu.SMEM)]
        + [pl.BlockSpec(memory_space=pltpu.VMEM)] * (2 + n),
        out_specs=[pl.BlockSpec(memory_space=pltpu.VMEM)] * 2,
        out_shape=[
            jax.ShapeDtypeStruct((tokens, weight.shape[1]), F32),
            jax.ShapeDtypeStruct((tokens, width), F32),
        ],
        compiler_params=pltpu.CompilerParams(vmem_limit_bytes=56 * 2**20),
        cost_estimate=TINY,
        name="rows_matmul",
    )(order, x, weight, *parts)


def rows_out(mixed, order, parts, start):
    tokens, block, n = mixed.shape[0], parts[0].shape[1], len(parts)

    def kernel(order_ref, x_ref, *refs):
        out = refs[n]
        for k, part in enumerate(refs[:n]):
            rows = part[:, :, start:].reshape(2 * block, x_ref.shape[1])
            term = dot_nt(x_ref[...], rows).astype(BF16)
            for h in (0, 1):
                lanes = pl.ds(pl.multiple_of(order_ref[2 * k + h] * block, block), block)
                out[:, lanes] = term[:, h * block : (h + 1) * block]

    return pl.pallas_call(
        kernel,
        in_specs=[pl.BlockSpec(memory_space=pltpu.SMEM)]
        + [pl.BlockSpec(memory_space=pltpu.VMEM)] * (1 + n),
        out_specs=pl.BlockSpec(memory_space=pltpu.VMEM),
        out_shape=jax.ShapeDtypeStruct((tokens, D), BF16),
        compiler_params=pltpu.CompilerParams(vmem_limit_bytes=56 * 2**20),
        cost_estimate=TINY,
        name="rows_out",
    )(order, mixed, *parts)


def weight_grads(pairs, order, split):
    count, step_blocks = 16, 4
    steps = count // step_blocks
    tokens = pairs[0][0].shape[0]
    rows = pairs[0][0].shape[1] // count
    widths = [y.shape[1] for _, y in pairs]
    total = sum(widths)
    n_x = len(pairs) * step_blocks

    def fill(out_ref, xs, ys):
        at = 0
        for k, (y, w) in enumerate(zip(ys, widths)):
            x = jnp.concatenate([v[...] for v in xs[k * step_blocks : (k + 1) * step_blocks]], axis=1)
            grad = lax.dot_general(x, y[...], (((0,), (0,)), NO_BATCH), preferred_element_type=F32)
            out_ref[:, :, at : at + w] = grad.astype(BF16).reshape(step_blocks, rows, w)
            at += w

    def kernel(order_ref, *refs):
        xs, ys, outs = refs[:n_x], refs[n_x : n_x + len(pairs)], refs[n_x + len(pairs) :]
        if not split:
            fill(outs[0], xs, ys)
            return
        step = pl.program_id(0)

        @pl.when(step < steps // 2)
        def _():
            fill(outs[0], xs, ys)

        @pl.when(step >= steps // 2)
        def _():
            fill(outs[1], xs, ys)

    half = steps // 2
    block = (step_blocks, rows, total)
    if split:
        out_shape = [jax.ShapeDtypeStruct((count // 2, rows, total), BF16)] * 2
        out_specs = [
            pl.BlockSpec(block, lambda i, o: (jnp.minimum(i, half - 1), 0, 0)),
            pl.BlockSpec(block, lambda i, o: (jnp.maximum(i - half, 0), 0, 0)),
        ]
    else:
        out_shape = [jax.ShapeDtypeStruct((count, rows, total), BF16)]
        out_specs = [pl.BlockSpec(block, lambda i, o: (i, 0, 0))]

    def x_spec(k):
        return pl.BlockSpec((tokens, rows), lambda i, o: (0, o[i * step_blocks + k]))

    return pl.pallas_call(
        kernel,
        grid_spec=pltpu.PrefetchScalarGridSpec(
            num_scalar_prefetch=1,
            grid=(steps,),
            in_specs=[x_spec(k) for _ in pairs for k in range(step_blocks)]
            + [pl.BlockSpec((tokens, w), lambda i, o: (0, 0)) for w in widths],
            out_specs=out_specs,
        ),
        out_shape=out_shape,
        compiler_params=pltpu.CompilerParams(vmem_limit_bytes=48 * 2**20),
        cost_estimate=TINY,
        name="weight_grads",
    )(order, *(x for x, _ in pairs for _ in range(step_blocks)), *(y for _, y in pairs))


def dot_nn(a, b):
    return lax.dot_general(
        a.astype(BF16), b.astype(BF16), (((1,), (0,)), NO_BATCH), preferred_element_type=F32
    )


def dot_nt(a, b):
    return lax.dot_general(
        a.astype(BF16), b.astype(BF16), (((1,), (1,)), NO_BATCH), preferred_element_type=F32
    )


def dot_tn(a, b):
    return lax.dot_general(
        a.astype(BF16), b.astype(BF16), (((0,), (0,)), NO_BATCH), preferred_element_type=F32
    )


def logistic(v):
    return 1.0 / (1.0 + jnp.exp(-v))


def softplus(v):
    return jnp.maximum(v, 0.0) + jnp.log1p(jnp.exp(-jnp.abs(v)))


class Mixer:
    def __init__(self, cuts, inner, proj_ref, rest_ref, taps_ref, heads_ref, column_ref, row_ref):
        length, left = proj_ref.shape
        self.inner, self.pairs, self.length = inner, inner // 128, length
        (self.zx0, self.zx1), (q0, q1), (kv0, _), (bc0, bc1), (st0, _) = cuts
        offset = column_ref[:, 0:1]
        self.keep = [(offset >= float(j)).astype(F32) for j in range(CONV)]
        across = lax.broadcasted_iota(jnp.int32, (length, length), 1)
        down = lax.broadcasted_iota(jnp.int32, (length, length), 0)
        self.allowed = (column_ref[:, 1:2] == row_ref[0:1, :]) & (across <= down)
        self.lower = (across <= down).astype(F32)
        self.upper = (across >= down).astype(F32)
        self.first_half = lax.broadcasted_iota(jnp.int32, (1, 128), 1) < P_SIZE
        q0, q1, kv0 = q0 - left, q1 - left, kv0 - left
        self.query, self.key = rest_ref[:, q0:q1], rest_ref[:, kv0 : kv0 + HD]
        self.value = rest_ref[:, kv0 + HD : kv0 + 2 * HD]
        self.signal = jnp.concatenate(
            [proj_ref[:, inner : 2 * inner], rest_ref[:, bc0 - left : bc1 - left]], axis=1
        )
        pre = self.signal * self.keep[0] * taps_ref[CONV - 1 : CONV, :]
        for j in range(1, CONV):
            tap = taps_ref[CONV - 1 - j : CONV - j, :]
            pre = pre + pltpu.roll(self.signal, j, 0) * self.keep[j] * tap
        self.pre = pre
        self.pre_gate = logistic(pre)
        self.act = pre * self.pre_gate
        self.b_state = self.act[:, inner : inner + N].astype(BF16)
        self.c_state = self.act[:, inner + N :].astype(BF16)
        self.heads = heads_ref
        self.step_pre = rest_ref[:, st0 - left : st0 - left + 128] + heads_ref[0:1, :]
        self.step = softplus(self.step_pre)
        self.rate = heads_ref[1:2, :]
        self.total = jnp.dot(self.lower, -self.step * self.rate, precision=PRECISE)
        self.total_t = self.total.T
        self.cb = dot_nt(self.c_state, self.b_state)
        self.proj_ref = proj_ref

    def by_half(self, first, second):
        return jnp.where(self.first_half, first, second)

    def decay(self, head):
        gap = self.total[:, head : head + 1] - self.total_t[head : head + 1, :]
        return jnp.where(self.allowed, jnp.exp(jnp.where(self.allowed, gap, 0.0)), 0.0)

    def pair(self, p):
        lanes = slice(128 * p, 128 * p + 128)
        a, b = 2 * p, 2 * p + 1
        inputs = self.act[:, lanes]
        step = self.by_half(self.step[:, a : a + 1], self.step[:, b : b + 1])
        skip = self.by_half(self.heads[2:3, a : a + 1], self.heads[2:3, b : b + 1])
        gate = self.proj_ref[:, lanes]
        return inputs, step, skip, gate, inputs * step

    def prob(self, query_rot, key_rot):
        scores = dot_nt(query_rot, key_rot) * (1.0 / math.sqrt(HD))
        scores = jnp.where(self.allowed, scores, -1e30)
        weight = jnp.exp(scores - jnp.max(scores, axis=1, keepdims=True))
        return weight / jnp.sum(weight, axis=1, keepdims=True)


def turn(v, cosine, sine, direction):
    return v * cosine + (direction * sine) * pltpu.roll(v, HD // 2, 1)


def mixer_forward_kernel(cuts, inner, proj, rest, taps, heads, column, row, cosine, sine, out):
    m = Mixer(cuts, inner, proj, rest, taps, heads, column, row)
    for p in range(m.pairs):
        inputs, step, skip, gate, scaled = m.pair(p)
        scaled = scaled.astype(BF16)
        mixed = [dot_nn(m.cb * m.decay(2 * p + k), scaled) for k in range(2)]
        ssm = m.by_half(*mixed) + skip * inputs
        out[:, 128 * p : 128 * p + 128] = (ssm * gate * logistic(gate)).astype(BF16)
    query_rot = turn(m.query, cosine[...], sine[...], 1.0)
    key_rot = turn(m.key, cosine[...], sine[...], 1.0)
    out[:, inner:] = dot_nn(m.prob(query_rot, key_rot), m.value).astype(BF16)


def mixer_backward_kernel(
    cuts, inner, proj, rest, taps, heads, column, row, cosine, sine, grad, out, out_rest, taps_grad, heads_grad
):
    m = Mixer(cuts, inner, proj, rest, taps, heads, column, row)
    lane = lax.broadcasted_iota(jnp.int32, (1, 128), 1)
    cos, sin = cosine[...], sine[...]
    (q0, q1), (kv0, _), (bc0, bc1), (st0, _) = cuts[1:]
    left = proj.shape[1]
    q0, q1, kv0 = q0 - left, q1 - left, kv0 - left

    query_rot, key_rot = turn(m.query, cos, sin, 1.0), turn(m.key, cos, sin, 1.0)
    prob = m.prob(query_rot, key_rot)
    attended_grad = grad[:, inner:]
    out_rest[:, kv0 + HD : kv0 + 2 * HD] = dot_tn(prob, attended_grad).astype(BF16)
    prob_grad = dot_nt(attended_grad, m.value)
    inner_sum = jnp.sum(prob * prob_grad, axis=1, keepdims=True)
    score_grad = prob * (prob_grad - inner_sum) * (1.0 / math.sqrt(HD))
    out_rest[:, q0:q1] = turn(dot_nn(score_grad, key_rot), cos, sin, -1.0).astype(BF16)
    out_rest[:, kv0 : kv0 + HD] = turn(dot_tn(score_grad, query_rot), cos, sin, -1.0).astype(BF16)

    cb_grad = jnp.zeros((m.length, m.length), F32)
    down_sums = jnp.zeros((m.length, 128), F32)
    across_sums = []
    step_grad = jnp.zeros((m.length, 128), F32)
    skip_grad = jnp.zeros((1, 128), F32)
    inputs_grads = []
    for p in range(m.pairs):
        inputs, step, skip, gate, scaled = m.pair(p)
        gated_grad = grad[:, 128 * p : 128 * p + 128]
        sig = logistic(gate)
        ssm_grad = gated_grad * gate * sig
        scaled_b, ssm_grad_b = scaled.astype(BF16), ssm_grad.astype(BF16)
        ssm, scaled_grad = [], []
        for k in range(2):
            h = 2 * p + k
            decay = m.decay(h)
            mixing = m.cb * decay
            mixing_b = mixing.astype(BF16)
            ssm.append(dot_nn(mixing_b, scaled_b))
            scaled_grad.append(dot_tn(mixing_b, ssm_grad_b))
            mine = m.first_half if k == 0 else jnp.logical_not(m.first_half)
            mixing_grad = dot_nt(jnp.where(mine, ssm_grad, 0.0), scaled_b)
            cb_grad = cb_grad + mixing_grad * decay
            gap_grad = mixing_grad * mixing
            down_sums = jnp.where(lane == h, jnp.sum(gap_grad, axis=1, keepdims=True), down_sums)
            across_sums.append(jnp.sum(gap_grad, axis=0, keepdims=True))
        ssm = m.by_half(*ssm) + skip * inputs
        scaled_grad = m.by_half(*scaled_grad)
        slope = sig * (1.0 + gate * (1.0 - sig))
        out[:, 128 * p : 128 * p + 128] = (gated_grad * ssm * slope).astype(BF16)
        inputs_grads.append(scaled_grad * step + ssm_grad * skip)
        by_step, by_skip = scaled_grad * inputs, ssm_grad * inputs
        for k in range(2):
            mine = m.first_half if k == 0 else jnp.logical_not(m.first_half)
            here = lane == 2 * p + k
            step_grad = jnp.where(
                here, jnp.sum(jnp.where(mine, by_step, 0.0), axis=1, keepdims=True), step_grad
            )
            own_skip = jnp.sum(jnp.where(mine, by_skip, 0.0), axis=0, keepdims=True)
            skip_grad = jnp.where(here, jnp.sum(own_skip, axis=1, keepdims=True), skip_grad)

    across = jnp.concatenate(
        across_sums + [jnp.zeros((128 - len(across_sums), m.length), F32)], axis=0
    )
    term_grad = jnp.dot(m.upper, down_sums - across.T, precision=PRECISE)
    step_grad = step_grad - term_grad * m.rate
    step_pre_grad = step_grad * logistic(m.step_pre)
    out_rest[:, st0 - left : st0 - left + 128] = step_pre_grad.astype(BF16)
    heads_grad[0:1, :] = jnp.sum(step_pre_grad, axis=0, keepdims=True)
    heads_grad[1:2, :] = -jnp.sum(term_grad * m.step, axis=0, keepdims=True) * m.rate
    heads_grad[2:3, :] = skip_grad
    heads_grad[3:8, :] = jnp.zeros((5, 128), F32)

    c_grad = dot_nn(cb_grad, m.b_state)
    b_grad = dot_tn(cb_grad, m.c_state)
    act_grad = jnp.concatenate(inputs_grads + [b_grad, c_grad], axis=1)
    pre_grad = act_grad * (m.pre_gate * (1.0 + m.pre * (1.0 - m.pre_gate)))
    signal_grad = jnp.zeros_like(pre_grad)
    for j in range(CONV):
        masked = pre_grad * m.keep[j]
        back = masked if j == 0 else pltpu.roll(masked, m.length - j, 0)
        shifted = m.signal if j == 0 else pltpu.roll(m.signal, j, 0)
        k = CONV - 1 - j
        signal_grad = signal_grad + back * taps[k : k + 1, :]
        taps_grad[k : k + 1, :] = jnp.sum(masked * shifted, axis=0, keepdims=True)
    taps_grad[CONV:8, :] = jnp.zeros((8 - CONV, pre_grad.shape[1]), F32)
    out[:, inner : 2 * inner] = signal_grad[:, :inner].astype(BF16)
    out_rest[:, bc0 - left : bc1 - left] = signal_grad[:, inner:].astype(BF16)


def mm(a, b, dims):
    return lax.dot_general(a, b, (dims, NO_BATCH), preferred_element_type=F32)


NN, NT = ((1,), (0,)), ((1,), (1,))


def proj_forward(x, weight, sizes):
    tokens, depth = x.shape
    tile = 256
    first, steps = sizes.left // tile, sizes.proj // tile

    def kernel(x_ref, w_ref, left, rest):
        value = mm(x_ref[...], w_ref[...], NN)
        step = pl.program_id(0)

        @pl.when(step < first)
        def _():
            left[...] = value

        @pl.when(step >= first)
        def _():
            rest[...] = value

    return pl.pallas_call(
        kernel,
        grid=(steps,),
        in_specs=[
            pl.BlockSpec((tokens, depth), lambda i: (0, 0)),
            pl.BlockSpec((depth, tile), lambda i: (0, i)),
        ],
        out_specs=[
            pl.BlockSpec((tokens, tile), lambda i: (0, jnp.minimum(i, first - 1))),
            pl.BlockSpec((tokens, tile), lambda i: (0, jnp.maximum(i - first, 0))),
        ],
        out_shape=[
            jax.ShapeDtypeStruct((tokens, sizes.left), F32),
            jax.ShapeDtypeStruct((tokens, sizes.rest), F32),
        ],
        compiler_params=pltpu.CompilerParams(vmem_limit_bytes=48 * 2**20),
        cost_estimate=TINY,
        name="proj_forward",
    )(x, weight)


def proj_backward(grads, w_zx, w_rest):
    rest = w_rest[:, : grads[1].shape[1]]
    return times_transposed(grads[0], w_zx) + times_transposed(grads[1], rest)


def feed_forward_call(kernel, name, x, tiled, weight, ff, tiled_outs, tile=256):
    tokens, depth = x[0].shape
    steps = ff // tile

    def whole_kernel(*refs):
        *rest, out, total = refs
        step = pl.program_id(0)
        term = kernel(*rest)

        @pl.when(step == 0)
        def _():
            total[...] = term

        @pl.when(step > 0)
        def _():
            total[...] += term

        @pl.when(step == steps - 1)
        def _():
            out[...] = total[...].astype(BF16)

    def column(part):
        return pl.BlockSpec((depth, tile), lambda i: (0, part * steps + i))

    def tile_spec(_):
        return pl.BlockSpec((tokens, tile), lambda i: (0, i))

    return pl.pallas_call(
        whole_kernel,
        grid=(steps,),
        in_specs=[pl.BlockSpec((tokens, depth), lambda i: (0, 0)) for _ in x]
        + [tile_spec(v) for v in tiled]
        + [column(k) for k in range(3)],
        out_specs=[tile_spec(v) for v in tiled_outs]
        + [pl.BlockSpec((tokens, depth), lambda i: (0, 0))],
        out_shape=[jax.ShapeDtypeStruct((tokens, ff), v) for v in tiled_outs]
        + [jax.ShapeDtypeStruct((tokens, depth), BF16)],
        scratch_shapes=[pltpu.VMEM((tokens, depth), F32)],
        compiler_params=pltpu.CompilerParams(vmem_limit_bytes=56 * 2**20),
        cost_estimate=TINY,
        name=name,
    )(*x, *tiled, weight, weight, weight)


def gate_grads(hidden_grad, gate, up):
    sig = logistic(gate)
    gate_grad = hidden_grad * up * (sig * (1.0 + gate * (1.0 - sig)))
    return gate_grad.astype(BF16), (hidden_grad * gate * sig).astype(BF16)


def feed_forward(x, weight, ff):
    def kernel(x_ref, w_gate, w_up, w_down, gate_ref, up_ref, hidden_ref):
        gate, up = mm(x_ref[...], w_gate[...], NN), mm(x_ref[...], w_up[...], NN)
        hidden = (gate * logistic(gate) * up).astype(BF16)
        gate_ref[...], up_ref[...], hidden_ref[...] = gate, up, hidden
        return mm(hidden, w_down[...], NT)

    return feed_forward_call(kernel, "feed_forward", (x,), (), weight, ff, (F32, F32, BF16))


def feed_forward_both(x, grad, weight, ff):
    def kernel(x_ref, grad_ref, w_gate, w_up, w_down, hidden_ref, gate_out, up_out):
        gate, up = mm(x_ref[...], w_gate[...], NN), mm(x_ref[...], w_up[...], NN)
        hidden_ref[...] = (gate * logistic(gate) * up).astype(BF16)
        grads = gate_grads(mm(grad_ref[...], w_down[...], NN), gate, up)
        gate_out[...], up_out[...] = grads
        return mm(grads[0], w_gate[...], NT) + mm(grads[1], w_up[...], NT)

    return feed_forward_call(
        kernel, "feed_forward_both", (x, grad), (), weight, ff, (BF16, BF16, BF16)
    )


def feed_forward_back(grad, gate, up, weight, ff):
    def kernel(grad_ref, gate_ref, up_ref, w_gate, w_up, w_down, gate_out, up_out):
        grads = gate_grads(mm(grad_ref[...], w_down[...], NN), gate_ref[...], up_ref[...])
        gate_out[...], up_out[...] = grads
        return mm(grads[0], w_gate[...], NT) + mm(grads[1], w_up[...], NT)

    return feed_forward_call(
        kernel, "feed_forward_back", (grad,), (gate, up), weight, ff, (BF16, BF16)
    )


def whole(shapes):
    return [pl.BlockSpec(memory_space=pltpu.VMEM) for _ in shapes]


def mixer_forward(proj, smalls, geometry, sizes):
    length = proj[0].shape[0]
    ins = (*proj, *smalls, *geometry)
    return pl.pallas_call(
        functools.partial(mixer_forward_kernel, sizes.cuts, sizes.inner),
        in_specs=whole([v.shape for v in ins]),
        out_specs=whole([(length, sizes.mixed)])[0],
        out_shape=jax.ShapeDtypeStruct((length, sizes.mixed), BF16),
        compiler_params=pltpu.CompilerParams(vmem_limit_bytes=48 * 2**20),
        cost_estimate=TINY,
        name="mixer_forward",
    )(*ins)


def mixer_backward(mixed_grad, proj, smalls, geometry, sizes):
    ins = (*proj, *smalls, *geometry, mixed_grad)
    outs = [jax.ShapeDtypeStruct(v.shape, BF16) for v in proj]
    outs += [jax.ShapeDtypeStruct(v.shape, F32) for v in smalls]
    return pl.pallas_call(
        functools.partial(mixer_backward_kernel, sizes.cuts, sizes.inner),
        in_specs=whole([v.shape for v in ins]),
        out_specs=whole([v.shape for v in outs]),
        out_shape=outs,
        compiler_params=pltpu.CompilerParams(vmem_limit_bytes=48 * 2**20),
        cost_estimate=TINY,
        name="mixer_backward",
    )(*ins)


def chunk_norm(got, residual, gain):
    n, rows, width = got.shape

    def kernel(got_ref, residual_ref, gain_ref, out, copies):
        total = residual_ref[...]
        for k in range(n):
            total = total + got_ref[k].astype(F32)
        out[...] = total
        normed = (unit_of(total)[0] * gain_ref[...]).astype(BF16)
        for k in range(n):
            copies[k] = normed

    ins = (got, residual, gain[None])
    outs = [jax.ShapeDtypeStruct((rows, width), F32), jax.ShapeDtypeStruct(got.shape, BF16)]
    return pl.pallas_call(
        kernel,
        in_specs=whole([v.shape for v in ins]),
        out_specs=whole([v.shape for v in outs]),
        out_shape=outs,
        cost_estimate=TINY,
        name="chunk_norm",
    )(*ins)


def chunk_norm_back(got, residual, gain, gradient, extra=None):
    n, rows, width = got.shape
    sent = rows if extra is None else rows + extra.shape[0]

    def kernel(got_ref, residual_ref, gain_ref, gradient_ref, *refs):
        out, copies, gain_grad = refs[-3:]
        normed_grad = got_ref[0].astype(F32)
        for k in range(1, n):
            normed_grad = normed_grad + got_ref[k].astype(F32)
        unit, factor = unit_of(residual_ref[...])
        gain_grad[...] = jnp.sum(normed_grad * unit, axis=0, keepdims=True)
        total = gradient_ref[...] + norm_back(normed_grad * gain_ref[...], unit, factor)
        out[...] = total
        total = total.astype(BF16)
        for k in range(n):
            copies[k, :rows] = total
            if extra is not None:
                copies[k, rows:] = refs[0][...]

    ins = (got, residual, gain[None], gradient) + (() if extra is None else (extra,))
    outs = [
        jax.ShapeDtypeStruct((rows, width), F32),
        jax.ShapeDtypeStruct((n, sent, width), BF16),
        jax.ShapeDtypeStruct((1, width), F32),
    ]
    return pl.pallas_call(
        kernel,
        in_specs=whole([v.shape for v in ins]),
        out_specs=whole([v.shape for v in outs]),
        out_shape=outs,
        cost_estimate=TINY,
        name="chunk_norm_back",
    )(*ins)


SMALL_ROWS, SMALL_WIDTH = 32, 1024


def pack_smalls(gains, taps, heads, n):
    gain_rows = len(gains) * D // SMALL_WIDTH
    tap_rows = len(taps) * CONV

    def kernel(*refs):
        *ins, out, held = refs
        held[...] = jnp.zeros(held.shape, F32)
        for g, ref in enumerate(ins[: len(gains)]):
            for h in range(D // SMALL_WIDTH):
                row = g * (D // SMALL_WIDTH) + h
                held[row : row + 1, :] = ref[:, h * SMALL_WIDTH : (h + 1) * SMALL_WIDTH]
        for l, ref in enumerate(ins[len(gains) : len(gains) + len(taps)]):
            row = gain_rows + l * CONV
            held[row : row + CONV, : ref.shape[1]] = ref[:CONV, :]
        for l, ref in enumerate(ins[len(gains) + len(taps) :]):
            row = gain_rows + tap_rows + 3 * l
            held[row : row + 3, :128] = ref[:3, :]
        for k in range(n):
            out[k] = held[...].astype(BF16)

    ins = (*gains, *taps, *heads)
    return pl.pallas_call(
        kernel,
        in_specs=whole([v.shape for v in ins]),
        out_specs=whole([0])[0],
        out_shape=jax.ShapeDtypeStruct((n, SMALL_ROWS, SMALL_WIDTH), BF16),
        scratch_shapes=[pltpu.VMEM((SMALL_ROWS, SMALL_WIDTH), F32)],
        cost_estimate=TINY,
        name="pack_smalls",
    )(*ins)


def join_smalls(got, sizes):
    n = got.shape[0]
    per_gain = D // SMALL_WIDTH
    gain_rows, inner = 4 * per_gain, sizes.inner
    width = NH * P_SIZE + 2 * N

    def kernel(got_ref, out):
        out[...] = jnp.zeros(out.shape, F32)
        taps = slice(gain_rows, gain_rows + 8)
        parts = [got_ref[k].astype(F32) for k in range(n)]
        for k, part in enumerate(parts):
            out[:8, k * inner : (k + 1) * inner] = part[taps, :inner]
        total = sum(parts[1:], parts[0])
        shared, gains = total[taps, inner : inner + 2 * N], total[:gain_rows]
        heads = parts[0][gain_rows + 8 : gain_rows + 16, :128]
        for k in range(1, n):
            part = parts[k][gain_rows + 8 : gain_rows + 16, :128]
            heads = heads + pltpu.roll(part, k * sizes.heads, 1)
        out[:8, n * inner :] = shared
        for g in range(4):
            for h in range(per_gain):
                lanes = slice(h * SMALL_WIDTH, (h + 1) * SMALL_WIDTH)
                row = g * per_gain + h
                out[8 + g : 9 + g, lanes] = gains[row : row + 1, :]
        for m in range(6):
            out[12:13, 128 * m : 128 * m + 128] = heads[m : m + 1, :]

    return pl.pallas_call(
        kernel,
        in_specs=whole([0]),
        out_specs=whole([0])[0],
        out_shape=jax.ShapeDtypeStruct((16, width), F32),
        cost_estimate=TINY,
        name="join_smalls",
    )(got)


def first_blocks(arrays):
    return [
        pl.BlockSpec((1, *v.shape[1:]), lambda i: (0, 0, 0)) if v.ndim == 3 else whole([0])[0]
        for v in arrays
    ]


def added(refs):
    total = refs[0][0].astype(F32)
    for ref in refs[1:]:
        total = total + ref[0].astype(F32)
    return total


def finish_mixers(layers, sizes, cuts):
    count, n = len(layers[0]), sizes.n_tensor
    rows = layers[0][0].shape[1]
    (q0, q1), out0, end = cuts, sizes.proj, sizes.proj + sizes.mixed
    edges = (0, q0, q1, out0, out0 + sizes.inner, end)

    def kernel(*refs):
        zx, query, mamba, attn, pieces = refs[2 * count :]
        for l in range(2):
            total = added(refs[l * count : (l + 1) * count])
            parts = [total[:, a:b] for a, b in zip(edges[:-1], edges[1:])]
            zx[l], query[l], mamba[l], attn[l] = parts[0], parts[1], parts[3], parts[4]
            shared = parts[2].astype(BF16)
            for k in range(n):
                pieces[k, l] = shared[k * (rows // n) : (k + 1) * (rows // n)]

    ins = (*layers[0], *layers[1])
    outs = [jax.ShapeDtypeStruct((2, rows, w), F32) for w in (q0, q1 - q0, sizes.inner, end - edges[4])]
    outs.append(jax.ShapeDtypeStruct((n, 2, rows // n, out0 - q1), BF16))
    return pl.pallas_call(
        kernel,
        grid=(1,),
        in_specs=first_blocks(ins),
        out_specs=whole(outs),
        out_shape=outs,
        compiler_params=pltpu.CompilerParams(vmem_limit_bytes=48 * 2**20),
        cost_estimate=TINY,
        name="finish_mixers",
    )(*ins)


def finish_feed_forward(first, second, cut):
    rows, width = second.shape

    def kernel(first_ref, second_ref, gate_up, down):
        for l, ref in enumerate((first_ref, second_ref)):
            total = ref[...].astype(F32)
            gate_up[l], down[l] = total[:, :cut], total[:, cut:]

    ins = (first, second)
    outs = [jax.ShapeDtypeStruct((2, rows, w), F32) for w in (cut, width - cut)]
    return pl.pallas_call(
        kernel,
        in_specs=whole(ins),
        out_specs=whole(outs),
        out_shape=outs,
        cost_estimate=TINY,
        name="finish_feed_forward",
    )(*ins)


def finish_shared(got, sizes):
    n, layers, rows, _ = got.shape
    pair = n // KV

    def kernel(got_ref, keyval, bc, step):
        for l in range(layers):
            parts = [got_ref[k, l].astype(F32) for k in range(n)]
            for p in range(KV):
                mine = sum(parts[p * pair + 1 : (p + 1) * pair], parts[p * pair])
                for c in range(2):
                    at = (c * KV + p) * HD
                    keyval[l, :, at : at + HD] = mine[:, c * HD : (c + 1) * HD]
            bc[l] = sum([v[:, 2 * HD : 2 * HD + 2 * N] for v in parts[1:]], parts[0][:, 2 * HD : 2 * HD + 2 * N])
            steps = parts[0][:, 2 * HD + 2 * N :]
            for k in range(1, n):
                steps = steps + pltpu.roll(parts[k][:, 2 * HD + 2 * N :], k * sizes.heads, 1)
            step[l] = steps[:, :NH]

    outs = [jax.ShapeDtypeStruct((layers, rows, w), F32) for w in (2 * KV * HD, 2 * N, NH)]
    return pl.pallas_call(
        kernel,
        in_specs=whole([0]),
        out_specs=whole(outs),
        out_shape=outs,
        cost_estimate=TINY,
        name="finish_shared",
    )(got)


def own_smalls(smalls, sizes):
    kernel, step_bias, log_rate, skip_gain = smalls
    own = jnp.concatenate(
        [
            lax.dynamic_slice_in_dim(kernel, sizes.head_start * P_SIZE, sizes.inner, 0),
            kernel[NH * P_SIZE :],
        ],
        axis=0,
    )
    taps = jnp.pad(own.T, ((0, 8 - CONV), (0, 0)))
    heads = jnp.stack([step_bias, jnp.exp(log_rate), skip_gain])
    heads = lax.dynamic_slice_in_dim(heads, sizes.head_start, sizes.heads, 1)
    return taps, jnp.pad(heads, ((0, 5), (0, 128 - sizes.heads)))


def layout_of(lengths, row_count):
    seq_ends = jnp.cumsum(lengths)
    seq_starts = seq_ends - lengths
    position = jnp.arange(row_count, dtype=jnp.int32)
    past = position[:, None] >= seq_ends[None, :]
    segment = jnp.sum(past.astype(jnp.int32), axis=1)
    first_of = jnp.max(jnp.where(past, seq_ends[None, :], 0), axis=1)
    offset = position - first_of
    in_use = (position < seq_ends[-1]).astype(F32)
    offset, segment = offset.astype(F32), segment.astype(F32)
    column = jnp.pad(jnp.stack([offset, segment], axis=1), ((0, 0), (0, 126)))
    row = jnp.broadcast_to(segment[None], (8, row_count))
    half_width = HD // 2
    frequency = jnp.exp(
        jnp.arange(half_width, dtype=F32) * (-2.0 * math.log(ROPE_BASE) / HD)
    )
    angles = offset[:, None] * frequency[None, :]
    cosine, sine = jnp.cos(angles), jnp.sin(angles)
    tables = jnp.concatenate([cosine, cosine], axis=1), jnp.concatenate([-sine, sine], axis=1)
    return (column, row, *tables), in_use


def body(
    layer_input,
    seq_lengths,
    norm_gains,
    conv_kernel,
    step_bias,
    log_rate,
    skip_gain,
    zx_weight,
    bc_weight,
    step_weight,
    query_weight,
    keyval_weight,
    mamba_out_weight,
    attn_out_weight,
    gate_up_weight,
    down_weight,
    cotangent,
):
    sizes = Sizes()
    ring = Ring()
    length = layer_input.shape[0]
    chunk = length // sizes.n_tensor
    first = sizes.tensor * chunk
    rows_own = zx_weight.shape[1]
    gate_up_width = 2 * sizes.ff
    geometry, in_use = layout_of(seq_lengths[0], length)

    def zx_part(layer):
        return [zx_weight[layer].reshape(rows_own, -1)]

    def rest_part(layer):
        step_own = lax.dynamic_slice_in_dim(step_weight[layer], sizes.head_start, sizes.heads, 1)
        pair = lax.dynamic_slice_in_dim(keyval_weight[layer], sizes.keyval * HD, HD, 2)
        parts = [query_weight[layer], pair.reshape(rows_own, -1), bc_weight[layer], step_own]
        used = sum(p.shape[1] for p in parts)
        return parts + [jnp.zeros((rows_own, sizes.rest - used), BF16)]

    def out_part(layer):
        return [mamba_out_weight[layer], attn_out_weight[layer]]

    def ffn_part(layer):
        return [gate_up_weight[layer].reshape(rows_own, -1), down_weight[layer]]

    def joined(parts):
        return jnp.concatenate(parts, axis=1)

    def gathered(parts):
        return lax.all_gather(joined(parts), "dp", axis=0, tiled=True)

    smalls = [
        own_smalls((conv_kernel[l], step_bias[l], log_rate[l], skip_gain[l]), sizes)
        for l in range(LAYERS)
    ]

    def own_rows(v):
        return lax.dynamic_slice_in_dim(v, first, chunk, 0)

    def gained(unit, layer, which):
        return unit * norm_gains[layer, which][None, :]

    def to_chunks(partial):
        return partial.astype(BF16).reshape(sizes.n_tensor, chunk, D)

    def exchange(pieces):
        return lax.all_to_all(pieces, "tensor", 0, 0)

    def copies(own):
        return jnp.broadcast_to(own.astype(BF16)[None], (sizes.n_tensor, *own.shape))

    def summed(got):
        return jnp.sum(got.astype(F32), axis=0)

    def full(got):
        return got.reshape(length, D)

    w_ffn = {}
    rows = RowGather(joined(rest_part(0) + out_part(0)), ring)
    w_zx_a = gathered(zx_part(0))
    moved = together(*rows.step_y())
    moved = together(*rows.step_z(moved))
    moved = together(*rows.step_far(moved))
    blocks_a = rows.blocks(together(*rows.step_core(moved)))
    w_ffn[0] = gathered(ffn_part(0))
    w_ffn[1] = gathered(ffn_part(1))

    residual_a = own_rows(layer_input).astype(F32)
    full_unit = unit_of(layer_input.astype(F32))[0]
    normed_a = gained(full_unit, 0, 0).astype(BF16)
    proj_a = rows_matmul(normed_a, ring.own_first, blocks_a, sizes.rest, w_zx_a)
    mixed_a = mixer_forward(proj_a, smalls[0], geometry, sizes)
    own_c = joined(zx_part(1) + rest_part(1) + out_part(1))
    rows_c = RowGather(own_c, ring)
    partial = rows_out(mixed_a, ring.own_first, blocks_a, sizes.rest)
    partial, *moved = together(partial, *rows_c.step_y())
    got = exchange(to_chunks(partial))
    moved = rows_c.step_z(moved)
    middle_a, own = chunk_norm(got, residual_a, norm_gains[0, 1])
    got = exchange(own)
    got, *moved = together(got, *moved)
    moved = rows_c.step_far(moved)
    normed_b = full(got)
    gate_a, up_a, hidden_a, partial = feed_forward(normed_b, w_ffn[0], sizes.ff)
    got = exchange(to_chunks(partial))
    got, *moved = together(got, *moved)
    moved = rows_c.step_core(moved)

    residual_c, own = chunk_norm(got, middle_a, norm_gains[1, 0])
    got = exchange(own)
    w_joint_c = rows_c.rows(rows_c.blocks(moved))
    got, w_joint_c = together(got, w_joint_c)
    w_out_c = w_joint_c[:, sizes.proj :]
    normed_c = full(got)
    proj_c = proj_forward(normed_c, w_joint_c, sizes)
    mixed_c = mixer_forward(proj_c, smalls[1], geometry, sizes)
    got = exchange(to_chunks(times_transposed(mixed_c, w_out_c)))
    middle_c, own = chunk_norm(got, residual_c, norm_gains[1, 1])
    got = exchange(own)
    w_rest_a = rows.rows(blocks_a)
    got, w_rest_a = together(got, w_rest_a)
    normed_d = full(got)

    out_grad_c = cotangent * in_use.astype(BF16)[:, None]
    gradient = own_rows(out_grad_c).astype(F32)
    hidden_c, gate_grad_c, up_grad_c, partial = feed_forward_both(
        normed_d, out_grad_c, w_ffn[1], sizes.ff
    )
    pairs = ((normed_d, gate_grad_c), (normed_d, up_grad_c), (out_grad_c, hidden_c))
    partial, pairs = after(partial, pairs)
    got = exchange(to_chunks(partial))
    in_order = jnp.arange(16, dtype=jnp.int32)
    (ffn_c,) = weight_grads(pairs, in_order, False)
    got, ffn_c = together(got, ffn_c)
    ffn_c = lax.psum_scatter(ffn_c.reshape(D, -1), "dp", tiled=True)
    middle_grad, own, gain_d = chunk_norm_back(got, middle_c, norm_gains[1, 1], gradient)
    got = exchange(own)
    mix_grad_c = full(got)
    ffn_partial = times_transposed(hidden_c, w_ffn[1][:, gate_up_width:])
    mix_grad_c, ffn_partial = together(mix_grad_c, ffn_partial)
    block_got = exchange(to_chunks(ffn_partial))
    mixed_grad = times(mix_grad_c, w_out_c)
    *proj_grad_c, taps_c, heads_c = mixer_backward(mixed_grad, proj_c, smalls[1], geometry, sizes)
    partial = proj_backward(proj_grad_c, w_joint_c[:, : sizes.left], w_joint_c[:, sizes.left :])
    partial, block_got = together(partial, block_got)
    pairs = (*((normed_c, v) for v in proj_grad_c), (mix_grad_c, mixed_c))
    partial, pairs = after(partial, pairs)
    got = exchange(to_chunks(partial))
    got, *halves = together(got, *weight_grads(pairs, ring.other_first, True))
    mix_c = RowScatter(halves, ring)
    gradient, own, gain_c = chunk_norm_back(got, residual_c, norm_gains[1, 0], middle_grad)
    got = exchange(own)
    got, *far = together(got, *mix_c.add_far(mix_c.step_core()))
    mix_c_moved = mix_c.step_z(far)

    out_grad_a = full(got)
    gate_grad_a, up_grad_a, partial = feed_forward_back(
        out_grad_a, gate_a, up_a, w_ffn[0], sizes.ff
    )
    pairs = ((normed_b, gate_grad_a), (normed_b, up_grad_a), (out_grad_a, hidden_a))
    partial, pairs = after(partial, pairs)
    got = exchange(to_chunks(partial))
    (ffn_a,) = weight_grads(pairs, in_order, False)
    got, ffn_a, ffn_c, *mix_c_moved = together(got, ffn_a, ffn_c, *mix_c_moved)
    ffn_a = lax.psum_scatter(ffn_a.reshape(D, -1), "dp", tiled=True)
    middle_grad, own, gain_b = chunk_norm_back(got, middle_a, norm_gains[0, 1], gradient)
    got = exchange(own)
    mix_c_moved = mix_c.step_z_again(mix_c.add_mid(mix_c_moved))
    got, *mix_c_moved = together(got, *mix_c_moved)
    mix_grad_a = full(got)
    block_own = (middle_c + summed(block_got)).astype(BF16)
    mixed_grad = times(mix_grad_a, w_rest_a[:, sizes.rest :])
    *proj_grad_a, taps_a, heads_a = mixer_backward(mixed_grad, proj_a, smalls[0], geometry, sizes)
    pairs = (*((normed_a, v) for v in proj_grad_a), (mix_grad_a, mixed_a))
    mix_c_moved = mix_c.step_y(mix_c.add_last(mix_c_moved))
    *proj_grad_a, other, own = together(
        *proj_grad_a, *weight_grads(pairs, ring.other_first, True)
    )
    mix_a = RowScatter((other, own), ring)
    pieces = to_chunks(proj_backward(proj_grad_a, w_zx_a, w_rest_a))
    pieces, mix_a_got = together(pieces, *mix_a.step_core())
    pieces, f0, f1 = together(pieces, *mix_a.add_far([mix_a_got]))
    moved = mix_a.step_z((f0, f1))
    got = exchange(pieces)
    got, block_own, m0, m1 = together(got, block_own, *moved)
    unused, own, gain_a = chunk_norm_back(
        got, residual_a, norm_gains[0, 0], middle_grad, block_own
    )
    got = exchange(own)
    moved = mix_a.step_z_again(mix_a.add_mid([m0, m1]))
    small = pack_smalls(
        (gain_a, gain_b, gain_c, gain_d), (taps_a, taps_c), (heads_a, heads_c), sizes.n_tensor
    )
    last = mix_a.add_last(moved)
    got, small, ffn_a, mix_a.mid, y_c, *last = together(
        got, small, ffn_a, mix_a.mid, *mix_c_moved, *last
    )
    moved = mix_a.step_y(last)
    small_got = exchange(small)
    (last,) = moved
    zx_grad, query_grad, mamba_out_grad, attn_out_grad, pieces = finish_mixers(
        (mix_a.terms(last), mix_c.terms(y_c)), sizes, sizes.cuts[1]
    )
    small_got, pieces = together(small_got, pieces)
    shared_got = exchange(pieces)
    small = join_smalls(small_got, sizes)
    others = [ring.swap(small, mask) for mask in (2, 4, 6)]
    unused, small, ffn_a, ffn_c, got, *others = together(
        pieces, small, ffn_a, ffn_c, got, *others
    )
    gate_up_grad, down_grad = finish_feed_forward(ffn_a, ffn_c, gate_up_width)
    input_grad, block_output = full(got[:, :chunk]).astype(F32), full(got[:, chunk:]).astype(F32)
    small = paired_sum(small, *others)
    others = [ring.swap(small, mask) for mask in (1, 8, 9)]
    shared_got, *others = together(shared_got, *others)
    small = paired_sum(small, *others)
    keyval_grad, bc_grad, step_grad = finish_shared(shared_got, sizes)
    keyval_grad = keyval_grad.reshape(LAYERS, -1, 2, KV * HD)
    zx_grad = zx_grad.reshape(LAYERS, rows_own, 2, sizes.inner)
    gate_up_grad = gate_up_grad.reshape(LAYERS, rows_own, 2, sizes.ff)
    gains = small[8:12, :D].reshape(LAYERS, 2, D)
    taps = small[:8].reshape(LAYERS, CONV, -1).transpose(0, 2, 1)
    heads = small[12, : 6 * 128].reshape(LAYERS, 3, 128)[:, :, :NH]
    small_out = (gains, taps, heads[:, 0], heads[:, 1], heads[:, 2])
    return (
        block_output,
        input_grad,
        *small_out,
        zx_grad,
        bc_grad,
        step_grad,
        query_grad,
        keyval_grad,
        mamba_out_grad,
        attn_out_grad,
        gate_up_grad,
        down_grad,
    )


def solution(mesh):
    placed = (
        P("dp", None),
        P("dp", None),
        P(),
        P(),
        P(),
        P(),
        P(),
        P(None, "dp", None, "tensor"),
        P(None, "dp", None),
        P(None, "dp", None),
        P(None, "dp", "tensor"),
        P(None, "dp", None, None),
        P(None, "dp", "tensor"),
        P(None, "dp", "tensor"),
        P(None, "dp", None, "tensor"),
        P(None, "dp", "tensor"),
        P("dp", None),
    )
    return jax.shard_map(
        body,
        mesh=mesh,
        in_specs=placed,
        out_specs=(
            P("dp", None),
            P("dp", None),
            P(),
            P(),
            P(),
            P(),
            P(),
            P(None, "dp", None, "tensor"),
            P(None, ("dp", "tensor"), None),
            P(None, ("dp", "tensor"), None),
            P(None, "dp", "tensor"),
            P(None, ("dp", "tensor"), None, None),
            P(None, "dp", "tensor"),
            P(None, "dp", "tensor"),
            P(None, "dp", None, "tensor"),
            P(None, "dp", "tensor"),
        ),
        check_vma=False,
    )
```
